32 devices in a mesh: tok: 4 (over y, core), head: 8 (over z, x).
Axes of the slice: x: 2, y: 2, z: 4, core: 2. Of those that a mesh axis runs over, the one named last changes fastest.
Arguments:
- hidden_states: bfloat16 [2560, 6144], P('tok', 'head'), may hold values from -6 to 6
- norm_gain: float32 [6144], replicated, may hold values from 0.5 to 1.5
- norm_bias: float32 [6144], replicated, may hold values from -2 to 2
- qkv_weight: bfloat16 [6144, 18432], P('tok', 'head'), may hold values from -0.125 to 0.125
- qkv_bias: bfloat16 [18432], P('head'), may hold values from -2 to 2
- dense_weight: bfloat16 [6144, 6144], P('head'), may hold values from -0.21875 to 0.21875
- dense_bias: bfloat16 [6144], P('head'), may hold values from -2 to 2
- prefix_keys: bfloat16 [8, 2048, 6144], P('tok', None, 'head'), may hold values from -70 to 70
- prefix_values: bfloat16 [8, 2048, 6144], P('tok', None, 'head'), may hold values from -10 to 10
- suffix_len: int32 [4, 8], P('tok'), may hold values from 1 to 240, as said below
- request_order: int32 [4, 8], P('tok'), may hold values from 0 to 7, each once within a row
- group_slot: int32 [8], replicated, may hold values from 0 to 7, each once
Outputs:
- layer_out: bfloat16 [2560, 6144], P('tok', 'head')
The draws below stay inside these ranges and needn't reach their ends.
Inputs may be any that keep to these rules, and one draw needn't show every extreme that they name: `suffix_len`: each row sums to 640; one group, the same in every row, has exactly 240 in every row. `request_order`: each row names every group once. `group_slot`: each slot holds one group.
All inputs are finite; a program needn't handle non-finite values.
Results may differ from the reference program's by a relative error of at most 0.007.
The reference program's roundings to bfloat16 on the way count: a program that leaves them out, or rounds other values in their place, can miss the bound.
Values may be sent and summed in bfloat16 or wider, within the bound.
No kernel may reach another device: no remote copies, remote signals or barrier semaphores. Data moves between devices by JAX's collectives and lax.ppermute only.
A program may use at most 192 MiB of HBM per device.

```python
import math
import jax
import jax.numpy as jnp
from jax import lax

D = 6144
HEADS = 64
HS = 96
ROT = 24
TOK_DEV = 640
PREFIX = 2048
GROUPS = 8
CAP = 240
TOKENS = 2560
N_TOK = 4


def draw_prefix_keys(key, part):
    base_key = jax.random.fold_in(key, 0)
    full_shape = (GROUPS, PREFIX, D)
    drawn = jax.random.normal(base_key, full_shape, jnp.float32)
    return drawn.astype(jnp.bfloat16)


def draw_suffix_len(key, part):
    heaviest_key, weight_key = jax.random.split(key)
    heaviest = jax.random.randint(heaviest_key, (), 0, GROUPS)
    labels = jnp.arange(GROUPS, dtype=jnp.int32)[None, :]
    weights = jax.random.randint(weight_key, (N_TOK, GROUPS), 2, 6)
    weights = jnp.where(labels == heaviest, 0, weights)
    surplus = TOK_DEV - CAP - (GROUPS - 1)
    shares = weights * surplus // jnp.sum(weights, axis=1, keepdims=True)
    leftover = surplus - jnp.sum(shares, axis=1, keepdims=True)
    ranking = labels - (labels > heaviest).astype(jnp.int32)
    extra_one = ((ranking < leftover) & (labels != heaviest)).astype(jnp.int32)
    return jnp.where(labels == heaviest, CAP, 1 + shares + extra_one).astype(jnp.int32)


def with_spikes(values, key, source, target, blocks, factor):
    owner, partner = [(jnp.arange(values.shape[axis_at]) // (values.shape[axis_at] // blocks)).reshape([-1 if axis == axis_at else 1 for axis in range(values.ndim)]) for axis_at in (source, target)]
    chosen = jax.random.permutation(key, blocks)[partner]
    strong = (owner == chosen) | (owner == (partner + blocks // 2) % blocks)
    return jnp.where(strong, factor * values, values)


def shard_levels(rng, shape, shards, smallest, largest):
    def one(dim, blocks):
        steps = jax.random.uniform(jax.random.fold_in(jax.random.fold_in(rng, 6), dim), (blocks,), jnp.float32, smallest / len(shards), largest / len(shards))
        return jnp.repeat(jnp.exp(steps), shape[dim] // blocks).reshape((-1,) + (1,) * (len(shape) - dim - 1))

    level = one(*shards[0])
    for cut in shards[1:]:
        level = level * one(*cut)
    return level


def bell_draw(rng, extent, scale, limit, pieces=(), kind=jnp.bfloat16):
    result = jax.random.normal(rng, extent, jnp.float32) * scale
    if len(pieces) > 0:
        result = shard_levels(rng, extent, pieces, -0.22, 0.18) * result
    return jnp.clip(result, min=-limit, max=limit).astype(kind)


def noise_with(rng, shape, width, bound, shards, heavy, held_as=jnp.bfloat16):
    array = width * jax.random.normal(rng, shape, jnp.float32)
    if shards:
        array = array * shard_levels(rng, shape, shards, -0.22, 0.18)
    return jnp.clip(with_spikes(array, jax.random.fold_in(rng, 3), *heavy), -bound, bound).astype(held_as)


def setup_inputs(seed: int = 0) -> dict:
    key_list = jax.random.split(jax.random.key(seed), 13)
    return {
        "hidden_states": bell_draw(key_list[0], (TOKENS, D), 1.0, 6.0, ((0, 4), (1, 8))),
        "norm_gain": jnp.clip(1.0 + 0.1 * jax.random.normal(key_list[1], (D,), jnp.float32), 0.5, 1.5),
        "norm_bias": bell_draw(key_list[2], (D,), 0.3, 2.0, (), jnp.float32),
        "qkv_weight": bell_draw(key_list[3], (D, 3 * D), (D // 3) ** -0.5, 0.125, ((0, 4), (1, 8))),
        "qkv_bias": bell_draw(key_list[4], (3 * D,), 0.3, 2.0, ((0, 8),)),
        "dense_weight": noise_with(key_list[5], (D, D), (D // 4) ** -0.5, 0.21875, ((0, 8),), (0, 1, 8, 2.0)),
        "dense_bias": bell_draw(key_list[6], (D,), 0.3, 2.0, ((0, 8),)),
        "prefix_keys": draw_prefix_keys(jax.random.fold_in(key_list[12], 71), 0),
        "prefix_values": bell_draw(key_list[8], (GROUPS, PREFIX, D), 1.7, 10.0, ((0, 4), (2, 8))),
        "suffix_len": draw_suffix_len(jax.random.fold_in(key_list[12], 71), 0),
        "request_order": jax.vmap(lambda own: jax.random.permutation(own, GROUPS))(jax.random.split(key_list[10], N_TOK)).reshape((N_TOK, GROUPS)).astype(jnp.int32),
        "group_slot": jax.random.permutation(key_list[11], GROUPS).astype(jnp.int32),
    }


def layer_norm(values_in, gain, shift):
    widened = values_in.astype(jnp.float32)
    center = lax.optimization_barrier(jnp.mean(widened, axis=-1, keepdims=True))
    spread = lax.optimization_barrier(jnp.mean(jnp.square(widened - center), axis=-1, keepdims=True))
    return ((widened - center) * lax.rsqrt(spread + 1e-05) * gain + shift).astype(jnp.bfloat16)

def shard_layout(lengths, ordering, row_count):
    group_count = lengths.shape[0]
    labels = jnp.arange(group_count, dtype=jnp.int32)
    chosen = (ordering[:, None] == labels[None, :]).astype(jnp.int32)
    ranking = lax.optimization_barrier(jnp.sum(labels[:, None] * chosen, axis=0))
    earlier = (ranking[None, :] < ranking[:, None]).astype(jnp.int32)
    starts = lax.optimization_barrier(jnp.sum(earlier * lengths[None, :], axis=1))
    places = jnp.arange(row_count, dtype=jnp.int32)
    member = ((places[:, None] >= starts[None, :]) & (places[:, None] < (starts + lengths)[None, :])).astype(jnp.int32)
    group_of = lax.optimization_barrier(jnp.sum(member * labels[None, :], axis=1))
    within = places - lax.optimization_barrier(jnp.sum(member * starts[None, :], axis=1))
    return (starts, member, group_of, within)

def rotary(tensor, positions, rot_dims):
    half_dims = rot_dims // 2
    inverse = 10000.0 ** (-(jnp.arange(half_dims, dtype=jnp.float32) * 2.0) / rot_dims)
    angles = positions.astype(jnp.float32)[:, None] * inverse[None, :]
    cosine = jnp.cos(angles)[:, None, :]
    sine_part = jnp.sin(angles)[:, None, :]
    lower_half = tensor[..., :half_dims]
    upper_half = tensor[..., half_dims:rot_dims]
    return jnp.concatenate([lower_half * cosine - upper_half * sine_part, upper_half * cosine + lower_half * sine_part, tensor[..., rot_dims:]], axis=-1)

def suffix_part(operands):
    queries, keys_new, values_new, group_of = operands
    scaling = 1.0 / math.sqrt(HS)
    scores = jnp.einsum('ihd,jhd->hij', queries.astype(jnp.float32), keys_new.astype(jnp.float32)) * scaling
    places = jnp.arange(queries.shape[0], dtype=jnp.int32)
    allowed = (group_of[:, None] == group_of[None, :]) & (places[None, :] <= places[:, None])
    masked = jnp.where(allowed[None], scores, -jnp.inf)
    row_peak = lax.optimization_barrier(jnp.max(masked, axis=-1))
    weights = jnp.exp(masked - row_peak[..., None])
    row_mass = lax.optimization_barrier(jnp.sum(weights, axis=-1))
    blended = jnp.einsum('hij,jhd->ihd', weights.astype(jnp.bfloat16).astype(jnp.float32), values_new.astype(jnp.float32)) / jnp.transpose(row_mass)[..., None]
    return (jnp.transpose(row_peak), jnp.transpose(row_mass), blended)

def reference(hidden_states, norm_gain, norm_bias, qkv_weight, qkv_bias, dense_weight, dense_bias, prefix_keys, prefix_values, suffix_len, request_order, group_slot):
    total_rows = hidden_states.shape[0]
    normed = layer_norm(hidden_states, norm_gain, norm_bias)
    projected = jnp.dot(normed, qkv_weight, preferred_element_type=jnp.float32) + qkv_bias.astype(jnp.float32)
    projected = projected.reshape(total_rows, HEADS, 3, HS)

    def layout_rows(lengths, ordering):
        return shard_layout(lengths, ordering, TOK_DEV)
    starts, member, group_of, within = jax.vmap(layout_rows)(suffix_len, request_order)
    positions = (PREFIX + within).reshape(total_rows)
    queries = rotary(projected[:, :, 0], positions, ROT).astype(jnp.bfloat16)
    keys_new = rotary(projected[:, :, 1], positions, ROT).astype(jnp.bfloat16)
    values_new = projected[:, :, 2].astype(jnp.bfloat16)
    suf_peak, suf_mass, suf_out = lax.map(suffix_part, (queries.reshape(N_TOK, TOK_DEV, HEADS, HS), keys_new.reshape(N_TOK, TOK_DEV, HEADS, HS), values_new.reshape(N_TOK, TOK_DEV, HEADS, HS), group_of))
    suf_peak = suf_peak.reshape(total_rows, HEADS)
    suf_mass = suf_mass.reshape(total_rows, HEADS)
    suf_out = suf_out.reshape(total_rows, HEADS, HS)
    shard_ids = jnp.arange(N_TOK, dtype=jnp.int32)
    cap_index = jnp.arange(CAP, dtype=jnp.int32)
    live_slot = cap_index[None, None, :] < jnp.transpose(suffix_len)[:, :, None]
    source_rows = shard_ids[None, :, None] * TOK_DEV + jnp.transpose(starts)[:, :, None] + cap_index[None, None, :]
    source_rows = jnp.where(live_slot, source_rows, 0).astype(jnp.int32)
    gathered = jnp.where(live_slot[..., None, None], queries[source_rows], jnp.zeros((), jnp.bfloat16))
    gathered = gathered.reshape(GROUPS, N_TOK * CAP, HEADS, HS)
    scaling = 1.0 / math.sqrt(HS)

    def one_group(operands):
        group_queries, slot_id = operands
        key_heads = prefix_keys[slot_id].reshape(PREFIX, HEADS, HS).astype(jnp.float32)
        value_heads = prefix_values[slot_id].reshape(PREFIX, HEADS, HS).astype(jnp.float32)
        scores = jnp.einsum('rhd,phd->hrp', group_queries.astype(jnp.float32), key_heads) * scaling
        row_peak = lax.optimization_barrier(jnp.max(scores, axis=-1))
        weights = jnp.exp(scores - row_peak[..., None])
        row_mass = lax.optimization_barrier(jnp.sum(weights, axis=-1))
        blended = jnp.einsum('hrp,phd->rhd', weights.astype(jnp.bfloat16).astype(jnp.float32), value_heads) / jnp.transpose(row_mass)[..., None]
        return (blended, jnp.transpose(row_peak), jnp.transpose(row_mass))
    pre_all, peak_all, mass_all = lax.map(one_group, (gathered, group_slot))
    token_group = group_of.reshape(total_rows)
    token_shard = (jnp.arange(total_rows, dtype=jnp.int32) // TOK_DEV).astype(jnp.int32)
    flat_index = (token_group * (N_TOK * CAP) + token_shard * CAP + within.reshape(total_rows)).astype(jnp.int32)
    pre_out = pre_all.reshape(GROUPS * N_TOK * CAP, HEADS, HS)[flat_index]
    pre_peak = peak_all.reshape(GROUPS * N_TOK * CAP, HEADS)[flat_index]
    pre_mass = mass_all.reshape(GROUPS * N_TOK * CAP, HEADS)[flat_index]
    joint_peak = jnp.maximum(pre_peak, suf_peak)
    pre_share = pre_mass * jnp.exp(pre_peak - joint_peak)
    suf_share = suf_mass * jnp.exp(suf_peak - joint_peak)
    combined = (pre_share[..., None] * pre_out + suf_share[..., None] * suf_out) / (pre_share + suf_share)[..., None]
    attention = combined.reshape(total_rows, D).astype(jnp.bfloat16)
    dense = jnp.dot(attention, dense_weight, preferred_element_type=jnp.float32)
    return (hidden_states.astype(jnp.float32) + dense_bias.astype(jnp.float32) + dense).astype(jnp.bfloat16)
```

```python
import functools
import math

import jax
import jax.numpy as jnp
from jax import lax
from jax.experimental import pallas as pl
from jax.experimental.pallas import tpu as pltpu
from jax.sharding import PartitionSpec as P

HS = 96
GROUP_HEADS = 4
GW = GROUP_HEADS * HS
PACK = 128
F32 = jnp.float32
BF16 = jnp.bfloat16
VMEM_LIMIT = 56 * 1024 * 1024
SCALE = 1.0 / math.sqrt(HS)
LOG2E = math.log2(math.e)


def windows():
    found = []
    for k in range(GROUP_HEADS):
        first = k * HS // 128 * 128
        last = -(-(k * HS + HS) // 128) * 128
        found.append((first, last - first))
    return found


def head_mask(k, first, shape):
    lane = lax.broadcasted_iota(jnp.int32, shape, 1) + first
    return (lane >= k * HS) & (lane < (k + 1) * HS)


def params():
    return pltpu.CompilerParams(vmem_limit_bytes=VMEM_LIMIT)


def layer_norm(values_in, gain, shift):
    widened = values_in.astype(F32)
    center = jnp.mean(widened, axis=-1, keepdims=True)
    spread = jnp.mean(jnp.square(widened - center), axis=-1, keepdims=True)
    return ((widened - center) * lax.rsqrt(spread + 1e-05) * gain + shift).astype(BF16)


def shard_layout(lengths, ordering, row_count):
    group_count = lengths.shape[0]
    labels = jnp.arange(group_count, dtype=jnp.int32)
    chosen = (ordering[:, None] == labels[None, :]).astype(jnp.int32)
    ranking = jnp.sum(labels[:, None] * chosen, axis=0)
    earlier = (ranking[None, :] < ranking[:, None]).astype(jnp.int32)
    starts = jnp.sum(earlier * lengths[None, :], axis=1)
    places = jnp.arange(row_count, dtype=jnp.int32)
    member = (
        (places[:, None] >= starts[None, :]) & (places[:, None] < (starts + lengths)[None, :])
    ).astype(jnp.int32)
    row_start = jnp.sum(member * starts[None, :], axis=1)
    return starts, row_start, places - row_start


def rotary_tables(positions):
    rot = HS // 4
    half = rot // 2
    inverse = 10000.0 ** (-(jnp.arange(half, dtype=F32) * 2.0) / rot)
    angles = positions.astype(F32)[:, None] * inverse[None, :]
    cosine, sine = jnp.cos(angles), jnp.sin(angles)
    rows = positions.shape[0]
    rest = jnp.zeros((rows, HS - rot), F32)
    none = jnp.zeros((rows, half), F32)
    straight = jnp.concatenate([cosine, cosine, rest + 1.0], axis=1)
    upper = jnp.concatenate([-sine, none, rest], axis=1)
    lower = jnp.concatenate([none, sine, rest], axis=1)
    return [jnp.tile(table, (1, GROUP_HEADS)) for table in (straight, upper, lower)]


def qkv_kernel(pieces, order, normed, *refs):
    weights = refs[:pieces]
    bias, straight, upper, lower, q_out, k_out, v_out, total = refs[pieces:]
    step = pl.program_id(0)
    depth = weights[0].shape[0]
    summed = None
    for j in range(pieces):
        columns = pl.ds(pl.multiple_of(order[j] * depth, 128), depth)
        part = jnp.dot(normed[:, columns], weights[j][...], preferred_element_type=F32)
        summed = part if summed is None else summed + part
    total[step] = summed + bias[...]

    @pl.when(step == 2)
    def _():
        tile = 64

        def body(i, carry):
            rows = pl.ds(pl.multiple_of(i * tile, tile), tile)
            wide = jnp.concatenate([total[n, rows, :] for n in range(3)], axis=1)

            def part(c):
                result = None
                for k in range(GROUP_HEADS):
                    first = 192 * k + HS * c
                    cut = wide[:, first : first + GW]
                    if result is None:
                        result = cut
                    else:
                        result = jnp.where(head_mask(k, 0, cut.shape), cut, result)
                return result

            def turn(x):
                return (
                    x * straight[rows, :]
                    + pltpu.roll(x, GW - HS // 8, 1) * upper[rows, :]
                    + pltpu.roll(x, HS // 8, 1) * lower[rows, :]
                )

            q_out[rows, :] = turn(part(0)).astype(BF16)
            k_out[rows, :] = turn(part(1)).astype(BF16)
            v_out[rows, :] = part(2).astype(BF16)
            return carry

        lax.fori_loop(0, total.shape[1] // tile, body, 0)


def project(normed, weights, order, bias, tables):
    rows, features = normed.shape
    pieces = len(weights)
    depth, columns = weights[0].shape
    out = jax.ShapeDtypeStruct((rows, GW), BF16)
    whole = lambda n, order: (0, 0)
    tile = lambda n, order: (0, n)
    return pl.pallas_call(
        functools.partial(qkv_kernel, pieces),
        out_shape=(out, out, out),
        grid_spec=pltpu.PrefetchScalarGridSpec(
            num_scalar_prefetch=1,
            grid=(columns // GW,),
            in_specs=[pl.BlockSpec((rows, features), whole)]
            + [pl.BlockSpec((depth, GW), tile)] * pieces
            + [pl.BlockSpec((1, GW), tile)]
            + [pl.BlockSpec((rows, GW), whole)] * 3,
            out_specs=[pl.BlockSpec((rows, GW), whole)] * 3,
            scratch_shapes=[pltpu.VMEM((columns // GW, rows, GW), F32)],
        ),
        compiler_params=params(),
        cost_estimate=pl.CostEstimate(
            flops=2 * rows * features * columns,
            bytes_accessed=2 * features * (rows + columns) + 9 * rows * GW * 2,
            transcendentals=0,
        ),
        name="project",
    )(order, normed, *weights, bias, *tables)


def prefix_kernel(blocks, starts, lengths, *refs):
    queries = refs[:blocks]
    k_own, k_other, v_own, v_other = refs[blocks : blocks + 4]
    outs = refs[blocks + 4 : 2 * blocks + 4]
    totals = refs[2 * blocks + 4]
    slot = pl.program_id(0)
    slots = pl.num_programs(0)
    rows = queries[0].shape[0]
    length = k_own.shape[1]

    @pl.when(slot == 0)
    def _():
        totals[...] = jnp.zeros_like(totals)

    begin, size, offset = [], [], []
    count = 0
    for b in range(blocks):
        begin.append(starts[slot * blocks + b])
        size.append(lengths[slot * blocks + b])
        offset.append(count)
        count = count + size[b]

    def serve(keys, values):
        def tile(base, height):
            down = lax.broadcasted_iota(jnp.int32, (height, 1), 0) + base
            across = lax.broadcasted_iota(jnp.int32, (1, height), 1) + base

            def sources(place, b):
                within = place - offset[b]
                return jnp.where((within >= 0) & (within < size[b]), within + begin[b], -1)

            picked = None
            for b in range(blocks):
                spread = lax.broadcasted_iota(jnp.int32, (height, rows), 1)
                one_hot = jnp.where(spread == sources(down, b), 1.0, 0.0).astype(BF16)
                part = jnp.dot(one_hot, queries[b][...], preferred_element_type=F32)
                picked = part if picked is None else picked + part
            picked = picked.astype(BF16)
            merged = [jnp.zeros((height, 128), F32) for _ in range(GW // 128)]
            extra = jnp.zeros((height, PACK), F32)
            place = lax.broadcasted_iota(jnp.int32, (height, PACK), 1)
            for k, (first, width) in enumerate(windows()):
                lanes = slice(first, first + width)
                mask = head_mask(k, first, (height, width))
                query = jnp.where(mask, picked[:, lanes], jnp.zeros((), BF16))
                scores = lax.dot_general(
                    query,
                    keys[0, :, lanes],
                    (((1,), (1,)), ((), ())),
                    preferred_element_type=F32,
                )
                peak = jnp.max(scores, axis=1, keepdims=True)
                weights = jnp.exp2((scores - peak) * (SCALE * LOG2E))
                mass = jnp.sum(weights, axis=1, keepdims=True)
                blended = jnp.dot(
                    weights.astype(BF16), values[0, :, lanes], preferred_element_type=F32
                )
                blended = blended * (1.0 / mass)
                for w in range(width // 128):
                    at = first // 128 + w
                    cut = slice(w * 128, w * 128 + 128)
                    merged[at] = jnp.where(mask[:, cut], blended[:, cut], merged[at])
                level = peak * SCALE + jnp.log(mass)
                high = level.astype(BF16).astype(F32)
                middle = (level - high).astype(BF16).astype(F32)
                low = level - high - middle
                for n, term in enumerate((high, middle, low)):
                    extra = jnp.where(place == 3 * k + n, term, extra)
            packed = jnp.concatenate(merged + [extra], axis=1).astype(BF16)
            for b in range(blocks):
                spread = lax.broadcasted_iota(jnp.int32, (rows, height), 0)
                one_hot = jnp.where(spread == sources(across, b), 1.0, 0.0).astype(BF16)
                totals[b] += jnp.dot(one_hot, packed, preferred_element_type=F32)

        large = 256
        small = 128
        full = lax.div(count, large)
        rest = count - full * large

        def body(j, carry):
            tile(j * large, large)
            return carry

        lax.fori_loop(0, full + jnp.where(rest > small, 1, 0), body, 0)

        @pl.when((rest > 0) & (rest <= small))
        def _():
            tile(full * large, small)

    half = slots // 2

    @pl.when(slot < half)
    def _():
        serve(k_own, v_own)

    @pl.when(slot >= half)
    def _():
        serve(k_other, v_other)

    @pl.when(slot == slots - 1)
    def _():
        for b in range(blocks):
            outs[b][...] = totals[b].astype(BF16)


def prefix_attention(group, queries, cache, starts, lengths):
    blocks = len(queries)
    rows = queries[0].shape[0]
    held, length, _ = cache[0].shape
    width = GW + PACK
    whole = lambda s, starts, lengths: (0, 0)
    own = lambda s, starts, lengths: (jnp.minimum(s, held - 1), 0, group)
    other = lambda s, starts, lengths: (jnp.maximum(s - held, 0), 0, group)
    block = (1, length, GW)
    return pl.pallas_call(
        functools.partial(prefix_kernel, blocks),
        out_shape=[jax.ShapeDtypeStruct((rows, width), BF16)] * blocks,
        grid_spec=pltpu.PrefetchScalarGridSpec(
            num_scalar_prefetch=2,
            grid=(2 * held,),
            in_specs=[pl.BlockSpec((rows, GW), whole)] * blocks
            + [
                pl.BlockSpec(block, own),
                pl.BlockSpec(block, other),
                pl.BlockSpec(block, own),
                pl.BlockSpec(block, other),
            ],
            out_specs=[pl.BlockSpec((rows, width), whole)] * blocks,
            scratch_shapes=[pltpu.VMEM((blocks, rows, width), F32)],
        ),
        compiler_params=params(),
        cost_estimate=pl.CostEstimate(
            flops=4 * rows * length * GROUP_HEADS * 256,
            bytes_accessed=2 * 2 * held * length * GW * 2,
            transcendentals=rows * length * GROUP_HEADS,
        ),
        name="prefix",
    )(starts, lengths, *queries, cache[0], cache[1], cache[2], cache[3])


def suffix_kernel(row_start, queries, keys, values, out, levels):
    rows = queries.shape[0]
    tile = 128
    for i in range(rows // tile):
        at = slice(i * tile, (i + 1) * tile)
        wide = (i + 1) * tile
        row = lax.broadcasted_iota(jnp.int32, (tile, wide), 0) + i * tile
        column = lax.broadcasted_iota(jnp.int32, (tile, wide), 1)
        allowed = (column <= row) & (column >= row_start[at, :])
        merged = [jnp.zeros((tile, 128), F32) for _ in range(GW // 128)]
        level_row = jnp.zeros((tile, PACK), F32)
        place = lax.broadcasted_iota(jnp.int32, (tile, PACK), 1)
        for k, (first, width) in enumerate(windows()):
            lanes = slice(first, first + width)
            mask = head_mask(k, first, (tile, width))
            query = jnp.where(mask, queries[at, lanes], jnp.zeros((), BF16))
            scores = lax.dot_general(
                query,
                keys[:wide, lanes],
                (((1,), (1,)), ((), ())),
                preferred_element_type=F32,
            )
            scores = jnp.where(allowed, scores, -jnp.inf)
            peak = jnp.max(scores, axis=1, keepdims=True)
            weights = jnp.exp2((scores - peak) * (SCALE * LOG2E))
            mass = jnp.sum(weights, axis=1, keepdims=True)
            blended = jnp.dot(
                weights.astype(BF16), values[:wide, lanes], preferred_element_type=F32
            )
            blended = blended * (1.0 / mass)
            for w in range(width // 128):
                spot = first // 128 + w
                cut = slice(w * 128, w * 128 + 128)
                merged[spot] = jnp.where(mask[:, cut], blended[:, cut], merged[spot])
            level_row = jnp.where(place == k, peak * SCALE + jnp.log(mass), level_row)
        out[at, :] = jnp.concatenate(merged, axis=1)
        levels[at, :] = level_row


def suffix_attention(row_start, queries, keys, values):
    rows = queries.shape[0]
    return pl.pallas_call(
        suffix_kernel,
        out_shape=(
            jax.ShapeDtypeStruct((rows, GW), F32),
            jax.ShapeDtypeStruct((rows, PACK), F32),
        ),
        compiler_params=params(),
        cost_estimate=pl.CostEstimate(
            flops=4 * rows * rows * GROUP_HEADS * 256,
            bytes_accessed=rows * GW * 10,
            transcendentals=rows * rows * GROUP_HEADS,
        ),
        name="suffix",
    )(row_start, queries, keys, values)


def merge_kernel(blocks, *refs):
    parts = refs[:blocks]
    suffix, levels, out = refs[blocks:]
    rows = suffix.shape[0]
    tile = 128
    for i in range(rows // tile):
        at = slice(i * tile, (i + 1) * tile)
        prefix = parts[0][at, :].astype(F32)
        for b in range(1, blocks):
            prefix = prefix + parts[b][at, :].astype(F32)
        share_pre = jnp.zeros((tile, GW), F32)
        share_suf = jnp.zeros((tile, GW), F32)
        for k in range(GROUP_HEADS):
            lane = GW + 3 * k
            pre = (
                prefix[:, lane : lane + 1]
                + prefix[:, lane + 1 : lane + 2]
                + prefix[:, lane + 2 : lane + 3]
            )
            suf = levels[at, k : k + 1]
            top = jnp.maximum(pre, suf)
            pre = jnp.exp(pre - top)
            suf = jnp.exp(suf - top)
            whole = 1.0 / (pre + suf)
            mask = head_mask(k, 0, (tile, GW))
            share_pre = jnp.where(mask, pre * whole, share_pre)
            share_suf = jnp.where(mask, suf * whole, share_suf)
        out[at, :] = (share_pre * prefix[:, :GW] + share_suf * suffix[at, :]).astype(BF16)


def merge(parts, suffix, levels):
    rows = suffix.shape[0]
    return pl.pallas_call(
        functools.partial(merge_kernel, len(parts)),
        out_shape=jax.ShapeDtypeStruct((rows, GW), BF16),
        compiler_params=params(),
        cost_estimate=pl.CostEstimate(
            flops=rows * GW * 8, bytes_accessed=rows * GW * 10, transcendentals=rows * 8
        ),
        name="merge",
    )(*parts, suffix, levels)


def on_device(
    hidden_states,
    norm_gain,
    norm_bias,
    qkv_weight,
    qkv_bias,
    dense_weight,
    dense_bias,
    prefix_keys,
    prefix_values,
    suffix_len,
    request_order,
    group_slot,
):
    rows, share = hidden_states.shape
    held, prefix_length, local_width = prefix_keys.shape
    groups_local = local_width // GW
    tok_size = lax.axis_size("tok")
    head_size = lax.axis_size("head")
    chips = tok_size // 2
    lines = head_size // 2
    group_count = held * tok_size
    tok = lax.axis_index("tok")
    head = lax.axis_index("head")
    core, chip = tok % 2, tok // 2
    side, line = head % 2, head // 2

    def to_core(x):
        return lax.ppermute(x, "tok", [(t, t ^ 1) for t in range(tok_size)])

    def to_chip(x, shift):
        return lax.ppermute(
            x,
            "tok",
            [(t, (t // 2 + shift) % chips * 2 + t % 2) for t in range(tok_size)],
        )

    def to_side(x):
        return lax.ppermute(x, "head", [(h, h ^ 1) for h in range(head_size)])

    columns = 3 * GW
    order = [tok, tok ^ 1]
    for shift in range(1, chips):
        source = (chip + chips - shift) % chips * 2 + core
        order += [source, source ^ 1]
    order = jnp.stack(order).astype(jnp.int32)
    gathered = []
    for g in range(groups_local):
        mine = qkv_weight[:, g * columns : (g + 1) * columns]
        pieces = [mine, to_core(mine)]
        for shift in range(1, chips):
            arrived = to_chip(mine, shift)
            pieces += [arrived, to_core(arrived)]
        gathered.append(pieces)
    full_rows = lax.all_gather(hidden_states, "head", axis=1, tiled=True)
    cache = [prefix_keys, to_core(prefix_keys), prefix_values, to_core(prefix_values)]

    lengths = suffix_len[0]
    starts, row_start, within = shard_layout(lengths, request_order[0], rows)
    labels = jnp.arange(group_count, dtype=jnp.int32)
    slot_match = (group_slot[:, None] == labels[None, :]).astype(jnp.int32)
    spans = jnp.stack(
        [
            jnp.sum(starts[:, None] * slot_match, axis=0),
            jnp.sum(lengths[:, None] * slot_match, axis=0),
        ]
    )
    all_spans = [spans] + [to_chip(spans, shift) for shift in range(1, chips)]
    served = jnp.stack(
        [
            jnp.concatenate(
                [
                    lax.dynamic_slice(one, (0, tok * held), (2, held)),
                    lax.dynamic_slice(one, (0, (tok ^ 1) * held), (2, held)),
                ],
                axis=1,
            )
            for one in all_spans
        ],
        axis=2,
    )
    span_start = served[0].reshape(-1)
    span_length = served[1].reshape(-1)
    tables = rotary_tables(prefix_length + within)
    bias = qkv_bias.astype(F32)[None, :]

    def side_columns(which):
        return [
            lax.dynamic_slice(
                dense_weight, (0, (2 * a + which) * share), (dense_weight.shape[0], share)
            )
            for a in range(lines)
        ]

    half = lines // 2
    outgoing = lax.dynamic_slice(
        jnp.concatenate(side_columns(1 - side), axis=1),
        (0, core * half * share),
        (dense_weight.shape[0], half * share),
    )
    landed = to_side(outgoing)
    crossed = to_core(landed)
    received = jnp.where(
        core == 0,
        jnp.concatenate([landed, crossed], axis=1),
        jnp.concatenate([crossed, landed], axis=1),
    )
    dense_both = jnp.concatenate(
        [jnp.concatenate(side_columns(side), axis=1), received], axis=0
    )

    normed = layer_norm(full_rows, norm_gain, norm_bias)
    attention_own, attention_side = [], []
    for g in range(groups_local):
        queries, keys, values = project(
            normed, gathered[g], order, bias[:, g * columns : (g + 1) * columns], tables
        )
        asked = [queries] + [to_chip(queries, shift) for shift in range(1, chips)]
        answers = prefix_attention(g, asked, cache, span_start, span_length)
        parts = [answers[0]] + [to_chip(answers[s], chips - s) for s in range(1, chips)]
        suffix, levels = suffix_attention(row_start[:, None], queries, keys, values)
        attention = merge(parts, suffix, levels)
        attention_own.append(attention)
        attention_side.append(to_side(attention))
    attention = jnp.concatenate(attention_own + attention_side, axis=1)
    partial = jnp.dot(attention, dense_both, preferred_element_type=F32)

    def chunk(place):
        place = jnp.clip(place, 0, lines - 1)
        return lax.dynamic_slice(partial, (0, place * share), (rows, share))

    upward = downward = None
    last = lines - 1
    for step in range(last):
        up = chunk(last + line - step)
        down = chunk(line - last + step)
        if upward is not None:
            up = up + upward.astype(F32)
            down = down + downward.astype(F32)
        up_pairs = [(h, h + 2) for h in range(head_size) if h // 2 <= step and h // 2 < last]
        down_pairs = [(h, h - 2) for h in range(head_size) if last - h // 2 <= step and h // 2 > 0]
        upward = lax.ppermute(up.astype(BF16), "head", up_pairs)
        downward = lax.ppermute(down.astype(BF16), "head", down_pairs)
    summed = chunk(line) + upward.astype(F32) + downward.astype(F32)
    return (hidden_states.astype(F32) + dense_bias.astype(F32) + summed).astype(BF16)


def solution(mesh):
    placed = (
        P("tok", "head"),
        P(),
        P(),
        P("tok", "head"),
        P("head"),
        P("head", None),
        P("head"),
        P("tok", None, "head"),
        P("tok", None, "head"),
        P("tok", None),
        P("tok", None),
        P(),
    )
    return jax.shard_map(
        on_device, mesh=mesh, in_specs=placed, out_specs=P("tok", "head"), check_vma=False
    )
```

```python
import functools
import math

import jax
import jax.numpy as jnp
from jax import lax
from jax.experimental import pallas as pl
from jax.experimental.pallas import tpu as pltpu
from jax.sharding import PartitionSpec as P

HS = 96
GROUP_HEADS = 4
GW = GROUP_HEADS * HS
PACK = 128
F32 = jnp.float32
BF16 = jnp.bfloat16
VMEM_LIMIT = 56 * 1024 * 1024
SCALE = 1.0 / math.sqrt(HS)
LOG2E = math.log2(math.e)


def windows():
    found = []
    for k in range(GROUP_HEADS):
        first = k * HS // 128 * 128
        last = -(-(k * HS + HS) // 128) * 128
        found.append((first, last - first))
    return found


def head_mask(k, first, shape):
    lane = lax.broadcasted_iota(jnp.int32, shape, 1) + first
    return (lane >= k * HS) & (lane < (k + 1) * HS)


def params():
    return pltpu.CompilerParams(vmem_limit_bytes=VMEM_LIMIT)


def norm_kernel(values, gain, shift, out):
    widened = values[...].astype(F32)
    center = jnp.mean(widened, axis=-1, keepdims=True)
    moved = widened - center
    spread = jnp.mean(jnp.square(moved), axis=-1, keepdims=True)
    out[...] = (moved * lax.rsqrt(spread + 1e-05) * gain[...] + shift[...]).astype(BF16)


def layer_norm(values, gain, shift):
    rows, features = values.shape
    tile = 64
    return pl.pallas_call(
        norm_kernel,
        out_shape=jax.ShapeDtypeStruct((rows, features), BF16),
        grid=(rows // tile,),
        in_specs=[
            pl.BlockSpec((tile, features), lambda i: (i, 0)),
            pl.BlockSpec((1, features), lambda i: (0, 0)),
            pl.BlockSpec((1, features), lambda i: (0, 0)),
        ],
        out_specs=pl.BlockSpec((tile, features), lambda i: (i, 0)),
        compiler_params=params(),
        cost_estimate=pl.CostEstimate(
            flops=rows * features * 8, bytes_accessed=rows * features * 4, transcendentals=rows
        ),
        name="norm",
    )(values, gain[None, :], shift[None, :])


def shard_layout(lengths, ordering, row_count):
    group_count = lengths.shape[0]
    labels = jnp.arange(group_count, dtype=jnp.int32)
    chosen = (ordering[:, None] == labels[None, :]).astype(jnp.int32)
    ranking = jnp.sum(labels[:, None] * chosen, axis=0)
    earlier = (ranking[None, :] < ranking[:, None]).astype(jnp.int32)
    starts = jnp.sum(earlier * lengths[None, :], axis=1)
    places = jnp.arange(row_count, dtype=jnp.int32)
    member = (
        (places[:, None] >= starts[None, :]) & (places[:, None] < (starts + lengths)[None, :])
    ).astype(jnp.int32)
    row_start = jnp.sum(member * starts[None, :], axis=1)
    return starts, row_start, places - row_start


def rotary_tables(positions):
    rot = HS // 4
    half = rot // 2
    inverse = 10000.0 ** (-(jnp.arange(half, dtype=F32) * 2.0) / rot)
    angles = positions.astype(F32)[:, None] * inverse[None, :]
    cosine, sine = jnp.cos(angles), jnp.sin(angles)
    rows = positions.shape[0]
    rest = jnp.zeros((rows, HS - rot), F32)
    none = jnp.zeros((rows, half), F32)
    straight = jnp.concatenate([cosine, cosine, rest + 1.0], axis=1)
    upper = jnp.concatenate([-sine, none, rest], axis=1)
    lower = jnp.concatenate([none, sine, rest], axis=1)
    return [jnp.tile(table, (1, GROUP_HEADS)) for table in (straight, upper, lower)]


def qkv_kernel(pieces, order, normed, *refs):
    weights = refs[:pieces]
    bias, straight, upper, lower, q_out, k_out, v_out = refs[pieces : pieces + 7]
    total, held_rows, held_weights, row_sems, weight_sems = refs[pieces + 7 :]
    depth, columns = weights[0].shape

    def row_copy(j):
        lanes = pl.ds(pl.multiple_of(order[j] * depth, 128), depth)
        return pltpu.make_async_copy(normed.at[:, lanes], held_rows.at[j], row_sems.at[j])

    def weight_copy(j):
        return pltpu.make_async_copy(weights[j], held_weights.at[j], weight_sems.at[j])

    for j in range(pieces):
        row_copy(j).start()
        weight_copy(j).start()
    for j in range(pieces):
        row_copy(j).wait()
        weight_copy(j).wait()
        for first in range(0, columns, 256):
            lanes = slice(first, min(first + 256, columns))
            part = jnp.dot(
                held_rows[j], held_weights[j, :, lanes], preferred_element_type=F32
            )
            if j == 0:
                total[:, lanes] = part + bias[:, lanes]
            else:
                total[:, lanes] += part

    tile = 64

    def body(i, carry):
        rows = pl.ds(pl.multiple_of(i * tile, tile), tile)
        wide = total[rows, :]

        def part(c):
            merged = [None] * (GW // 128)
            for k, (first, width) in enumerate(windows()):
                source = 192 * k + HS * c + first
                cut = wide[:, source : source + width]
                mask = head_mask(k, first, cut.shape)
                for w in range(width // 128):
                    at = first // 128 + w
                    lanes = slice(w * 128, w * 128 + 128)
                    if merged[at] is None:
                        merged[at] = cut[:, lanes]
                    else:
                        merged[at] = jnp.where(mask[:, lanes], cut[:, lanes], merged[at])
            return jnp.concatenate(merged, axis=1)

        def turn(x):
            return (
                x * straight[rows, :]
                + pltpu.roll(x, GW - HS // 8, 1) * upper[rows, :]
                + pltpu.roll(x, HS // 8, 1) * lower[rows, :]
            )

        q_out[rows, :] = turn(part(0)).astype(BF16)
        k_out[rows, :] = turn(part(1)).astype(BF16)
        v_out[rows, :] = part(2).astype(BF16)
        return carry

    lax.fori_loop(0, total.shape[0] // tile, body, 0)


def project(normed, weights, order, bias, tables):
    rows, features = normed.shape
    pieces = len(weights)
    depth, columns = weights[0].shape
    out = jax.ShapeDtypeStruct((rows, GW), BF16)
    vmem = pl.BlockSpec(memory_space=pltpu.VMEM)
    anywhere = pl.BlockSpec(memory_space=pl.ANY)
    return pl.pallas_call(
        functools.partial(qkv_kernel, pieces),
        out_shape=(out, out, out),
        in_specs=[pl.BlockSpec(memory_space=pltpu.SMEM)]
        + [anywhere] * (pieces + 1)
        + [vmem] * 4,
        out_specs=[vmem] * 3,
        scratch_shapes=[
            pltpu.VMEM((rows, columns), F32),
            pltpu.VMEM((pieces, rows, depth), BF16),
            pltpu.VMEM((pieces, depth, columns), BF16),
            pltpu.SemaphoreType.DMA((pieces,)),
            pltpu.SemaphoreType.DMA((pieces,)),
        ],
        compiler_params=params(),
        cost_estimate=pl.CostEstimate(
            flops=2 * rows * features * columns,
            bytes_accessed=2 * features * (rows + columns) + 9 * rows * GW * 2,
            transcendentals=0,
        ),
        name="project",
    )(order, normed, *weights, bias, *tables)


def prefix_kernel(blocks, starts, lengths, *refs):
    queries = refs[:blocks]
    k_own, k_other, v_own, v_other = refs[blocks : blocks + 4]
    outs = refs[blocks + 4 : 2 * blocks + 4]
    totals = refs[2 * blocks + 4]
    slot = pl.program_id(0)
    slots = pl.num_programs(0)
    rows = queries[0].shape[0]
    length = k_own.shape[1]

    @pl.when(slot == 0)
    def _():
        totals[...] = jnp.zeros_like(totals)

    begin, size, offset = [], [], []
    count = 0
    for b in range(blocks):
        begin.append(starts[slot * blocks + b])
        size.append(lengths[slot * blocks + b])
        offset.append(count)
        count = count + size[b]

    def serve(keys, values):
        def tile(base, height):
            down = lax.broadcasted_iota(jnp.int32, (height, 1), 0) + base
            across = lax.broadcasted_iota(jnp.int32, (1, height), 1) + base

            def sources(place, b):
                within = place - offset[b]
                return jnp.where((within >= 0) & (within < size[b]), within + begin[b], -1)

            picked = None
            for b in range(blocks):
                spread = lax.broadcasted_iota(jnp.int32, (height, rows), 1)
                one_hot = jnp.where(spread == sources(down, b), 1.0, 0.0).astype(BF16)
                part = jnp.dot(one_hot, queries[b][...], preferred_element_type=F32)
                picked = part if picked is None else picked + part
            picked = picked.astype(BF16)
            merged = [jnp.zeros((height, 128), F32) for _ in range(GW // 128)]
            extra = jnp.zeros((height, PACK), F32)
            place = lax.broadcasted_iota(jnp.int32, (height, PACK), 1)
            for k, (first, width) in enumerate(windows()):
                lanes = slice(first, first + width)
                mask = head_mask(k, first, (height, width))
                query = jnp.where(mask, picked[:, lanes], jnp.zeros((), BF16))
                scores = lax.dot_general(
                    query,
                    keys[0, :, lanes],
                    (((1,), (1,)), ((), ())),
                    preferred_element_type=F32,
                )
                peak = jnp.max(scores, axis=1, keepdims=True)
                weights = jnp.exp2((scores - peak) * (SCALE * LOG2E))
                mass = jnp.sum(weights, axis=1, keepdims=True)
                blended = jnp.dot(
                    weights.astype(BF16), values[0, :, lanes], preferred_element_type=F32
                )
                blended = blended * (1.0 / mass)
                for w in range(width // 128):
                    at = first // 128 + w
                    cut = slice(w * 128, w * 128 + 128)
                    merged[at] = jnp.where(mask[:, cut], blended[:, cut], merged[at])
                level = peak * SCALE + jnp.log(mass)
                high = level.astype(BF16).astype(F32)
                middle = (level - high).astype(BF16).astype(F32)
                low = level - high - middle
                for n, term in enumerate((high, middle, low)):
                    extra = jnp.where(place == 32 * n + k, term, extra)
            packed = jnp.concatenate(merged + [extra], axis=1).astype(BF16)
            for b in range(blocks):
                spread = lax.broadcasted_iota(jnp.int32, (rows, height), 0)
                one_hot = jnp.where(spread == sources(across, b), 1.0, 0.0).astype(BF16)
                totals[b] += jnp.dot(one_hot, packed, preferred_element_type=F32)

        large = 256
        small = 128
        full = lax.div(count, large)
        rest = count - full * large

        def body(j, carry):
            tile(j * large, large)
            return carry

        lax.fori_loop(0, full + jnp.where(rest > small, 1, 0), body, 0)

        @pl.when((rest > 0) & (rest <= small))
        def _():
            tile(full * large, small)

    half = slots // 2

    @pl.when(slot < half)
    def _():
        serve(k_own, v_own)

    @pl.when(slot >= half)
    def _():
        serve(k_other, v_other)

    @pl.when(slot == slots - 1)
    def _():
        for b in range(blocks):
            outs[b][...] = totals[b].astype(BF16)


def prefix_attention(group, queries, cache, starts, lengths):
    blocks = len(queries)
    rows = queries[0].shape[0]
    held, length, _ = cache[0].shape
    width = GW + PACK
    whole = lambda s, starts, lengths: (0, 0)
    own = lambda s, starts, lengths: (jnp.minimum(s, held - 1), 0, group)
    other = lambda s, starts, lengths: (jnp.maximum(s - held, 0), 0, group)
    block = (1, length, GW)
    return pl.pallas_call(
        functools.partial(prefix_kernel, blocks),
        out_shape=[jax.ShapeDtypeStruct((rows, width), BF16)] * blocks,
        grid_spec=pltpu.PrefetchScalarGridSpec(
            num_scalar_prefetch=2,
            grid=(2 * held,),
            in_specs=[pl.BlockSpec((rows, GW), whole)] * blocks
            + [
                pl.BlockSpec(block, own),
                pl.BlockSpec(block, other),
                pl.BlockSpec(block, own),
                pl.BlockSpec(block, other),
            ],
            out_specs=[pl.BlockSpec((rows, width), whole)] * blocks,
            scratch_shapes=[pltpu.VMEM((blocks, rows, width), F32)],
        ),
        compiler_params=params(),
        cost_estimate=pl.CostEstimate(
            flops=4 * rows * length * GROUP_HEADS * 256,
            bytes_accessed=2 * 2 * held * length * GW * 2,
            transcendentals=rows * length * GROUP_HEADS,
        ),
        name="prefix",
    )(starts, lengths, *queries, cache[0], cache[1], cache[2], cache[3])


def suffix_kernel(row_start, queries, keys, values, out, levels):
    rows = queries.shape[0]
    tile = 128
    for i in range(rows // tile):
        at = slice(i * tile, (i + 1) * tile)
        wide = (i + 1) * tile
        row = lax.broadcasted_iota(jnp.int32, (tile, wide), 0) + i * tile
        column = lax.broadcasted_iota(jnp.int32, (tile, wide), 1)
        allowed = (column <= row) & (column >= row_start[at, :])
        merged = [jnp.zeros((tile, 128), F32) for _ in range(GW // 128)]
        level_row = jnp.zeros((tile, PACK), F32)
        place = lax.broadcasted_iota(jnp.int32, (tile, PACK), 1)
        for k, (first, width) in enumerate(windows()):
            lanes = slice(first, first + width)
            mask = head_mask(k, first, (tile, width))
            query = jnp.where(mask, queries[at, lanes], jnp.zeros((), BF16))
            scores = lax.dot_general(
                query,
                keys[:wide, lanes],
                (((1,), (1,)), ((), ())),
                preferred_element_type=F32,
            )
            scores = jnp.where(allowed, scores, -jnp.inf)
            peak = jnp.max(scores, axis=1, keepdims=True)
            weights = jnp.exp2((scores - peak) * (SCALE * LOG2E))
            mass = jnp.sum(weights, axis=1, keepdims=True)
            blended = jnp.dot(
                weights.astype(BF16), values[:wide, lanes], preferred_element_type=F32
            )
            blended = blended * (1.0 / mass)
            for w in range(width // 128):
                spot = first // 128 + w
                cut = slice(w * 128, w * 128 + 128)
                merged[spot] = jnp.where(mask[:, cut], blended[:, cut], merged[spot])
            level_row = jnp.where(place == k, peak * SCALE + jnp.log(mass), level_row)
        out[at, :] = jnp.concatenate(merged, axis=1)
        levels[at, :] = level_row


def suffix_attention(row_start, queries, keys, values):
    rows = queries.shape[0]
    return pl.pallas_call(
        suffix_kernel,
        out_shape=(
            jax.ShapeDtypeStruct((rows, GW), F32),
            jax.ShapeDtypeStruct((rows, PACK), F32),
        ),
        compiler_params=params(),
        cost_estimate=pl.CostEstimate(
            flops=4 * rows * rows * GROUP_HEADS * 256,
            bytes_accessed=rows * GW * 10,
            transcendentals=rows * rows * GROUP_HEADS,
        ),
        name="suffix",
    )(row_start, queries, keys, values)


def merge_kernel(blocks, *refs):
    parts = refs[:blocks]
    suffix, levels, out = refs[blocks:]
    rows = suffix.shape[0]
    tile = 128
    for i in range(rows // tile):
        at = slice(i * tile, (i + 1) * tile)
        prefix = parts[0][at, :].astype(F32)
        for b in range(1, blocks):
            prefix = prefix + parts[b][at, :].astype(F32)
        terms = prefix[:, GW:]
        pre = terms + pltpu.roll(terms, PACK - 32, 1) + pltpu.roll(terms, PACK - 64, 1)
        suf = levels[at, :]
        top = jnp.maximum(pre, suf)
        pre = jnp.exp(pre - top)
        suf = jnp.exp(suf - top)
        shares = pre / (pre + suf)
        spread = jnp.zeros((tile, GW), F32)
        for k in range(GROUP_HEADS):
            spread = jnp.where(head_mask(k, 0, (tile, GW)), shares[:, k : k + 1], spread)
        out[at, :] = (spread * prefix[:, :GW] + (1.0 - spread) * suffix[at, :]).astype(BF16)


def merge(parts, suffix, levels):
    rows = suffix.shape[0]
    return pl.pallas_call(
        functools.partial(merge_kernel, len(parts)),
        out_shape=jax.ShapeDtypeStruct((rows, GW), BF16),
        compiler_params=params(),
        cost_estimate=pl.CostEstimate(
            flops=rows * GW * 8, bytes_accessed=rows * GW * 10, transcendentals=rows * 8
        ),
        name="merge",
    )(*parts, suffix, levels)


def on_device(
    hidden_states,
    norm_gain,
    norm_bias,
    qkv_weight,
    qkv_bias,
    dense_weight,
    dense_bias,
    prefix_keys,
    prefix_values,
    suffix_len,
    request_order,
    group_slot,
):
    rows, share = hidden_states.shape
    held, prefix_length, local_width = prefix_keys.shape
    groups_local = local_width // GW
    tok_size = lax.axis_size("tok")
    head_size = lax.axis_size("head")
    chips = tok_size // 2
    lines = head_size // 2
    group_count = held * tok_size
    tok = lax.axis_index("tok")
    head = lax.axis_index("head")
    core, chip = tok % 2, tok // 2
    side, line = head % 2, head // 2

    def to_core(x):
        return lax.ppermute(x, "tok", [(t, t ^ 1) for t in range(tok_size)])

    def to_chip(x, shift):
        return lax.ppermute(
            x,
            "tok",
            [(t, (t // 2 + shift) % chips * 2 + t % 2) for t in range(tok_size)],
        )

    def to_side(x):
        return lax.ppermute(x, "head", [(h, h ^ 1) for h in range(head_size)])

    layout = jnp.stack([suffix_len[0], request_order[0]])
    layouts = [layout] + [to_chip(layout, shift) for shift in range(1, chips)]
    full_rows = lax.all_gather(hidden_states, "head", axis=1, tiled=True)

    columns = 3 * GW
    order = [tok, tok ^ 1]
    for shift in range(1, chips):
        source = (chip + chips - shift) % chips * 2 + core
        order += [source, source ^ 1]
    order = jnp.stack(order).astype(jnp.int32)
    gathered = []
    earlier = layouts
    source = qkv_weight
    for g in range(groups_local):
        mine = source[:, g * columns : (g + 1) * columns]
        mine, earlier = lax.optimization_barrier((mine, earlier))
        if g == 0:
            layouts = earlier
            source, _ = lax.optimization_barrier((qkv_weight, layouts))
        arrived = [to_chip(mine, shift) for shift in range(1, chips)]
        pieces = [mine, to_core(mine)]
        for one in arrived:
            pieces += [one, to_core(one)]
        gathered.append(pieces)
        earlier = arrived
    cache = [prefix_keys, to_core(prefix_keys), prefix_values, to_core(prefix_values)]

    lengths = suffix_len[0]
    starts, row_start, within = shard_layout(lengths, request_order[0], rows)
    labels = jnp.arange(group_count, dtype=jnp.int32)
    slot_match = (group_slot[:, None] == labels[None, :]).astype(jnp.int32)

    def served_spans(one):
        firsts = shard_layout(one[0], one[1], rows)[0]
        spans = jnp.stack(
            [
                jnp.sum(firsts[:, None] * slot_match, axis=0),
                jnp.sum(one[0][:, None] * slot_match, axis=0),
            ]
        )
        return jnp.concatenate(
            [
                lax.dynamic_slice(spans, (0, tok * held), (2, held)),
                lax.dynamic_slice(spans, (0, (tok ^ 1) * held), (2, held)),
            ],
            axis=1,
        )

    served = jnp.stack([served_spans(one) for one in layouts], axis=2)
    span_start = served[0].reshape(-1)
    span_length = served[1].reshape(-1)
    tables = rotary_tables(prefix_length + within)
    bias = qkv_bias.astype(F32)[None, :]

    def side_columns(which):
        return [
            lax.dynamic_slice(
                dense_weight, (0, (2 * a + which) * share), (dense_weight.shape[0], share)
            )
            for a in range(lines)
        ]

    half = lines // 2
    outgoing = lax.dynamic_slice(
        jnp.concatenate(side_columns(1 - side), axis=1),
        (0, core * half * share),
        (dense_weight.shape[0], half * share),
    )
    outgoing, full_rows = lax.optimization_barrier((outgoing, full_rows))
    landed = to_side(outgoing)
    crossed = to_core(landed)
    received = jnp.where(
        core == 0,
        jnp.concatenate([landed, crossed], axis=1),
        jnp.concatenate([crossed, landed], axis=1),
    )
    dense_both = jnp.concatenate(
        [jnp.concatenate(side_columns(side), axis=1), received], axis=0
    )

    normed = layer_norm(full_rows, norm_gain, norm_bias)
    attention_own, attention_side = [], []
    for g in range(groups_local):
        queries, keys, values = project(
            normed, gathered[g], order, bias[:, g * columns : (g + 1) * columns], tables
        )
        asked = [queries] + [to_chip(queries, shift) for shift in range(1, chips)]
        answers = prefix_attention(g, asked, cache, span_start, span_length)
        parts = [answers[0]] + [to_chip(answers[s], chips - s) for s in range(1, chips)]
        suffix, levels = suffix_attention(row_start[:, None], queries, keys, values)
        if g == groups_local - 1:
            levels, dense_both = lax.optimization_barrier((levels, dense_both))
        attention = merge(parts, suffix, levels)
        attention_own.append(attention)
        attention_side.append(to_side(attention))
    attention = jnp.concatenate(attention_own + attention_side, axis=1)
    partial = jnp.dot(attention, dense_both, preferred_element_type=F32)

    last = lines - 1
    cuts = 2
    height = rows // cuts

    def chunk(place, cut):
        place = jnp.clip(place, 0, last)
        return lax.dynamic_slice(partial, (cut * height, place * share), (height, share))

    passing = [None] * cuts
    for step in range(last):
        up_pairs = [(h, h + 2) for h in range(head_size) if h // 2 <= step and h // 2 < last]
        down_pairs = [(h, h - 2) for h in range(head_size) if last - h // 2 <= step and h // 2 > 0]
        for cut in range(cuts):
            up = chunk(last + line - step, cut)
            down = chunk(line - last + step, cut)
            if passing[cut] is not None:
                if cut > 0:
                    passing[cut], sent = lax.optimization_barrier((passing[cut], sent))
                up = up + passing[cut][0].astype(F32)
                down = down + passing[cut][1].astype(F32)
            up, down = lax.optimization_barrier((up.astype(BF16), down.astype(BF16)))
            sent = up
            passing[cut] = lax.optimization_barrier(
                (lax.ppermute(up, "head", up_pairs), lax.ppermute(down, "head", down_pairs))
            )
    base = hidden_states.astype(F32) + dense_bias.astype(F32)
    done = [
        base[cut * height : (cut + 1) * height]
        + (chunk(line, cut) + passing[cut][0].astype(F32) + passing[cut][1].astype(F32))
        for cut in range(cuts)
    ]
    return jnp.concatenate(done, axis=0).astype(BF16)


def solution(mesh):
    placed = (
        P("tok", "head"),
        P(),
        P(),
        P("tok", "head"),
        P("head"),
        P("head", None),
        P("head"),
        P("tok", None, "head"),
        P("tok", None, "head"),
        P("tok", None),
        P("tok", None),
        P(),
    )
    return jax.shard_map(
        on_device, mesh=mesh, in_specs=placed, out_specs=P("tok", "head"), check_vma=False
    )
```

```python
import functools
import math

import jax
import jax.numpy as jnp
from jax import lax
from jax.experimental import pallas as pl
from jax.experimental.pallas import tpu as pltpu
from jax.sharding import PartitionSpec as P

HS = 96
GROUP_HEADS = 4
GW = GROUP_HEADS * HS
PACK = 128
F32 = jnp.float32
BF16 = jnp.bfloat16
VMEM_LIMIT = 56 * 1024 * 1024
SCALE = 1.0 / math.sqrt(HS)
LOG2E = math.log2(math.e)


def windows():
    found = []
    for k in range(GROUP_HEADS):
        first = k * HS // 128 * 128
        last = -(-(k * HS + HS) // 128) * 128
        found.append((first, last - first))
    return found


def head_mask(k, first, shape):
    lane = lax.broadcasted_iota(jnp.int32, shape, 1) + first
    return (lane >= k * HS) & (lane < (k + 1) * HS)


def params():
    return pltpu.CompilerParams(vmem_limit_bytes=VMEM_LIMIT)


def norm_kernel(values, gain, shift, out):
    widened = values[...].astype(F32)
    center = jnp.mean(widened, axis=-1, keepdims=True)
    moved = widened - center
    spread = jnp.mean(jnp.square(moved), axis=-1, keepdims=True)
    out[...] = (moved * lax.rsqrt(spread + 1e-05) * gain[...] + shift[...]).astype(BF16)


def layer_norm(values, gain, shift):
    rows, features = values.shape
    tile = 64
    return pl.pallas_call(
        norm_kernel,
        out_shape=jax.ShapeDtypeStruct((rows, features), BF16),
        grid=(rows // tile,),
        in_specs=[
            pl.BlockSpec((tile, features), lambda i: (i, 0)),
            pl.BlockSpec((1, features), lambda i: (0, 0)),
            pl.BlockSpec((1, features), lambda i: (0, 0)),
        ],
        out_specs=pl.BlockSpec((tile, features), lambda i: (i, 0)),
        compiler_params=params(),
        cost_estimate=pl.CostEstimate(
            flops=rows * features * 8, bytes_accessed=rows * features * 4, transcendentals=rows
        ),
        name="norm",
    )(values, gain[None, :], shift[None, :])


def shard_layout(lengths, ordering, row_count):
    group_count = lengths.shape[0]
    labels = jnp.arange(group_count, dtype=jnp.int32)
    chosen = (ordering[:, None] == labels[None, :]).astype(jnp.int32)
    ranking = jnp.sum(labels[:, None] * chosen, axis=0)
    earlier = (ranking[None, :] < ranking[:, None]).astype(jnp.int32)
    starts = jnp.sum(earlier * lengths[None, :], axis=1)
    places = jnp.arange(row_count, dtype=jnp.int32)
    member = (
        (places[:, None] >= starts[None, :]) & (places[:, None] < (starts + lengths)[None, :])
    ).astype(jnp.int32)
    row_start = jnp.sum(member * starts[None, :], axis=1)
    return starts, row_start, places - row_start


def rotary_tables(positions):
    rot = HS // 4
    half = rot // 2
    inverse = 10000.0 ** (-(jnp.arange(half, dtype=F32) * 2.0) / rot)
    angles = positions.astype(F32)[:, None] * inverse[None, :]
    cosine, sine = jnp.cos(angles), jnp.sin(angles)
    rows = positions.shape[0]
    rest = jnp.zeros((rows, HS - rot), F32)
    none = jnp.zeros((rows, half), F32)
    straight = jnp.concatenate([cosine, cosine, rest + 1.0], axis=1)
    upper = jnp.concatenate([-sine, none, rest], axis=1)
    lower = jnp.concatenate([none, sine, rest], axis=1)
    return [jnp.tile(table, (1, GROUP_HEADS)) for table in (straight, upper, lower)]


def part_kernel(wide, out):
    columns = wide[...].astype(F32)
    for c in range(3):
        merged = [None] * (GW // 128)
        for k, (first, width) in enumerate(windows()):
            source = 2 * HS * k + HS * c + first
            cut = columns[:, source : source + width]
            mask = head_mask(k, first, cut.shape)
            for w in range(width // 128):
                at = first // 128 + w
                lanes = slice(w * 128, w * 128 + 128)
                if merged[at] is None:
                    merged[at] = cut[:, lanes]
                else:
                    merged[at] = jnp.where(mask[:, lanes], cut[:, lanes], merged[at])
        for at, piece in enumerate(merged):
            first = c * GW + at * 128
            out[:, first : first + 128] = piece.astype(BF16)


def part_by_part(weight, group):
    rows = weight.shape[0]
    tile = 128
    return pl.pallas_call(
        part_kernel,
        out_shape=jax.ShapeDtypeStruct((rows, 3 * GW), BF16),
        grid=(rows // tile,),
        in_specs=[pl.BlockSpec((tile, 3 * GW), lambda i: (i, group))],
        out_specs=pl.BlockSpec((tile, 3 * GW), lambda i: (i, 0)),
        compiler_params=params(),
        cost_estimate=pl.CostEstimate(
            flops=rows * GW * 12, bytes_accessed=rows * GW * 12, transcendentals=0
        ),
        name="parts",
    )(weight)


def qkv_kernel(pieces, order, normed, *refs):
    weights = refs[:pieces]
    bias, straight, upper, lower, q_out, k_out, v_out = refs[pieces : pieces + 7]
    total, held_rows, held_weights, row_sems, weight_sems = refs[pieces + 7 :]
    depth = weights[0].shape[0]

    def row_copy(j):
        lanes = pl.ds(pl.multiple_of(order[j] * depth, 128), depth)
        return pltpu.make_async_copy(normed.at[:, lanes], held_rows.at[j], row_sems.at[j])

    def weight_copy(j):
        return pltpu.make_async_copy(weights[j], held_weights.at[j], weight_sems.at[j])

    for j in range(pieces):
        row_copy(j).start()
        weight_copy(j).start()
    for j in range(pieces):
        row_copy(j).wait()
        weight_copy(j).wait()
        part = jnp.dot(held_rows[j], held_weights[j], preferred_element_type=F32)
        if j == 0:
            total[...] = part
        else:
            total[...] += part

    tile = 64

    def body(i, carry):
        rows = pl.ds(pl.multiple_of(i * tile, tile), tile)

        def part(c):
            lanes = slice(c * GW, (c + 1) * GW)
            return total[rows, lanes] + bias[:, lanes]

        def turn(x):
            return (
                x * straight[rows, :]
                + pltpu.roll(x, GW - HS // 8, 1) * upper[rows, :]
                + pltpu.roll(x, HS // 8, 1) * lower[rows, :]
            )

        q_out[rows, :] = turn(part(0)).astype(BF16)
        k_out[rows, :] = turn(part(1)).astype(BF16)
        v_out[rows, :] = part(2).astype(BF16)
        return carry

    lax.fori_loop(0, total.shape[0] // tile, body, 0)


def project(normed, weights, order, bias, tables):
    rows, features = normed.shape
    pieces = len(weights)
    depth, columns = weights[0].shape
    out = jax.ShapeDtypeStruct((rows, GW), BF16)
    vmem = pl.BlockSpec(memory_space=pltpu.VMEM)
    anywhere = pl.BlockSpec(memory_space=pl.ANY)
    return pl.pallas_call(
        functools.partial(qkv_kernel, pieces),
        out_shape=(out, out, out),
        in_specs=[pl.BlockSpec(memory_space=pltpu.SMEM)]
        + [anywhere] * (pieces + 1)
        + [vmem] * 4,
        out_specs=[vmem] * 3,
        scratch_shapes=[
            pltpu.VMEM((rows, columns), F32),
            pltpu.VMEM((pieces, rows, depth), BF16),
            pltpu.VMEM((pieces, depth, columns), BF16),
            pltpu.SemaphoreType.DMA((pieces,)),
            pltpu.SemaphoreType.DMA((pieces,)),
        ],
        compiler_params=params(),
        cost_estimate=pl.CostEstimate(
            flops=2 * rows * features * columns,
            bytes_accessed=2 * features * (rows + columns) + 9 * rows * GW * 2,
            transcendentals=0,
        ),
        name="project",
    )(order, normed, *weights, bias, *tables)


def prefix_kernel(blocks, starts, lengths, *refs):
    queries = refs[:blocks]
    k_own, k_other, v_own, v_other = refs[blocks : blocks + 4]
    outs = refs[blocks + 4 : 2 * blocks + 4]
    totals = refs[2 * blocks + 4]
    slot = pl.program_id(0)
    slots = pl.num_programs(0)
    rows = queries[0].shape[0]
    length = k_own.shape[1]

    @pl.when(slot == 0)
    def _():
        totals[...] = jnp.zeros_like(totals)

    begin, size, offset = [], [], []
    count = 0
    for b in range(blocks):
        begin.append(starts[slot * blocks + b])
        size.append(lengths[slot * blocks + b])
        offset.append(count)
        count = count + size[b]

    def serve(keys, values):
        def tile(base, height):
            down = lax.broadcasted_iota(jnp.int32, (height, 1), 0) + base
            across = lax.broadcasted_iota(jnp.int32, (1, height), 1) + base

            def sources(place, b):
                within = place - offset[b]
                return jnp.where((within >= 0) & (within < size[b]), within + begin[b], -1)

            picked = None
            for b in range(blocks):
                spread = lax.broadcasted_iota(jnp.int32, (height, rows), 1)
                one_hot = jnp.where(spread == sources(down, b), 1.0, 0.0).astype(BF16)
                part = jnp.dot(one_hot, queries[b][...], preferred_element_type=F32)
                picked = part if picked is None else picked + part
            picked = picked.astype(BF16)
            merged = [jnp.zeros((height, 128), F32) for _ in range(GW // 128)]
            extra = jnp.zeros((height, PACK), F32)
            place = lax.broadcasted_iota(jnp.int32, (height, PACK), 1)
            for k, (first, width) in enumerate(windows()):
                lanes = slice(first, first + width)
                mask = head_mask(k, first, (height, width))
                query = jnp.where(mask, picked[:, lanes], jnp.zeros((), BF16))
                scores = lax.dot_general(
                    query,
                    keys[0, :, lanes],
                    (((1,), (1,)), ((), ())),
                    preferred_element_type=F32,
                )
                peak = jnp.max(scores, axis=1, keepdims=True)
                weights = jnp.exp2((scores - peak) * (SCALE * LOG2E))
                mass = jnp.sum(weights, axis=1, keepdims=True)
                blended = jnp.dot(
                    weights.astype(BF16), values[0, :, lanes], preferred_element_type=F32
                )
                blended = blended * (1.0 / mass)
                for w in range(width // 128):
                    at = first // 128 + w
                    cut = slice(w * 128, w * 128 + 128)
                    merged[at] = jnp.where(mask[:, cut], blended[:, cut], merged[at])
                level = peak * SCALE + jnp.log(mass)
                high = level.astype(BF16).astype(F32)
                middle = (level - high).astype(BF16).astype(F32)
                low = level - high - middle
                for n, term in enumerate((high, middle, low)):
                    extra = jnp.where(place == 32 * n + k, term, extra)
            packed = jnp.concatenate(merged + [extra], axis=1).astype(BF16)
            for b in range(blocks):
                spread = lax.broadcasted_iota(jnp.int32, (rows, height), 0)
                one_hot = jnp.where(spread == sources(across, b), 1.0, 0.0).astype(BF16)
                totals[b] += jnp.dot(one_hot, packed, preferred_element_type=F32)

        large = 256
        small = 128
        full = lax.div(count, large)
        rest = count - full * large

        def body(j, carry):
            tile(j * large, large)
            return carry

        lax.fori_loop(0, full + jnp.where(rest > small, 1, 0), body, 0)

        @pl.when((rest > 0) & (rest <= small))
        def _():
            tile(full * large, small)

    half = slots // 2

    @pl.when(slot < half)
    def _():
        serve(k_own, v_own)

    @pl.when(slot >= half)
    def _():
        serve(k_other, v_other)

    @pl.when(slot == slots - 1)
    def _():
        for b in range(blocks):
            outs[b][...] = totals[b].astype(BF16)


def prefix_attention(group, queries, cache, starts, lengths):
    blocks = len(queries)
    rows = queries[0].shape[0]
    held, length, _ = cache[0].shape
    width = GW + PACK
    whole = lambda s, starts, lengths: (0, 0)
    own = lambda s, starts, lengths: (jnp.minimum(s, held - 1), 0, group)
    other = lambda s, starts, lengths: (jnp.maximum(s - held, 0), 0, group)
    block = (1, length, GW)
    return pl.pallas_call(
        functools.partial(prefix_kernel, blocks),
        out_shape=[jax.ShapeDtypeStruct((rows, width), BF16)] * blocks,
        grid_spec=pltpu.PrefetchScalarGridSpec(
            num_scalar_prefetch=2,
            grid=(2 * held,),
            in_specs=[pl.BlockSpec((rows, GW), whole)] * blocks
            + [
                pl.BlockSpec(block, own),
                pl.BlockSpec(block, other),
                pl.BlockSpec(block, own),
                pl.BlockSpec(block, other),
            ],
            out_specs=[pl.BlockSpec((rows, width), whole)] * blocks,
            scratch_shapes=[pltpu.VMEM((blocks, rows, width), F32)],
        ),
        compiler_params=params(),
        cost_estimate=pl.CostEstimate(
            flops=4 * rows * length * GROUP_HEADS * 256,
            bytes_accessed=2 * 2 * held * length * GW * 2,
            transcendentals=rows * length * GROUP_HEADS,
        ),
        name="prefix",
    )(starts, lengths, *queries, cache[0], cache[1], cache[2], cache[3])


def suffix_kernel(row_start, queries, keys, values, out, levels):
    rows = queries.shape[0]
    tile = 128
    for i in range(rows // tile):
        at = slice(i * tile, (i + 1) * tile)
        wide = (i + 1) * tile
        row = lax.broadcasted_iota(jnp.int32, (tile, wide), 0) + i * tile
        column = lax.broadcasted_iota(jnp.int32, (tile, wide), 1)
        allowed = (column <= row) & (column >= row_start[at, :])
        merged = [jnp.zeros((tile, 128), F32) for _ in range(GW // 128)]
        level_row = jnp.zeros((tile, PACK), F32)
        place = lax.broadcasted_iota(jnp.int32, (tile, PACK), 1)
        for k, (first, width) in enumerate(windows()):
            lanes = slice(first, first + width)
            mask = head_mask(k, first, (tile, width))
            query = jnp.where(mask, queries[at, lanes], jnp.zeros((), BF16))
            scores = lax.dot_general(
                query,
                keys[:wide, lanes],
                (((1,), (1,)), ((), ())),
                preferred_element_type=F32,
            )
            scores = jnp.where(allowed, scores, -jnp.inf)
            peak = jnp.max(scores, axis=1, keepdims=True)
            weights = jnp.exp2((scores - peak) * (SCALE * LOG2E))
            mass = jnp.sum(weights, axis=1, keepdims=True)
            blended = jnp.dot(
                weights.astype(BF16), values[:wide, lanes], preferred_element_type=F32
            )
            blended = blended * (1.0 / mass)
            for w in range(width // 128):
                spot = first // 128 + w
                cut = slice(w * 128, w * 128 + 128)
                merged[spot] = jnp.where(mask[:, cut], blended[:, cut], merged[spot])
            level_row = jnp.where(place == k, peak * SCALE + jnp.log(mass), level_row)
        out[at, :] = jnp.concatenate(merged, axis=1)
        levels[at, :] = level_row


def suffix_attention(row_start, queries, keys, values):
    rows = queries.shape[0]
    return pl.pallas_call(
        suffix_kernel,
        out_shape=(
            jax.ShapeDtypeStruct((rows, GW), F32),
            jax.ShapeDtypeStruct((rows, PACK), F32),
        ),
        compiler_params=params(),
        cost_estimate=pl.CostEstimate(
            flops=4 * rows * rows * GROUP_HEADS * 256,
            bytes_accessed=rows * GW * 10,
            transcendentals=rows * rows * GROUP_HEADS,
        ),
        name="suffix",
    )(row_start, queries, keys, values)


def merge_kernel(blocks, *refs):
    parts = refs[:blocks]
    suffix, levels, out = refs[blocks:]
    rows = suffix.shape[0]
    tile = 128
    for i in range(rows // tile):
        at = slice(i * tile, (i + 1) * tile)
        prefix = parts[0][at, :].astype(F32)
        for b in range(1, blocks):
            prefix = prefix + parts[b][at, :].astype(F32)
        terms = prefix[:, GW:]
        pre = terms + pltpu.roll(terms, PACK - 32, 1) + pltpu.roll(terms, PACK - 64, 1)
        suf = levels[at, :]
        top = jnp.maximum(pre, suf)
        pre = jnp.exp(pre - top)
        suf = jnp.exp(suf - top)
        shares = pre / (pre + suf)
        spread = jnp.zeros((tile, GW), F32)
        for k in range(GROUP_HEADS):
            spread = jnp.where(head_mask(k, 0, (tile, GW)), shares[:, k : k + 1], spread)
        out[at, :] = (spread * prefix[:, :GW] + (1.0 - spread) * suffix[at, :]).astype(BF16)


def merge(parts, suffix, levels):
    rows = suffix.shape[0]
    return pl.pallas_call(
        functools.partial(merge_kernel, len(parts)),
        out_shape=jax.ShapeDtypeStruct((rows, GW), BF16),
        compiler_params=params(),
        cost_estimate=pl.CostEstimate(
            flops=rows * GW * 8, bytes_accessed=rows * GW * 10, transcendentals=rows * 8
        ),
        name="merge",
    )(*parts, suffix, levels)


def output_kernel(groups, lines, place, *refs):
    attention = refs[: 2 * groups]
    own, landed, crossed, out, held, sems = refs[2 * groups :]
    at = pl.program_id(0)
    rows, share = out.shape[1:]
    depth = own.shape[0]
    half = lines // 2
    side, core = place[0], place[1]

    def own_copy(a):
        lanes = pl.ds(pl.multiple_of((2 * a + side) * share, 128), share)
        return pltpu.make_async_copy(
            own.at[:, lanes], held.at[a, pl.ds(0, depth)], sems.at[2 * a]
        )

    def other_copy(a):
        source = landed if a < half else crossed
        spot = lax.rem(a + core * half, lines)
        lanes = pl.ds((a % half) * share, share)
        return pltpu.make_async_copy(
            source.at[:, lanes], held.at[spot, pl.ds(depth, depth)], sems.at[2 * a + 1]
        )

    @pl.when(at == 0)
    def _():
        for a in range(lines):
            own_copy(a).start()
            other_copy(a).start()

    own_copy(at).wait()
    sent = lax.rem(at + core * half, lines)
    pltpu.make_async_copy(
        landed.at[:, pl.ds(0, share)],
        held.at[at, pl.ds(depth, depth)],
        sems.at[2 * sent + 1],
    ).wait()
    total = None
    for n in range(2 * groups):
        part = jnp.dot(
            attention[n][...],
            held[at, n * GW : (n + 1) * GW, :],
            preferred_element_type=F32,
        )
        total = part if total is None else total + part
    out[0] = total


def output_projection(place, attention, own, landed, crossed, lines):
    rows = attention[0].shape[0]
    depth, features = own.shape
    share = features // (2 * lines)
    vmem = pl.BlockSpec((rows, GW), lambda a, place: (0, 0))
    anywhere = pl.BlockSpec(memory_space=pl.ANY)
    return pl.pallas_call(
        functools.partial(output_kernel, len(attention) // 2, lines),
        out_shape=jax.ShapeDtypeStruct((lines, rows, share), F32),
        grid_spec=pltpu.PrefetchScalarGridSpec(
            num_scalar_prefetch=1,
            grid=(lines,),
            in_specs=[vmem] * len(attention) + [anywhere] * 3,
            out_specs=pl.BlockSpec((1, rows, share), lambda a, place: (a, 0, 0)),
            scratch_shapes=[
                pltpu.VMEM((lines, 2 * depth, share), BF16),
                pltpu.SemaphoreType.DMA((2 * lines,)),
            ],
        ),
        compiler_params=params(),
        cost_estimate=pl.CostEstimate(
            flops=2 * rows * depth * features,
            bytes_accessed=2 * depth * features + 2 * rows * features,
            transcendentals=0,
        ),
        name="output",
    )(place, *attention, own, landed, crossed)


def on_device(
    hidden_states,
    norm_gain,
    norm_bias,
    qkv_weight,
    qkv_bias,
    dense_weight,
    dense_bias,
    prefix_keys,
    prefix_values,
    suffix_len,
    request_order,
    group_slot,
):
    rows, share = hidden_states.shape
    held, prefix_length, local_width = prefix_keys.shape
    groups_local = local_width // GW
    tok_size = lax.axis_size("tok")
    head_size = lax.axis_size("head")
    chips = tok_size // 2
    lines = head_size // 2
    group_count = held * tok_size
    tok = lax.axis_index("tok")
    head = lax.axis_index("head")
    core, chip = tok % 2, tok // 2
    side, line = head % 2, head // 2

    def to_core(x):
        return lax.ppermute(x, "tok", [(t, t ^ 1) for t in range(tok_size)])

    def to_chip(x, shift):
        return lax.ppermute(
            x,
            "tok",
            [(t, (t // 2 + shift) % chips * 2 + t % 2) for t in range(tok_size)],
        )

    def to_side(x):
        return lax.ppermute(x, "head", [(h, h ^ 1) for h in range(head_size)])

    layout = jnp.stack([suffix_len[0], request_order[0]])
    layouts = [layout] + [to_chip(layout, shift) for shift in range(1, chips)]
    full_rows = lax.all_gather(hidden_states, "head", axis=1, tiled=True)

    columns = 3 * GW
    order = [tok, tok ^ 1]
    for shift in range(1, chips):
        source = (chip + chips - shift) % chips * 2 + core
        order += [source, source ^ 1]
    order = jnp.stack(order).astype(jnp.int32)
    first = part_by_part(qkv_weight, 0)
    first, layouts = lax.optimization_barrier((first, layouts))
    arriving = [to_chip(first, shift) for shift in range(1, chips)]
    source, _ = lax.optimization_barrier((qkv_weight, layouts))
    later = [part_by_part(source, g) for g in range(1, groups_local)]
    cache = [prefix_keys, to_core(prefix_keys), prefix_values, to_core(prefix_values)]

    lengths = suffix_len[0]
    starts, row_start, within = shard_layout(lengths, request_order[0], rows)
    labels = jnp.arange(group_count, dtype=jnp.int32)
    slot_match = (group_slot[:, None] == labels[None, :]).astype(jnp.int32)

    def served_spans(one):
        firsts = shard_layout(one[0], one[1], rows)[0]
        spans = jnp.stack(
            [
                jnp.sum(firsts[:, None] * slot_match, axis=0),
                jnp.sum(one[0][:, None] * slot_match, axis=0),
            ]
        )
        return jnp.concatenate(
            [
                lax.dynamic_slice(spans, (0, tok * held), (2, held)),
                lax.dynamic_slice(spans, (0, (tok ^ 1) * held), (2, held)),
            ],
            axis=1,
        )

    served = jnp.stack([served_spans(one) for one in layouts], axis=2)
    tables = rotary_tables(prefix_length + within)
    bias = qkv_bias.astype(F32).reshape(groups_local, GROUP_HEADS, 3, HS)
    bias = jnp.transpose(bias, (0, 2, 1, 3)).reshape(groups_local, 1, columns)
    bias = [bias[g] for g in range(groups_local)]

    half = lines // 2
    outgoing = jnp.concatenate(
        [
            lax.dynamic_slice(
                dense_weight,
                (0, (2 * (core * half + a) + 1 - side) * share),
                (dense_weight.shape[0], share),
            )
            for a in range(half)
        ],
        axis=1,
    )
    ready = (
        served[0].reshape(-1),
        served[1].reshape(-1),
        tables,
        bias,
        order,
        row_start[:, None],
        jnp.stack([side, core]).astype(jnp.int32),
        outgoing,
        cache,
        later,
    )
    arriving, ready = lax.optimization_barrier((arriving, ready))
    span_start, span_length, tables, bias, order, row_start, place, outgoing, cache, later = ready
    weight = [first] + later
    arrived = [arriving]
    for g in range(1, groups_local):
        mine, _ = lax.optimization_barrier((weight[g], arrived[g - 1]))
        arrived.append([to_chip(mine, shift) for shift in range(1, chips)])

    def pieces_of(g):
        pieces = [weight[g], to_core(weight[g])]
        for one in arrived[g]:
            pieces += [one, to_core(one)]
        return pieces

    outgoing, full_rows = lax.optimization_barrier((outgoing, full_rows))
    landed = to_side(outgoing)
    normed = layer_norm(full_rows, norm_gain, norm_bias)
    heads = []
    for g in range(groups_local):
        heads.append(project(normed, pieces_of(g), order, bias[g], tables))
        if g + 1 < groups_local:
            arrived[g + 1], heads[g] = lax.optimization_barrier((arrived[g + 1], heads[g]))
    landed, heads[-1] = lax.optimization_barrier((landed, heads[-1]))
    crossed = to_core(landed)
    asked = [[q] + [to_chip(q, shift) for shift in range(1, chips)] for q, _, _ in heads]
    asked[0], last_heads = lax.optimization_barrier((asked[0], heads[-1]))
    heads[-1] = last_heads
    attention_own, attention_side = [], []
    for g in range(groups_local):
        answers = prefix_attention(g, asked[g], cache, span_start, span_length)
        parts = [answers[0]] + [to_chip(answers[s], chips - s) for s in range(1, chips)]
        suffix, levels = suffix_attention(row_start, *heads[g])
        attention = merge(parts, suffix, levels)
        attention_own.append(attention)
        attention_side.append(to_side(attention))
    partial = output_projection(
        place, attention_own + attention_side, dense_weight, landed, crossed, lines
    )

    last = lines - 1
    cuts = 2
    height = rows // cuts

    def chunk(place, cut):
        place = jnp.clip(place, 0, last)
        return lax.dynamic_slice(
            partial, (place, cut * height, 0), (1, height, share)
        ).reshape(height, share)

    passing = [None] * cuts
    for step in range(last):
        up_pairs = [(h, h + 2) for h in range(head_size) if h // 2 <= step and h // 2 < last]
        down_pairs = [(h, h - 2) for h in range(head_size) if last - h // 2 <= step and h // 2 > 0]
        for cut in range(cuts):
            up = chunk(last + line - step, cut)
            down = chunk(line - last + step, cut)
            if passing[cut] is not None:
                if cut > 0:
                    passing[cut], sent = lax.optimization_barrier((passing[cut], sent))
                up = up + passing[cut][0].astype(F32)
                down = down + passing[cut][1].astype(F32)
            up, down = lax.optimization_barrier((up.astype(BF16), down.astype(BF16)))
            sent = up
            passing[cut] = lax.optimization_barrier(
                (lax.ppermute(up, "head", up_pairs), lax.ppermute(down, "head", down_pairs))
            )
    base = hidden_states.astype(F32) + dense_bias.astype(F32)
    done = [
        base[cut * height : (cut + 1) * height]
        + (chunk(line, cut) + passing[cut][0].astype(F32) + passing[cut][1].astype(F32))
        for cut in range(cuts)
    ]
    return jnp.concatenate(done, axis=0).astype(BF16)


def solution(mesh):
    placed = (
        P("tok", "head"),
        P(),
        P(),
        P("tok", "head"),
        P("head"),
        P("head", None),
        P("head"),
        P("tok", None, "head"),
        P("tok", None, "head"),
        P("tok", None),
        P("tok", None),
        P(),
    )
    return jax.shard_map(
        on_device, mesh=mesh, in_specs=placed, out_specs=P("tok", "head"), check_vma=False
    )
```

```python
import functools
import math

import jax
import jax.numpy as jnp
from jax import lax
from jax.experimental import pallas as pl
from jax.experimental.pallas import tpu as pltpu
from jax.sharding import PartitionSpec as P

HS = 96
GROUP_HEADS = 4
GW = GROUP_HEADS * HS
PACK = 128
F32 = jnp.float32
BF16 = jnp.bfloat16
VMEM_LIMIT = 56 * 1024 * 1024
SCALE = 1.0 / math.sqrt(HS)
LOG2E = math.log2(math.e)


def windows():
    found = []
    for k in range(GROUP_HEADS):
        first = k * HS // 128 * 128
        last = -(-(k * HS + HS) // 128) * 128
        found.append((first, last - first))
    return found


def head_mask(k, first, shape):
    lane = lax.broadcasted_iota(jnp.int32, shape, 1) + first
    return (lane >= k * HS) & (lane < (k + 1) * HS)


def params():
    return pltpu.CompilerParams(vmem_limit_bytes=VMEM_LIMIT)


def norm_kernel(count, places, *refs):
    blocks = refs[:count]
    gain, shift, out, held, sems = refs[count:]
    share = blocks[0].shape[1]

    def copy(j):
        lanes = pl.ds(pl.multiple_of(places[j] * share, 128), share)
        return pltpu.make_async_copy(blocks[j], held.at[:, lanes], sems.at[j])

    for j in range(count):

        @pl.when(places[j] >= 0)
        def _(j=j):
            copy(j).start()

    for j in range(count):

        @pl.when(places[j] >= 0)
        def _(j=j):
            copy(j).wait()

    tile = 32

    def body(i, carry):
        rows = pl.ds(pl.multiple_of(i * tile, tile), tile)
        widened = held[rows, :].astype(F32)
        center = jnp.mean(widened, axis=-1, keepdims=True)
        moved = widened - center
        spread = jnp.mean(jnp.square(moved), axis=-1, keepdims=True)
        out[rows, :] = (moved * lax.rsqrt(spread + 1e-05) * gain[...] + shift[...]).astype(BF16)
        return carry

    lax.fori_loop(0, held.shape[0] // tile, body, 0)


def layer_norm(blocks, places, gain, shift):
    rows = blocks[0].shape[0]
    features = gain.shape[0]
    count = len(blocks)
    vmem = pl.BlockSpec(memory_space=pltpu.VMEM)
    return pl.pallas_call(
        functools.partial(norm_kernel, count),
        out_shape=jax.ShapeDtypeStruct((rows, features), BF16),
        in_specs=[pl.BlockSpec(memory_space=pltpu.SMEM)]
        + [pl.BlockSpec(memory_space=pl.ANY)] * count
        + [vmem] * 2,
        out_specs=vmem,
        scratch_shapes=[
            pltpu.VMEM((rows, features), BF16),
            pltpu.SemaphoreType.DMA((count,)),
        ],
        compiler_params=params(),
        cost_estimate=pl.CostEstimate(
            flops=rows * features * 8, bytes_accessed=rows * features * 4, transcendentals=rows
        ),
        name="norm",
    )(places, *blocks, gain[None, :], shift[None, :])


def shard_layout(lengths, ordering, row_count):
    group_count = lengths.shape[0]
    labels = jnp.arange(group_count, dtype=jnp.int32)
    chosen = (ordering[:, None] == labels[None, :]).astype(jnp.int32)
    ranking = jnp.sum(labels[:, None] * chosen, axis=0)
    earlier = (ranking[None, :] < ranking[:, None]).astype(jnp.int32)
    starts = jnp.sum(earlier * lengths[None, :], axis=1)
    places = jnp.arange(row_count, dtype=jnp.int32)
    member = (
        (places[:, None] >= starts[None, :]) & (places[:, None] < (starts + lengths)[None, :])
    ).astype(jnp.int32)
    row_start = jnp.sum(member * starts[None, :], axis=1)
    return starts, row_start, places - row_start


def rotary_tables(positions):
    rot = HS // 4
    half = rot // 2
    inverse = 10000.0 ** (-(jnp.arange(half, dtype=F32) * 2.0) / rot)
    angles = positions.astype(F32)[:, None] * inverse[None, :]
    cosine, sine = jnp.cos(angles), jnp.sin(angles)
    rows = positions.shape[0]
    rest = jnp.zeros((rows, HS - rot), F32)
    none = jnp.zeros((rows, half), F32)
    straight = jnp.concatenate([cosine, cosine, rest + 1.0], axis=1)
    upper = jnp.concatenate([-sine, none, rest], axis=1)
    lower = jnp.concatenate([none, sine, rest], axis=1)
    return [jnp.tile(table, (1, GROUP_HEADS)) for table in (straight, upper, lower)]


def part_kernel(bundles, wide, *outs):
    columns = wide[...].astype(F32)
    for out, bundle in zip(outs, bundles):
        for spot, c in enumerate(bundle):
            merged = [None] * (GW // 128)
            for k, (first, width) in enumerate(windows()):
                source = 2 * HS * k + HS * c + first
                cut = columns[:, source : source + width]
                mask = head_mask(k, first, cut.shape)
                for w in range(width // 128):
                    at = first // 128 + w
                    lanes = slice(w * 128, w * 128 + 128)
                    if merged[at] is None:
                        merged[at] = cut[:, lanes]
                    else:
                        merged[at] = jnp.where(mask[:, lanes], cut[:, lanes], merged[at])
            for at, piece in enumerate(merged):
                first = spot * GW + at * 128
                out[:, first : first + 128] = piece.astype(BF16)


def part_by_part(weight, group, bundles):
    rows = weight.shape[0]
    tile = 128
    return pl.pallas_call(
        functools.partial(part_kernel, bundles),
        out_shape=[jax.ShapeDtypeStruct((rows, len(b) * GW), BF16) for b in bundles],
        grid=(rows // tile,),
        in_specs=[pl.BlockSpec((tile, 3 * GW), lambda i: (i, group))],
        out_specs=[pl.BlockSpec((tile, len(b) * GW), lambda i: (i, 0)) for b in bundles],
        compiler_params=params(),
        cost_estimate=pl.CostEstimate(
            flops=rows * GW * 12, bytes_accessed=rows * GW * 12, transcendentals=0
        ),
        name="parts",
    )(weight)


def qkv_kernel(pieces, bundle, order, normed, *refs):
    weights = refs[:pieces]
    bias, straight, upper, lower = refs[pieces : pieces + 4]
    outs = refs[pieces + 4 : pieces + 4 + len(bundle)]
    total, held_rows, held_weights, row_sems, weight_sems = refs[pieces + 4 + len(bundle) :]
    depth = weights[0].shape[0]

    def row_copy(j):
        lanes = pl.ds(pl.multiple_of(order[j] * depth, 128), depth)
        return pltpu.make_async_copy(normed.at[:, lanes], held_rows.at[j], row_sems.at[j])

    def weight_copy(j):
        return pltpu.make_async_copy(weights[j], held_weights.at[j], weight_sems.at[j])

    for j in range(pieces):
        row_copy(j).start()
        weight_copy(j).start()
    for j in range(pieces):
        row_copy(j).wait()
        weight_copy(j).wait()
        part = jnp.dot(held_rows[j], held_weights[j], preferred_element_type=F32)
        if j == 0:
            total[...] = part
        else:
            total[...] += part

    tile = 64

    def body(i, carry):
        rows = pl.ds(pl.multiple_of(i * tile, tile), tile)
        for spot, c in enumerate(bundle):
            lanes = slice(spot * GW, (spot + 1) * GW)
            x = total[rows, lanes] + bias[:, lanes]
            if c < 2:
                x = (
                    x * straight[rows, :]
                    + pltpu.roll(x, GW - HS // 8, 1) * upper[rows, :]
                    + pltpu.roll(x, HS // 8, 1) * lower[rows, :]
                )
            outs[spot][rows, :] = x.astype(BF16)
        return carry

    lax.fori_loop(0, total.shape[0] // tile, body, 0)


def project(normed, weights, order, bias, tables, bundle):
    rows, features = normed.shape
    pieces = len(weights)
    depth, columns = weights[0].shape
    out = jax.ShapeDtypeStruct((rows, GW), BF16)
    vmem = pl.BlockSpec(memory_space=pltpu.VMEM)
    anywhere = pl.BlockSpec(memory_space=pl.ANY)
    return pl.pallas_call(
        functools.partial(qkv_kernel, pieces, bundle),
        out_shape=[out] * len(bundle),
        in_specs=[pl.BlockSpec(memory_space=pltpu.SMEM)]
        + [anywhere] * (pieces + 1)
        + [vmem] * 4,
        out_specs=[vmem] * len(bundle),
        scratch_shapes=[
            pltpu.VMEM((rows, columns), F32),
            pltpu.VMEM((pieces, rows, depth), BF16),
            pltpu.VMEM((pieces, depth, columns), BF16),
            pltpu.SemaphoreType.DMA((pieces,)),
            pltpu.SemaphoreType.DMA((pieces,)),
        ],
        compiler_params=params(),
        cost_estimate=pl.CostEstimate(
            flops=2 * rows * features * columns,
            bytes_accessed=2 * features * (rows + columns) + 9 * rows * GW * 2,
            transcendentals=0,
        ),
        name="project",
    )(order, normed, *weights, bias, *tables)


def prefix_kernel(blocks, starts, lengths, *refs):
    queries = refs[:blocks]
    k_own, k_other, v_own, v_other = refs[blocks : blocks + 4]
    outs = refs[blocks + 4 : 2 * blocks + 4]
    totals = refs[2 * blocks + 4]
    slot = pl.program_id(0)
    slots = pl.num_programs(0)
    rows = queries[0].shape[0]
    length = k_own.shape[1]

    @pl.when(slot == 0)
    def _():
        totals[...] = jnp.zeros_like(totals)

    begin, size, offset = [], [], []
    count = 0
    for b in range(blocks):
        begin.append(starts[slot * blocks + b])
        size.append(lengths[slot * blocks + b])
        offset.append(count)
        count = count + size[b]

    def serve(keys, values):
        def tile(base, height):
            down = lax.broadcasted_iota(jnp.int32, (height, 1), 0) + base
            across = lax.broadcasted_iota(jnp.int32, (1, height), 1) + base

            def sources(place, b):
                within = place - offset[b]
                return jnp.where((within >= 0) & (within < size[b]), within + begin[b], -1)

            picked = None
            for b in range(blocks):
                spread = lax.broadcasted_iota(jnp.int32, (height, rows), 1)
                one_hot = jnp.where(spread == sources(down, b), 1.0, 0.0).astype(BF16)
                part = jnp.dot(one_hot, queries[b][...], preferred_element_type=F32)
                picked = part if picked is None else picked + part
            picked = picked.astype(BF16)
            merged = [jnp.zeros((height, 128), F32) for _ in range(GW // 128)]
            extra = jnp.zeros((height, PACK), F32)
            place = lax.broadcasted_iota(jnp.int32, (height, PACK), 1)
            for k, (first, width) in enumerate(windows()):
                lanes = slice(first, first + width)
                mask = head_mask(k, first, (height, width))
                query = jnp.where(mask, picked[:, lanes], jnp.zeros((), BF16))
                scores = lax.dot_general(
                    query,
                    keys[0, :, lanes],
                    (((1,), (1,)), ((), ())),
                    preferred_element_type=F32,
                )
                peak = jnp.max(scores, axis=1, keepdims=True)
                weights = jnp.exp2((scores - peak) * (SCALE * LOG2E))
                mass = jnp.sum(weights, axis=1, keepdims=True)
                blended = jnp.dot(
                    weights.astype(BF16), values[0, :, lanes], preferred_element_type=F32
                )
                blended = blended * (1.0 / mass)
                for w in range(width // 128):
                    at = first // 128 + w
                    cut = slice(w * 128, w * 128 + 128)
                    merged[at] = jnp.where(mask[:, cut], blended[:, cut], merged[at])
                level = peak * SCALE + jnp.log(mass)
                high = level.astype(BF16).astype(F32)
                middle = (level - high).astype(BF16).astype(F32)
                low = level - high - middle
                for n, term in enumerate((high, middle, low)):
                    extra = jnp.where(place == 32 * n + k, term, extra)
            packed = jnp.concatenate(merged + [extra], axis=1).astype(BF16)
            for b in range(blocks):
                spread = lax.broadcasted_iota(jnp.int32, (rows, height), 0)
                one_hot = jnp.where(spread == sources(across, b), 1.0, 0.0).astype(BF16)
                totals[b] += jnp.dot(one_hot, packed, preferred_element_type=F32)

        large = 256
        small = 128
        full = lax.div(count, large)
        rest = count - full * large

        def body(j, carry):
            tile(j * large, large)
            return carry

        lax.fori_loop(0, full + jnp.where(rest > small, 1, 0), body, 0)

        @pl.when((rest > 0) & (rest <= small))
        def _():
            tile(full * large, small)

    half = slots // 2

    @pl.when(slot < half)
    def _():
        serve(k_own, v_own)

    @pl.when(slot >= half)
    def _():
        serve(k_other, v_other)

    @pl.when(slot == slots - 1)
    def _():
        for b in range(blocks):
            outs[b][...] = totals[b].astype(BF16)


def prefix_attention(group, queries, cache, starts, lengths):
    blocks = len(queries)
    rows = queries[0].shape[0]
    held, length, _ = cache[0].shape
    width = GW + PACK
    whole = lambda s, starts, lengths: (0, 0)
    own = lambda s, starts, lengths: (jnp.minimum(s, held - 1), 0, group)
    other = lambda s, starts, lengths: (jnp.maximum(s - held, 0), 0, group)
    block = (1, length, GW)
    return pl.pallas_call(
        functools.partial(prefix_kernel, blocks),
        out_shape=[jax.ShapeDtypeStruct((rows, width), BF16)] * blocks,
        grid_spec=pltpu.PrefetchScalarGridSpec(
            num_scalar_prefetch=2,
            grid=(2 * held,),
            in_specs=[pl.BlockSpec((rows, GW), whole)] * blocks
            + [
                pl.BlockSpec(block, own),
                pl.BlockSpec(block, other),
                pl.BlockSpec(block, own),
                pl.BlockSpec(block, other),
            ],
            out_specs=[pl.BlockSpec((rows, width), whole)] * blocks,
            scratch_shapes=[pltpu.VMEM((blocks, rows, width), F32)],
        ),
        compiler_params=params(),
        cost_estimate=pl.CostEstimate(
            flops=4 * rows * length * GROUP_HEADS * 256,
            bytes_accessed=2 * 2 * held * length * GW * 2,
            transcendentals=rows * length * GROUP_HEADS,
        ),
        name="prefix",
    )(starts, lengths, *queries, cache[0], cache[1], cache[2], cache[3])


def suffix_kernel(row_start, queries, keys, values, out, levels):
    rows = queries.shape[0]
    tile = 128
    for i in range(rows // tile):
        at = slice(i * tile, (i + 1) * tile)
        wide = (i + 1) * tile
        row = lax.broadcasted_iota(jnp.int32, (tile, wide), 0) + i * tile
        column = lax.broadcasted_iota(jnp.int32, (tile, wide), 1)
        allowed = (column <= row) & (column >= row_start[at, :])
        merged = [jnp.zeros((tile, 128), F32) for _ in range(GW // 128)]
        level_row = jnp.zeros((tile, PACK), F32)
        place = lax.broadcasted_iota(jnp.int32, (tile, PACK), 1)
        for k, (first, width) in enumerate(windows()):
            lanes = slice(first, first + width)
            mask = head_mask(k, first, (tile, width))
            query = jnp.where(mask, queries[at, lanes], jnp.zeros((), BF16))
            scores = lax.dot_general(
                query,
                keys[:wide, lanes],
                (((1,), (1,)), ((), ())),
                preferred_element_type=F32,
            )
            scores = jnp.where(allowed, scores, -jnp.inf)
            peak = jnp.max(scores, axis=1, keepdims=True)
            weights = jnp.exp2((scores - peak) * (SCALE * LOG2E))
            mass = jnp.sum(weights, axis=1, keepdims=True)
            blended = jnp.dot(
                weights.astype(BF16), values[:wide, lanes], preferred_element_type=F32
            )
            blended = blended * (1.0 / mass)
            for w in range(width // 128):
                spot = first // 128 + w
                cut = slice(w * 128, w * 128 + 128)
                merged[spot] = jnp.where(mask[:, cut], blended[:, cut], merged[spot])
            level_row = jnp.where(place == k, peak * SCALE + jnp.log(mass), level_row)
        out[at, :] = jnp.concatenate(merged, axis=1)
        levels[at, :] = level_row


def suffix_attention(row_start, queries, keys, values):
    rows = queries.shape[0]
    return pl.pallas_call(
        suffix_kernel,
        out_shape=(
            jax.ShapeDtypeStruct((rows, GW), F32),
            jax.ShapeDtypeStruct((rows, PACK), F32),
        ),
        compiler_params=params(),
        cost_estimate=pl.CostEstimate(
            flops=4 * rows * rows * GROUP_HEADS * 256,
            bytes_accessed=rows * GW * 10,
            transcendentals=rows * rows * GROUP_HEADS,
        ),
        name="suffix",
    )(row_start, queries, keys, values)


def merge_kernel(blocks, *refs):
    parts = refs[:blocks]
    suffix, levels, out = refs[blocks:]
    rows = suffix.shape[0]
    tile = 128
    for i in range(rows // tile):
        at = slice(i * tile, (i + 1) * tile)
        prefix = parts[0][at, :].astype(F32)
        for b in range(1, blocks):
            prefix = prefix + parts[b][at, :].astype(F32)
        terms = prefix[:, GW:]
        pre = terms + pltpu.roll(terms, PACK - 32, 1) + pltpu.roll(terms, PACK - 64, 1)
        suf = levels[at, :]
        top = jnp.maximum(pre, suf)
        pre = jnp.exp(pre - top)
        suf = jnp.exp(suf - top)
        shares = pre / (pre + suf)
        spread = jnp.zeros((tile, GW), F32)
        for k in range(GROUP_HEADS):
            spread = jnp.where(head_mask(k, 0, (tile, GW)), shares[:, k : k + 1], spread)
        out[at, :] = (spread * prefix[:, :GW] + (1.0 - spread) * suffix[at, :]).astype(BF16)


def merge(parts, suffix, levels):
    rows = suffix.shape[0]
    return pl.pallas_call(
        functools.partial(merge_kernel, len(parts)),
        out_shape=jax.ShapeDtypeStruct((rows, GW), BF16),
        compiler_params=params(),
        cost_estimate=pl.CostEstimate(
            flops=rows * GW * 8, bytes_accessed=rows * GW * 10, transcendentals=rows * 8
        ),
        name="merge",
    )(*parts, suffix, levels)


def output_kernel(groups, lines, place, *refs):
    attention = refs[: 2 * groups]
    own, landed, crossed, out, held, sems = refs[2 * groups :]
    at = pl.program_id(0)
    rows, share = out.shape[1:]
    depth = own.shape[0]
    half = lines // 2
    side, core = place[0], place[1]

    def own_copy(a):
        lanes = pl.ds(pl.multiple_of((2 * a + side) * share, 128), share)
        return pltpu.make_async_copy(
            own.at[:, lanes], held.at[a, pl.ds(0, depth)], sems.at[2 * a]
        )

    def other_copy(a):
        source = landed if a < half else crossed
        spot = lax.rem(a + core * half, lines)
        lanes = pl.ds((a % half) * share, share)
        return pltpu.make_async_copy(
            source.at[:, lanes], held.at[spot, pl.ds(depth, depth)], sems.at[2 * a + 1]
        )

    @pl.when(at == 0)
    def _():
        for a in range(lines):
            own_copy(a).start()
            other_copy(a).start()

    own_copy(at).wait()
    sent = lax.rem(at + core * half, lines)
    pltpu.make_async_copy(
        landed.at[:, pl.ds(0, share)],
        held.at[at, pl.ds(depth, depth)],
        sems.at[2 * sent + 1],
    ).wait()
    total = None
    for n in range(2 * groups):
        part = jnp.dot(
            attention[n][...],
            held[at, n * GW : (n + 1) * GW, :],
            preferred_element_type=F32,
        )
        total = part if total is None else total + part
    out[0] = total


def output_projection(place, attention, own, landed, crossed, lines):
    rows = attention[0].shape[0]
    depth, features = own.shape
    share = features // (2 * lines)
    vmem = pl.BlockSpec((rows, GW), lambda a, place: (0, 0))
    anywhere = pl.BlockSpec(memory_space=pl.ANY)
    return pl.pallas_call(
        functools.partial(output_kernel, len(attention) // 2, lines),
        out_shape=jax.ShapeDtypeStruct((lines, rows, share), F32),
        grid_spec=pltpu.PrefetchScalarGridSpec(
            num_scalar_prefetch=1,
            grid=(lines,),
            in_specs=[vmem] * len(attention) + [anywhere] * 3,
            out_specs=pl.BlockSpec((1, rows, share), lambda a, place: (a, 0, 0)),
            scratch_shapes=[
                pltpu.VMEM((lines, 2 * depth, share), BF16),
                pltpu.SemaphoreType.DMA((2 * lines,)),
            ],
        ),
        compiler_params=params(),
        cost_estimate=pl.CostEstimate(
            flops=2 * rows * depth * features,
            bytes_accessed=2 * depth * features + 2 * rows * features,
            transcendentals=0,
        ),
        name="output",
    )(place, *attention, own, landed, crossed)


def on_device(
    hidden_states,
    norm_gain,
    norm_bias,
    qkv_weight,
    qkv_bias,
    dense_weight,
    dense_bias,
    prefix_keys,
    prefix_values,
    suffix_len,
    request_order,
    group_slot,
):
    rows, share = hidden_states.shape
    held, prefix_length, local_width = prefix_keys.shape
    groups_local = local_width // GW
    tok_size = lax.axis_size("tok")
    head_size = lax.axis_size("head")
    chips = tok_size // 2
    lines = head_size // 2
    group_count = held * tok_size
    tok = lax.axis_index("tok")
    head = lax.axis_index("head")
    core, chip = tok % 2, tok // 2
    side, line = head % 2, head // 2

    def to_core(x):
        return lax.ppermute(x, "tok", [(t, t ^ 1) for t in range(tok_size)])

    def to_chip(x, shift):
        return lax.ppermute(
            x,
            "tok",
            [(t, (t // 2 + shift) % chips * 2 + t % 2) for t in range(tok_size)],
        )

    def to_side(x):
        return lax.ppermute(x, "head", [(h, h ^ 1) for h in range(head_size)])

    def after(x, *others):
        return lax.optimization_barrier((x, others))[0]

    layout = jnp.stack([suffix_len[0], request_order[0]])
    layouts = [layout] + [to_chip(layout, shift) for shift in range(1, chips)]
    (first,) = part_by_part(qkv_weight, 0, ((0, 1, 2),))
    first, layouts = lax.optimization_barrier((first, layouts))

    last = lines - 1

    def to_side_from(x, lowest, highest):
        return lax.ppermute(
            x, "head", [(h, h ^ 1) for h in range(head_size) if lowest <= h // 2 <= highest]
        )

    across = to_side(hidden_states)
    blocks = [hidden_states, across]
    places = [head, head ^ 1]
    arriving = [to_chip(first, shift) for shift in range(1, chips)]
    up = down = hidden_states
    settled = across
    for step in range(last):
        if step > 0:
            up, down, settled, first = lax.optimization_barrier((up, down, settled, first))
            blocks[4 * step - 5 if step > 1 else 1] = settled
        up = lax.ppermute(
            up, "head", [(h, h + 2) for h in range(head_size) if step <= h // 2 < last]
        )
        down = lax.ppermute(
            down, "head", [(h, h - 2) for h in range(head_size) if 0 < h // 2 <= last - step]
        )
        settled = across if step == 0 else blocks[4 * step - 1]
        blocks += [up, to_side_from(up, step + 1, last)]
        blocks += [down, to_side_from(down, 0, last - 1 - step)]
        for there, valid in (
            (line - 1 - step, line >= step + 1),
            (line + 1 + step, line + 1 + step <= last),
        ):
            places += [
                jnp.where(valid, 2 * there + side, -1),
                jnp.where(valid, 2 * there + 1 - side, -1),
            ]
    places = jnp.stack(places).astype(jnp.int32)

    columns = 3 * GW
    order = [tok, tok ^ 1]
    for shift in range(1, chips):
        source = (chip + chips - shift) % chips * 2 + core
        order += [source, source ^ 1]
    order = jnp.stack(order).astype(jnp.int32)
    source, _ = lax.optimization_barrier((qkv_weight, layouts))
    later = [part_by_part(source, g, ((0, 1), (2,))) for g in range(1, groups_local)]
    lengths = suffix_len[0]
    starts, row_start, within = shard_layout(lengths, request_order[0], rows)
    labels = jnp.arange(group_count, dtype=jnp.int32)
    slot_match = (group_slot[:, None] == labels[None, :]).astype(jnp.int32)

    def served_spans(one):
        firsts = shard_layout(one[0], one[1], rows)[0]
        spans = jnp.stack(
            [
                jnp.sum(firsts[:, None] * slot_match, axis=0),
                jnp.sum(one[0][:, None] * slot_match, axis=0),
            ]
        )
        return jnp.concatenate(
            [
                lax.dynamic_slice(spans, (0, tok * held), (2, held)),
                lax.dynamic_slice(spans, (0, (tok ^ 1) * held), (2, held)),
            ],
            axis=1,
        )

    served = jnp.stack([served_spans(one) for one in layouts], axis=2)
    tables = rotary_tables(prefix_length + within)
    bias = qkv_bias.astype(F32).reshape(groups_local, GROUP_HEADS, 3, HS)
    bias = jnp.transpose(bias, (0, 2, 1, 3)).reshape(groups_local, 1, columns)
    bias = [
        [bias[g]] if g == 0 else [bias[g][:, : 2 * GW], bias[g][:, 2 * GW :]]
        for g in range(groups_local)
    ]

    half = lines // 2
    outgoing = jnp.concatenate(
        [
            lax.dynamic_slice(
                dense_weight,
                (0, (2 * (core * half + a) + 1 - side) * share),
                (dense_weight.shape[0], share),
            )
            for a in range(half)
        ],
        axis=1,
    )
    ready = (
        served[0].reshape(-1),
        served[1].reshape(-1),
        tables,
        bias,
        order,
        row_start[:, None],
        jnp.stack([side, core]).astype(jnp.int32),
        outgoing,
        later,
        places,
        blocks,
    )
    arriving, ready = lax.optimization_barrier((arriving, ready))
    span_start, span_length, tables, bias, order, row_start, place, outgoing, later = ready[:9]
    places, blocks = ready[9:]

    def send(mine):
        return [to_chip(mine, shift) for shift in range(1, chips)]

    def pieces_of(mine, arrived):
        pieces = [mine, to_core(mine)]
        for one in arrived:
            pieces += [one, to_core(one)]
        return pieces

    def exchange(queries):
        return [queries] + [to_chip(queries, shift) for shift in range(1, chips)]

    coming = [send(after(one[0], arriving)) for one in later]
    pieces = pieces_of(first, arriving)
    keys_core = to_core(after(prefix_keys, arriving))
    normed = layer_norm(blocks, places, norm_gain, norm_bias)
    cache = [prefix_keys, keys_core, prefix_values, to_core(after(prefix_values, normed))]
    outgoing = after(outgoing, blocks[1:])
    landed = to_side(outgoing)
    heads = [project(normed, pieces, order, bias[0][0], tables, (0, 1, 2))]
    asked = [exchange(heads[0][0])]
    suffixes = [suffix_attention(row_start, *heads[0])]
    settled = suffixes[0]
    values_coming = []
    for g in range(1, groups_local):
        arrived = after(coming[g - 1], settled)
        pair = project(
            normed, pieces_of(later[g - 1][0], arrived), order, bias[g][0], tables, (0, 1)
        )
        asked.append(exchange(pair[0]))
        heads.append(pair)
        settled = pair
        values_coming.append(send(after(later[g - 1][1], pair, asked[0][1:])))
    asked[0] = after(asked[0], settled)
    returned = []
    for g in range(groups_local):
        if g > 0:
            arrived = after(values_coming[g - 1], answers)
            (values,) = project(
                normed, pieces_of(later[g - 1][1], arrived), order, bias[g][1], tables, (2,)
            )
            asked[g], values = lax.optimization_barrier((asked[g], values))
            suffixes.append((heads[g][0], heads[g][1], values))
        answers = prefix_attention(g, asked[g], cache, span_start, span_length)
        returned.append([answers[0]] + [to_chip(answers[s], chips - s) for s in range(1, chips)])
        if g == 0:
            crossed = to_core(after(landed, answers))
    for g in range(1, groups_local):
        q, k, v = suffixes[g]
        suffixes[g] = suffix_attention(after(row_start, answers), q, k, v)
    attention_own, attention_side = [], []
    for g in range(groups_local):
        attention = merge(returned[g], *suffixes[g])
        attention_own.append(attention)
        attention_side.append(to_side(attention))
    partial = output_projection(
        place, attention_own + attention_side, dense_weight, landed, crossed, lines
    )

    cuts = 2
    height = rows // cuts

    def chunk(place, cut):
        place = jnp.clip(place, 0, last)
        return lax.dynamic_slice(
            partial, (place, cut * height, 0), (1, height, share)
        ).reshape(height, share)

    passing = [None] * cuts
    for step in range(last):
        up_pairs = [(h, h + 2) for h in range(head_size) if h // 2 <= step and h // 2 < last]
        down_pairs = [(h, h - 2) for h in range(head_size) if last - h // 2 <= step and h // 2 > 0]
        for cut in range(cuts):
            up = chunk(last + line - step, cut)
            down = chunk(line - last + step, cut)
            if passing[cut] is not None:
                if cut > 0:
                    passing[cut], sent = lax.optimization_barrier((passing[cut], sent))
                up = up + passing[cut][0].astype(F32)
                down = down + passing[cut][1].astype(F32)
            up, down = lax.optimization_barrier((up.astype(BF16), down.astype(BF16)))
            sent = up
            passing[cut] = lax.optimization_barrier(
                (lax.ppermute(up, "head", up_pairs), lax.ppermute(down, "head", down_pairs))
            )
    base = hidden_states.astype(F32) + dense_bias.astype(F32)
    done = [
        base[cut * height : (cut + 1) * height]
        + (chunk(line, cut) + passing[cut][0].astype(F32) + passing[cut][1].astype(F32))
        for cut in range(cuts)
    ]
    return jnp.concatenate(done, axis=0).astype(BF16)


def solution(mesh):
    placed = (
        P("tok", "head"),
        P(),
        P(),
        P("tok", "head"),
        P("head"),
        P("head", None),
        P("head"),
        P("tok", None, "head"),
        P("tok", None, "head"),
        P("tok", None),
        P("tok", None),
        P(),
    )
    return jax.shard_map(
        on_device, mesh=mesh, in_specs=placed, out_specs=P("tok", "head"), check_vma=False
    )
```

```python
import functools
import math

import jax
import jax.numpy as jnp
from jax import lax
from jax.experimental import pallas as pl
from jax.experimental.pallas import tpu as pltpu
from jax.sharding import PartitionSpec as P

HS = 96
GROUP_HEADS = 4
GW = GROUP_HEADS * HS
PACK = 128
F32 = jnp.float32
BF16 = jnp.bfloat16
VMEM_LIMIT = 56 * 1024 * 1024
SCALE = 1.0 / math.sqrt(HS)
LOG2E = math.log2(math.e)
LIGHT = pl.CostEstimate(flops=1000, bytes_accessed=1000, transcendentals=0)


def windows():
    found = []
    for k in range(GROUP_HEADS):
        first = k * HS // 128 * 128
        last = -(-(k * HS + HS) // 128) * 128
        found.append((first, last - first))
    return found


def head_mask(k, first, shape):
    lane = lax.broadcasted_iota(jnp.int32, shape, 1) + first
    return (lane >= k * HS) & (lane < (k + 1) * HS)


def params():
    return pltpu.CompilerParams(vmem_limit_bytes=VMEM_LIMIT)


def norm_kernel(count, chunks, places, *refs):
    blocks = refs[:count]
    gain, shift, out, held, ready, sems, out_sems = refs[count:]
    share = blocks[0].shape[1]
    height = held.shape[0] // chunks
    tile = 32

    def copy(j, chunk):
        lanes = pl.ds(pl.multiple_of(places[j] * share, 128), share)
        rows = pl.ds(chunk * height, height)
        return pltpu.make_async_copy(
            blocks[j].at[rows, :], held.at[rows, lanes], sems.at[j, chunk]
        )

    def out_copy(chunk):
        rows = pl.ds(chunk * height, height)
        return pltpu.make_async_copy(ready.at[rows, :], out.at[rows, :], out_sems.at[chunk])

    for chunk in range(chunks):
        for j in range(count):

            @pl.when(places[j] >= 0)
            def _(j=j, chunk=chunk):
                copy(j, chunk).start()

    for chunk in range(chunks):
        for j in range(count):

            @pl.when(places[j] >= 0)
            def _(j=j, chunk=chunk):
                copy(j, chunk).wait()

        def body(i, carry, chunk=chunk):
            rows = pl.ds(pl.multiple_of(chunk * height + i * tile, tile), tile)
            widened = held[rows, :].astype(F32)
            center = jnp.mean(widened, axis=-1, keepdims=True)
            moved = widened - center
            spread = jnp.mean(jnp.square(moved), axis=-1, keepdims=True)
            scaled = moved * lax.rsqrt(spread + 1e-05) * gain[...] + shift[...]
            ready[rows, :] = scaled.astype(BF16)
            return carry

        lax.fori_loop(0, height // tile, body, 0)
        out_copy(chunk).start()
    for chunk in range(chunks):
        out_copy(chunk).wait()


def layer_norm(blocks, places, gain, shift):
    rows = blocks[0].shape[0]
    features = gain.shape[0]
    count = len(blocks)
    chunks = 4
    vmem = pl.BlockSpec(memory_space=pltpu.VMEM)
    return pl.pallas_call(
        functools.partial(norm_kernel, count, chunks),
        out_shape=jax.ShapeDtypeStruct((rows, features), BF16),
        in_specs=[pl.BlockSpec(memory_space=pltpu.SMEM)]
        + [pl.BlockSpec(memory_space=pl.ANY)] * count
        + [vmem] * 2,
        out_specs=pl.BlockSpec(memory_space=pl.ANY),
        scratch_shapes=[
            pltpu.VMEM((rows, features), BF16),
            pltpu.VMEM((rows, features), BF16),
            pltpu.SemaphoreType.DMA((count, chunks)),
            pltpu.SemaphoreType.DMA((chunks,)),
        ],
        compiler_params=params(),
        cost_estimate=LIGHT,
        name="norm",
    )(places, *blocks, gain[None, :], shift[None, :])


def shard_layout(lengths, ordering, row_count):
    group_count = lengths.shape[0]
    labels = jnp.arange(group_count, dtype=jnp.int32)
    chosen = (ordering[:, None] == labels[None, :]).astype(jnp.int32)
    ranking = jnp.sum(labels[:, None] * chosen, axis=0)
    earlier = (ranking[None, :] < ranking[:, None]).astype(jnp.int32)
    starts = jnp.sum(earlier * lengths[None, :], axis=1)
    places = jnp.arange(row_count, dtype=jnp.int32)
    member = (
        (places[:, None] >= starts[None, :]) & (places[:, None] < (starts + lengths)[None, :])
    ).astype(jnp.int32)
    row_start = jnp.sum(member * starts[None, :], axis=1)
    return starts, row_start, places - row_start


def rotary_tables(positions):
    rot = HS // 4
    half = rot // 2
    inverse = 10000.0 ** (-(jnp.arange(half, dtype=F32) * 2.0) / rot)
    angles = positions.astype(F32)[:, None] * inverse[None, :]
    cosine, sine = jnp.cos(angles), jnp.sin(angles)
    rows = positions.shape[0]
    rest = jnp.zeros((rows, HS - rot), F32)
    none = jnp.zeros((rows, half), F32)
    straight = jnp.concatenate([cosine, cosine, rest + 1.0], axis=1)
    upper = jnp.concatenate([-sine, none, rest], axis=1)
    lower = jnp.concatenate([none, sine, rest], axis=1)
    return [jnp.tile(table, (1, GROUP_HEADS)) for table in (straight, upper, lower)]


def part_kernel(bundles, wide, *outs):
    columns = wide[...]
    for c in range(3):
        merged = [None] * (GW // 128)
        for k, (first, width) in enumerate(windows()):
            source = 2 * HS * k + HS * c + first
            cut = columns[:, source : source + width]
            mask = head_mask(k, first, cut.shape)
            for w in range(width // 128):
                at = first // 128 + w
                lanes = slice(w * 128, w * 128 + 128)
                if merged[at] is None:
                    merged[at] = cut[:, lanes]
                else:
                    merged[at] = jnp.where(mask[:, lanes], cut[:, lanes], merged[at])
        for out, (begin, end) in zip(outs, bundles):
            for at, piece in enumerate(merged):
                first = c * GW + at * 128
                if begin <= first < end:
                    out[:, first - begin : first - begin + 128] = piece


def part_by_part(weight, group, bundles):
    rows = weight.shape[0]
    tile = 128
    return pl.pallas_call(
        functools.partial(part_kernel, bundles),
        out_shape=[jax.ShapeDtypeStruct((rows, end - begin), BF16) for begin, end in bundles],
        grid=(rows // tile,),
        in_specs=[pl.BlockSpec((tile, 3 * GW), lambda i: (i, group))],
        out_specs=[pl.BlockSpec((tile, end - begin), lambda i: (i, 0)) for begin, end in bundles],
        compiler_params=params(),
        cost_estimate=LIGHT,
        name="parts",
    )(weight)


def qkv_kernel(pieces, bundle, order, normed, *refs):
    count = 1 + max(part[0] for piece in pieces for part in piece)
    weights = refs[:count]
    bias, straight, upper, lower = refs[count : count + 4]
    outs = refs[count + 4 : count + 4 + len(bundle)]
    total, held_rows, held_weights, row_sems, weight_sems = refs[count + 4 + len(bundle) :]
    depth = weights[0].shape[0]

    def row_copy(j):
        lanes = pl.ds(pl.multiple_of(order[j] * depth, 128), depth)
        return pltpu.make_async_copy(
            normed.at[:, lanes], held_rows.at[:, pl.ds(j * depth, depth)], row_sems.at[j]
        )

    def weight_copies(j):
        found, at = [], 0
        for n, (source, first, width) in enumerate(pieces[j]):
            found.append(
                pltpu.make_async_copy(
                    weights[source].at[:, pl.ds(first, width)],
                    held_weights.at[pl.ds(j * depth, depth), pl.ds(at, width)],
                    weight_sems.at[j, n],
                )
            )
            at += width
        return found

    for j in range(len(pieces)):
        row_copy(j).start()
        for one in weight_copies(j):
            one.start()
    halves = 2
    each = len(pieces) // halves
    height = total.shape[0] // 2
    for n in range(halves):
        for j in range(n * each, (n + 1) * each):
            row_copy(j).wait()
            for one in weight_copies(j):
                one.wait()
        inner = slice(n * each * depth, (n + 1) * each * depth)
        for m in range(2):
            rows = slice(m * height, (m + 1) * height)
            part = jnp.dot(
                held_rows[rows, inner], held_weights[inner, :], preferred_element_type=F32
            )
            if n == 0:
                total[rows, :] = part
            else:
                total[rows, :] += part

    tile = 64

    def body(i, carry):
        rows = pl.ds(pl.multiple_of(i * tile, tile), tile)
        for spot, c in enumerate(bundle):
            lanes = slice(spot * GW, (spot + 1) * GW)
            x = total[rows, lanes] + bias[:, lanes]
            if c < 2:
                x = (
                    x * straight[rows, :]
                    + pltpu.roll(x, GW - HS // 8, 1) * upper[rows, :]
                    + pltpu.roll(x, HS // 8, 1) * lower[rows, :]
                )
            outs[spot][rows, :] = x.astype(BF16)
        return carry

    lax.fori_loop(0, total.shape[0] // tile, body, 0)


def project(normed, pieces, order, bias, tables, bundle):
    rows, features = normed.shape
    arrays, plan = [], []
    for piece in pieces:
        parts = []
        for array, first, width in piece:
            arrays.append(array)
            parts.append((len(arrays) - 1, first, width))
        plan.append(parts)
    depth = arrays[0].shape[0]
    columns = len(bundle) * GW
    out = jax.ShapeDtypeStruct((rows, GW), BF16)
    vmem = pl.BlockSpec(memory_space=pltpu.VMEM)
    anywhere = pl.BlockSpec(memory_space=pl.ANY)
    return pl.pallas_call(
        functools.partial(qkv_kernel, plan, bundle),
        out_shape=[out] * len(bundle),
        in_specs=[pl.BlockSpec(memory_space=pltpu.SMEM)]
        + [anywhere] * (len(arrays) + 1)
        + [vmem] * 4,
        out_specs=[vmem] * len(bundle),
        scratch_shapes=[
            pltpu.VMEM((rows, columns), F32),
            pltpu.VMEM((rows, features), BF16),
            pltpu.VMEM((features, columns), BF16),
            pltpu.SemaphoreType.DMA((len(plan),)),
            pltpu.SemaphoreType.DMA((len(plan), max(len(parts) for parts in plan))),
        ],
        compiler_params=params(),
        cost_estimate=LIGHT,
        name="project",
    )(order, normed, *arrays, bias, *tables)


def prefix_kernel(blocks, starts, lengths, *refs):
    queries = refs[:blocks]
    keys, values = refs[blocks : blocks + 2]
    outs = refs[blocks + 2 : 2 * blocks + 2]
    totals = refs[2 * blocks + 2]
    slot = pl.program_id(0)
    slots = pl.num_programs(0)
    rows = queries[0].shape[0]

    @pl.when(slot == 0)
    def _():
        totals[...] = jnp.zeros_like(totals)

    begin, size, offset = [], [], []
    count = 0
    for b in range(blocks):
        begin.append(starts[slot * blocks + b])
        size.append(lengths[slot * blocks + b])
        offset.append(count)
        count = count + size[b]

    def tile(base, height):
        down = lax.broadcasted_iota(jnp.int32, (height, 1), 0) + base
        across = lax.broadcasted_iota(jnp.int32, (1, height), 1) + base

        def sources(place, b):
            within = place - offset[b]
            return jnp.where((within >= 0) & (within < size[b]), within + begin[b], -1)

        picked = None
        for b in range(blocks):
            spread = lax.broadcasted_iota(jnp.int32, (height, rows), 1)
            one_hot = jnp.where(spread == sources(down, b), 1.0, 0.0).astype(BF16)
            part = jnp.dot(one_hot, queries[b][...], preferred_element_type=F32)
            picked = part if picked is None else picked + part
        picked = picked.astype(BF16)
        merged = [jnp.zeros((height, 128), F32) for _ in range(GW // 128)]
        extra = jnp.zeros((height, PACK), F32)
        place = lax.broadcasted_iota(jnp.int32, (height, PACK), 1)
        for k, (first, width) in enumerate(windows()):
            lanes = slice(first, first + width)
            mask = head_mask(k, first, (height, width))
            query = jnp.where(mask, picked[:, lanes], jnp.zeros((), BF16))
            scores = lax.dot_general(
                query,
                keys[0, :, lanes],
                (((1,), (1,)), ((), ())),
                preferred_element_type=F32,
            )
            peak = jnp.max(scores, axis=1, keepdims=True)
            weights = jnp.exp2((scores - peak) * (SCALE * LOG2E))
            mass = jnp.sum(weights, axis=1, keepdims=True)
            blended = jnp.dot(
                weights.astype(BF16), values[0, :, lanes], preferred_element_type=F32
            )
            blended = blended * (1.0 / mass)
            for w in range(width // 128):
                at = first // 128 + w
                cut = slice(w * 128, w * 128 + 128)
                merged[at] = jnp.where(mask[:, cut], blended[:, cut], merged[at])
            level = peak * SCALE + jnp.log(mass)
            high = level.astype(BF16).astype(F32)
            middle = (level - high).astype(BF16).astype(F32)
            low = level - high - middle
            for n, term in enumerate((high, middle, low)):
                extra = jnp.where(place == 32 * n + k, term, extra)
        packed = jnp.concatenate(merged + [extra], axis=1).astype(BF16)
        for b in range(blocks):
            spread = lax.broadcasted_iota(jnp.int32, (rows, height), 0)
            one_hot = jnp.where(spread == sources(across, b), 1.0, 0.0).astype(BF16)
            totals[b] += jnp.dot(one_hot, packed, preferred_element_type=F32)

    large = 256
    small = 128
    full = lax.div(count, large)
    rest = count - full * large

    def body(j, carry):
        tile(j * large, large)
        return carry

    lax.fori_loop(0, full + jnp.where(rest > small, 1, 0), body, 0)

    @pl.when((rest > 0) & (rest <= small))
    def _():
        tile(full * large, small)

    @pl.when(slot == slots - 1)
    def _():
        for b in range(blocks):
            outs[b][...] = totals[b].astype(BF16)


def prefix_attention(group, queries, cache, starts, lengths):
    blocks = len(queries)
    rows = queries[0].shape[0]
    slots, length, _ = cache[0].shape
    width = GW + PACK
    whole = lambda s, starts, lengths: (0, 0)
    block = pl.BlockSpec((1, length, GW), lambda s, starts, lengths: (s, 0, group))
    return pl.pallas_call(
        functools.partial(prefix_kernel, blocks),
        out_shape=[jax.ShapeDtypeStruct((rows, width), BF16)] * blocks,
        grid_spec=pltpu.PrefetchScalarGridSpec(
            num_scalar_prefetch=2,
            grid=(slots,),
            in_specs=[pl.BlockSpec((rows, GW), whole)] * blocks + [block] * 2,
            out_specs=[pl.BlockSpec((rows, width), whole)] * blocks,
            scratch_shapes=[pltpu.VMEM((blocks, rows, width), F32)],
        ),
        compiler_params=params(),
        cost_estimate=LIGHT,
        name="prefix",
    )(starts, lengths, *queries, *cache)


def suffix_kernel(row_start, queries, keys, values, out, levels):
    rows = queries.shape[0]
    tile = 128
    for i in range(rows // tile):
        at = slice(i * tile, (i + 1) * tile)
        wide = (i + 1) * tile
        row = lax.broadcasted_iota(jnp.int32, (tile, wide), 0) + i * tile
        column = lax.broadcasted_iota(jnp.int32, (tile, wide), 1)
        allowed = (column <= row) & (column >= row_start[at, :])
        merged = [jnp.zeros((tile, 128), F32) for _ in range(GW // 128)]
        level_row = jnp.zeros((tile, PACK), F32)
        place = lax.broadcasted_iota(jnp.int32, (tile, PACK), 1)
        for k, (first, width) in enumerate(windows()):
            lanes = slice(first, first + width)
            mask = head_mask(k, first, (tile, width))
            query = jnp.where(mask, queries[at, lanes], jnp.zeros((), BF16))
            scores = lax.dot_general(
                query,
                keys[:wide, lanes],
                (((1,), (1,)), ((), ())),
                preferred_element_type=F32,
            )
            scores = jnp.where(allowed, scores, -jnp.inf)
            peak = jnp.max(scores, axis=1, keepdims=True)
            weights = jnp.exp2((scores - peak) * (SCALE * LOG2E))
            mass = jnp.sum(weights, axis=1, keepdims=True)
            blended = jnp.dot(
                weights.astype(BF16), values[:wide, lanes], preferred_element_type=F32
            )
            blended = blended * (1.0 / mass)
            for w in range(width // 128):
                spot = first // 128 + w
                cut = slice(w * 128, w * 128 + 128)
                merged[spot] = jnp.where(mask[:, cut], blended[:, cut], merged[spot])
            level_row = jnp.where(place == k, peak * SCALE + jnp.log(mass), level_row)
        out[at, :] = jnp.concatenate(merged, axis=1)
        levels[at, :] = level_row


def suffix_attention(row_start, queries, keys, values):
    rows = queries.shape[0]
    return pl.pallas_call(
        suffix_kernel,
        out_shape=(
            jax.ShapeDtypeStruct((rows, GW), F32),
            jax.ShapeDtypeStruct((rows, PACK), F32),
        ),
        compiler_params=params(),
        cost_estimate=LIGHT,
        name="suffix",
    )(row_start, queries, keys, values)


def merge_kernel(blocks, *refs):
    parts = refs[:blocks]
    suffix, levels, out = refs[blocks:]
    rows = suffix.shape[0]
    tile = 128
    for i in range(rows // tile):
        at = slice(i * tile, (i + 1) * tile)
        prefix = parts[0][at, :].astype(F32)
        for b in range(1, blocks):
            prefix = prefix + parts[b][at, :].astype(F32)
        terms = prefix[:, GW:]
        pre = terms + pltpu.roll(terms, PACK - 32, 1) + pltpu.roll(terms, PACK - 64, 1)
        suf = levels[at, :]
        top = jnp.maximum(pre, suf)
        pre = jnp.exp(pre - top)
        suf = jnp.exp(suf - top)
        shares = pre / (pre + suf)
        spread = jnp.zeros((tile, GW), F32)
        for k in range(GROUP_HEADS):
            spread = jnp.where(head_mask(k, 0, (tile, GW)), shares[:, k : k + 1], spread)
        out[at, :] = (spread * prefix[:, :GW] + (1.0 - spread) * suffix[at, :]).astype(BF16)


def merge(parts, suffix, levels):
    rows = suffix.shape[0]
    return pl.pallas_call(
        functools.partial(merge_kernel, len(parts)),
        out_shape=jax.ShapeDtypeStruct((rows, GW), BF16),
        compiler_params=params(),
        cost_estimate=LIGHT,
        name="merge",
    )(*parts, suffix, levels)


def output_kernel(groups, lines, place, *refs):
    attention = refs[: 2 * groups]
    own, landed, crossed, out, held, joined, sems = refs[2 * groups :]
    at = pl.program_id(0)
    rows, share = out.shape[1:]
    depth = own.shape[0]
    half = lines // 2
    side, core = place[0], place[1]

    def own_copy(a):
        lanes = pl.ds(pl.multiple_of((2 * a + side) * share, 128), share)
        return pltpu.make_async_copy(
            own.at[:, lanes], held.at[a, pl.ds(0, depth)], sems.at[2 * a]
        )

    def other_copy(a):
        source = landed if a < half else crossed
        spot = lax.rem(a + core * half, lines)
        lanes = pl.ds((a % half) * share, share)
        return pltpu.make_async_copy(
            source.at[:, lanes], held.at[spot, pl.ds(depth, depth)], sems.at[2 * a + 1]
        )

    @pl.when(at == 0)
    def _():
        for a in range(lines):
            own_copy(a).start()
            other_copy(a).start()
        for n in range(2 * groups):
            joined[:, n * GW : (n + 1) * GW] = attention[n][...]

    own_copy(at).wait()
    sent = lax.rem(at + core * half, lines)
    pltpu.make_async_copy(
        landed.at[:, pl.ds(0, share)],
        held.at[at, pl.ds(depth, depth)],
        sems.at[2 * sent + 1],
    ).wait()
    out[0] = jnp.dot(joined[...], held[at], preferred_element_type=F32)


def output_projection(place, attention, own, landed, crossed, lines):
    rows = attention[0].shape[0]
    depth, features = own.shape
    share = features // (2 * lines)
    vmem = pl.BlockSpec((rows, GW), lambda a, place: (0, 0))
    anywhere = pl.BlockSpec(memory_space=pl.ANY)
    return pl.pallas_call(
        functools.partial(output_kernel, len(attention) // 2, lines),
        out_shape=jax.ShapeDtypeStruct((lines, rows, share), F32),
        grid_spec=pltpu.PrefetchScalarGridSpec(
            num_scalar_prefetch=1,
            grid=(lines,),
            in_specs=[vmem] * len(attention) + [anywhere] * 3,
            out_specs=pl.BlockSpec((1, rows, share), lambda a, place: (a, 0, 0)),
            scratch_shapes=[
                pltpu.VMEM((lines, 2 * depth, share), BF16),
                pltpu.VMEM((rows, 2 * depth), BF16),
                pltpu.SemaphoreType.DMA((2 * lines,)),
            ],
        ),
        compiler_params=params(),
        cost_estimate=LIGHT,
        name="output",
    )(place, *attention, own, landed, crossed)


def on_device(
    hidden_states,
    norm_gain,
    norm_bias,
    qkv_weight,
    qkv_bias,
    dense_weight,
    dense_bias,
    prefix_keys,
    prefix_values,
    suffix_len,
    request_order,
    group_slot,
):
    rows, share = hidden_states.shape
    held, prefix_length, local_width = prefix_keys.shape
    groups_local = local_width // GW
    tok_size = lax.axis_size("tok")
    head_size = lax.axis_size("head")
    chips = tok_size // 2
    lines = head_size // 2
    group_count = held * tok_size
    tok = lax.axis_index("tok")
    head = lax.axis_index("head")
    core, chip = tok % 2, tok // 2
    side, line = head % 2, head // 2

    def to_core(x):
        return lax.ppermute(x, "tok", [(t, t ^ 1) for t in range(tok_size)])

    def to_chip(x, shift):
        return lax.ppermute(
            x,
            "tok",
            [(t, (t // 2 + shift) % chips * 2 + t % 2) for t in range(tok_size)],
        )

    def to_side(x):
        return lax.ppermute(x, "head", [(h, h ^ 1) for h in range(head_size)])

    def after(x, *others):
        return lax.optimization_barrier((x, others))[0]

    layout = jnp.stack([suffix_len[0], request_order[0]])
    layouts = [layout] + [to_chip(layout, shift) for shift in range(1, chips)]
    (first,) = part_by_part(qkv_weight, 0, ((0, 3 * GW),))
    first, layouts = lax.optimization_barrier((first, layouts))

    pairs = [[2 * n, 2 * n + 1] for n in range(chips)]
    cache = [
        lax.all_gather(one, "tok", axis=0, tiled=True, axis_index_groups=pairs)
        for one in (prefix_keys, prefix_values)
    ]

    last = lines - 1

    def to_side_from(x, lowest, highest):
        return lax.ppermute(
            x, "head", [(h, h ^ 1) for h in range(head_size) if lowest <= h // 2 <= highest]
        )

    across = to_side(hidden_states)
    blocks = [hidden_states, across]
    places = [head, head ^ 1]
    arriving = [to_chip(first, shift) for shift in range(1, chips)]
    up = down = hidden_states
    settled = across
    for step in range(last):
        if step > 0:
            up, down, settled, first = lax.optimization_barrier((up, down, settled, first))
            blocks[4 * step - 5 if step > 1 else 1] = settled
        up = lax.ppermute(
            up, "head", [(h, h + 2) for h in range(head_size) if step <= h // 2 < last]
        )
        down = lax.ppermute(
            down, "head", [(h, h - 2) for h in range(head_size) if 0 < h // 2 <= last - step]
        )
        settled = across if step == 0 else blocks[4 * step - 1]
        blocks += [up, to_side_from(up, step + 1, last)]
        blocks += [down, to_side_from(down, 0, last - 1 - step)]
        for there, valid in (
            (line - 1 - step, line >= step + 1),
            (line + 1 + step, line + 1 + step <= last),
        ):
            places += [
                jnp.where(valid, 2 * there + side, -1),
                jnp.where(valid, 2 * there + 1 - side, -1),
            ]
    places = jnp.stack(places).astype(jnp.int32)

    columns = 3 * GW
    order = [tok, tok ^ 1]
    for shift in range(1, chips):
        source = (chip + chips - shift) % chips * 2 + core
        order += [source, source ^ 1]
    order = jnp.stack(order).astype(jnp.int32)
    source, _ = lax.optimization_barrier((qkv_weight, layouts))
    cuts = ((0, columns), (0, GW), (GW, 2 * GW), (2 * GW, columns))
    later = [part_by_part(source, g, cuts) for g in range(1, groups_local)]
    lengths = suffix_len[0]
    starts, row_start, within = shard_layout(lengths, request_order[0], rows)
    labels = jnp.arange(group_count, dtype=jnp.int32)
    slot_match = (group_slot[:, None] == labels[None, :]).astype(jnp.int32)

    def served_spans(one):
        firsts = shard_layout(one[0], one[1], rows)[0]
        spans = jnp.stack(
            [
                jnp.sum(firsts[:, None] * slot_match, axis=0),
                jnp.sum(one[0][:, None] * slot_match, axis=0),
            ]
        )
        return lax.dynamic_slice(spans, (0, chip * 2 * held), (2, 2 * held))

    served = jnp.stack([served_spans(one) for one in layouts], axis=2)
    tables = rotary_tables(prefix_length + within)
    bias = qkv_bias.astype(F32).reshape(groups_local, GROUP_HEADS, 3, HS)
    bias = jnp.transpose(bias, (0, 2, 1, 3)).reshape(groups_local, 1, columns)
    bias = [
        [bias[g]] if g == 0 else [bias[g][:, :GW], bias[g][:, GW:]]
        for g in range(groups_local)
    ]

    half = lines // 2
    outgoing = jnp.concatenate(
        [
            lax.dynamic_slice(
                dense_weight,
                (0, (2 * (core * half + a) + 1 - side) * share),
                (dense_weight.shape[0], share),
            )
            for a in range(half)
        ],
        axis=1,
    )
    ready = (
        served[0].reshape(-1),
        served[1].reshape(-1),
        tables,
        bias,
        order,
        row_start[:, None],
        jnp.stack([side, core]).astype(jnp.int32),
        outgoing,
        later,
        places,
        blocks,
    )
    arriving, ready = lax.optimization_barrier((arriving, ready))
    span_start, span_length, tables, bias, order, row_start, place, outgoing, later = ready[:9]
    places, blocks = ready[9:]

    def send(mine):
        return [to_chip(mine, shift) for shift in range(1, chips)]

    def exchange(queries):
        return [queries] + [to_chip(queries, shift) for shift in range(1, chips)]

    def pieces_of(own, arrived, first, width):
        pieces = [[(one, first, width)] for one in own]
        for n in range(chips - 1):
            for which in range(2):
                pieces.append([(part[n][which], 0, part[n][which].shape[1]) for part in arrived])
        return pieces

    def crossing(arrived):
        return [(one, to_core(one)) for one in arrived]

    coming = [send(after(one[1], arriving)) for one in later]
    first_pieces = pieces_of((first, to_core(first)), [crossing(arriving)], 0, columns)
    normed = layer_norm(blocks, places, norm_gain, norm_bias)
    settled = (normed, coming)
    normed = after(normed, coming)
    landed = to_side(after(outgoing, settled))
    own = [(one[0], to_core(after(one[0], arriving))) for one in later]
    keys_coming = [send(after(one[2], settled)) for one in later]
    heads = [project(normed, first_pieces, order, bias[0][0], tables, (0, 1, 2))]
    asked = [exchange(heads[0][0])]
    settled = heads[0]
    for g in range(1, groups_local):
        arrived = crossing(after(coming[g - 1], settled, keys_coming))
        (queries,) = project(
            normed, pieces_of(own[g - 1], [arrived], 0, GW), order, bias[g][0], tables, (0,)
        )
        asked.append(exchange(queries))
        settled = queries
    suffixes = [suffix_attention(after(row_start, settled), *heads[0])]
    values_coming = [send(after(one[3], asked[1][1:])) for one in later]
    asked[0] = after(asked[0], suffixes[0])
    returned = []
    for g in range(groups_local):
        if g > 0:
            asked[g] = after(asked[g], answers)
        answers = prefix_attention(g, asked[g], cache, span_start, span_length)
        returned.append([answers[0]] + [to_chip(answers[s], chips - s) for s in range(1, chips)])
    crossed = to_core(after(landed, returned[0][1:]))
    for g in range(1, groups_local):
        arrived = [
            crossing(keys_coming[g - 1]),
            crossing(after(values_coming[g - 1], answers, returned[0])),
        ]
        keys, values = project(
            normed, pieces_of(own[g - 1], arrived, GW, 2 * GW), order, bias[g][1], tables, (1, 2)
        )
        suffixes.append(suffix_attention(row_start, asked[g][0], keys, values))
    attention_own, attention_side = [], []
    for g in range(groups_local):
        attention = merge(returned[g], *suffixes[g])
        attention_own.append(attention)
        attention_side.append(to_side(attention))
    partial = output_projection(
        place, attention_own + attention_side, dense_weight, landed, crossed, lines
    )

    cuts = 2
    height = rows // cuts

    def chunk(place, cut):
        place = jnp.clip(place, 0, last)
        return lax.dynamic_slice(
            partial, (place, cut * height, 0), (1, height, share)
        ).reshape(height, share)

    passing = [None] * cuts
    for step in range(last):
        up_pairs = [(h, h + 2) for h in range(head_size) if h // 2 <= step and h // 2 < last]
        down_pairs = [(h, h - 2) for h in range(head_size) if last - h // 2 <= step and h // 2 > 0]
        for cut in range(cuts):
            up = chunk(last + line - step, cut)
            down = chunk(line - last + step, cut)
            if passing[cut] is not None:
                if cut > 0:
                    passing[cut], sent = lax.optimization_barrier((passing[cut], sent))
                up = up + passing[cut][0].astype(F32)
                down = down + passing[cut][1].astype(F32)
            up, down = lax.optimization_barrier((up.astype(BF16), down.astype(BF16)))
            sent = up
            passing[cut] = lax.optimization_barrier(
                (lax.ppermute(up, "head", up_pairs), lax.ppermute(down, "head", down_pairs))
            )
    base = hidden_states.astype(F32) + dense_bias.astype(F32)
    done = [
        base[cut * height : (cut + 1) * height]
        + (chunk(line, cut) + passing[cut][0].astype(F32) + passing[cut][1].astype(F32))
        for cut in range(cuts)
    ]
    return jnp.concatenate(done, axis=0).astype(BF16)


def solution(mesh):
    placed = (
        P("tok", "head"),
        P(),
        P(),
        P("tok", "head"),
        P("head"),
        P("head", None),
        P("head"),
        P("tok", None, "head"),
        P("tok", None, "head"),
        P("tok", None),
        P("tok", None),
        P(),
    )
    return jax.shard_map(
        on_device, mesh=mesh, in_specs=placed, out_specs=P("tok", "head"), check_vma=False
    )
```

```python
import functools
import math

import jax
import jax.numpy as jnp
from jax import lax
from jax.experimental import pallas as pl
from jax.experimental.pallas import tpu as pltpu
from jax.sharding import PartitionSpec as P

HS = 96
GROUP_HEADS = 4
GW = GROUP_HEADS * HS
PACK = 128
F32 = jnp.float32
BF16 = jnp.bfloat16
VMEM_LIMIT = 56 * 1024 * 1024
SCALE = 1.0 / math.sqrt(HS)
LOG2E = math.log2(math.e)
LIGHT = pl.CostEstimate(flops=1000, bytes_accessed=1000, transcendentals=0)


def windows():
    found = []
    for k in range(GROUP_HEADS):
        first = k * HS // 128 * 128
        last = -(-(k * HS + HS) // 128) * 128
        found.append((first, last - first))
    return found


def head_mask(k, first, shape):
    lane = lax.broadcasted_iota(jnp.int32, shape, 1) + first
    return (lane >= k * HS) & (lane < (k + 1) * HS)


def params():
    return pltpu.CompilerParams(vmem_limit_bytes=VMEM_LIMIT)


def norm_kernel(values, gain, shift, out):
    widened = values[...].astype(F32)
    center = jnp.mean(widened, axis=-1, keepdims=True)
    moved = widened - center
    spread = jnp.mean(jnp.square(moved), axis=-1, keepdims=True)
    out[...] = (moved * lax.rsqrt(spread + 1e-05) * gain[...] + shift[...]).astype(BF16)


def layer_norm(values, gain, shift):
    rows, features = values.shape
    tile = 64
    return pl.pallas_call(
        norm_kernel,
        out_shape=jax.ShapeDtypeStruct((rows, features), BF16),
        grid=(rows // tile,),
        in_specs=[
            pl.BlockSpec((tile, features), lambda i: (i, 0)),
            pl.BlockSpec((1, features), lambda i: (0, 0)),
            pl.BlockSpec((1, features), lambda i: (0, 0)),
        ],
        out_specs=pl.BlockSpec((tile, features), lambda i: (i, 0)),
        compiler_params=params(),
        cost_estimate=LIGHT,
        name="norm",
    )(values, gain[None, :], shift[None, :])


def shard_layout(lengths, ordering, row_count):
    group_count = lengths.shape[0]
    labels = jnp.arange(group_count, dtype=jnp.int32)
    chosen = (ordering[:, None] == labels[None, :]).astype(jnp.int32)
    ranking = jnp.sum(labels[:, None] * chosen, axis=0)
    earlier = (ranking[None, :] < ranking[:, None]).astype(jnp.int32)
    starts = jnp.sum(earlier * lengths[None, :], axis=1)
    places = jnp.arange(row_count, dtype=jnp.int32)
    member = (
        (places[:, None] >= starts[None, :]) & (places[:, None] < (starts + lengths)[None, :])
    ).astype(jnp.int32)
    row_start = jnp.sum(member * starts[None, :], axis=1)
    return starts, row_start, places - row_start


def rotary_tables(positions):
    rot = HS // 4
    half = rot // 2
    inverse = 10000.0 ** (-(jnp.arange(half, dtype=F32) * 2.0) / rot)
    lanes = jnp.concatenate([inverse, inverse, jnp.zeros((HS - rot,), F32)])
    lanes = jnp.tile(lanes, GROUP_HEADS)
    angles = positions.astype(F32)[:, None] * lanes[None, :]
    return [jnp.cos(angles), jnp.sin(angles)]


def part_kernel(bundles, wide, *outs):
    columns = wide[...]
    for c in range(3):
        merged = [None] * (GW // 128)
        for k, (first, width) in enumerate(windows()):
            source = 2 * HS * k + HS * c + first
            cut = columns[:, source : source + width]
            mask = head_mask(k, first, cut.shape)
            for w in range(width // 128):
                at = first // 128 + w
                lanes = slice(w * 128, w * 128 + 128)
                if merged[at] is None:
                    merged[at] = cut[:, lanes]
                else:
                    merged[at] = jnp.where(mask[:, lanes], cut[:, lanes], merged[at])
        for out, (begin, end) in zip(outs, bundles):
            for at, piece in enumerate(merged):
                first = c * GW + at * 128
                if begin <= first < end:
                    out[:, first - begin : first - begin + 128] = piece


def part_by_part(weight, group, bundles):
    rows = weight.shape[0]
    tile = 128
    return pl.pallas_call(
        functools.partial(part_kernel, bundles),
        out_shape=[jax.ShapeDtypeStruct((rows, end - begin), BF16) for begin, end in bundles],
        grid=(rows // tile,),
        in_specs=[pl.BlockSpec((tile, 3 * GW), lambda i: (i, group))],
        out_specs=[pl.BlockSpec((tile, end - begin), lambda i: (i, 0)) for begin, end in bundles],
        compiler_params=params(),
        cost_estimate=LIGHT,
        name="parts",
    )(weight)


def qkv_kernel(pieces, bundle, order, normed, *refs):
    count = 1 + max(part[0] for piece in pieces for part in piece)
    weights = refs[:count]
    bias, cosine, sine = refs[count : count + 3]
    outs = refs[count + 3 : count + 3 + len(bundle)]
    total, held_rows, held_weights, row_sems, weight_sems = refs[count + 3 + len(bundle) :]
    depth = weights[0].shape[0]

    def row_copy(j):
        lanes = pl.ds(pl.multiple_of(order[j] * depth, 128), depth)
        return pltpu.make_async_copy(
            normed.at[:, lanes], held_rows.at[:, pl.ds(j * depth, depth)], row_sems.at[j]
        )

    def weight_copies(j):
        found, at = [], 0
        for n, (source, first, width) in enumerate(pieces[j]):
            found.append(
                pltpu.make_async_copy(
                    weights[source].at[:, pl.ds(first, width)],
                    held_weights.at[pl.ds(j * depth, depth), pl.ds(at, width)],
                    weight_sems.at[j, n],
                )
            )
            at += width
        return found

    for j in range(len(pieces)):
        row_copy(j).start()
        for one in weight_copies(j):
            one.start()
    halves = 2
    each = len(pieces) // halves
    height = total.shape[0] // 2
    for n in range(halves):
        for j in range(n * each, (n + 1) * each):
            row_copy(j).wait()
            for one in weight_copies(j):
                one.wait()
        inner = slice(n * each * depth, (n + 1) * each * depth)
        for m in range(2):
            rows = slice(m * height, (m + 1) * height)
            part = jnp.dot(
                held_rows[rows, inner], held_weights[inner, :], preferred_element_type=F32
            )
            if n == 0:
                total[rows, :] = part
            else:
                total[rows, :] += part

    tile = 64

    def body(i, carry):
        rows = pl.ds(pl.multiple_of(i * tile, tile), tile)
        for spot, c in enumerate(bundle):
            lanes = slice(spot * GW, (spot + 1) * GW)
            x = total[rows, lanes] + bias[:, lanes]
            if c < 2:
                lane = lax.broadcasted_iota(jnp.int32, x.shape, 1) % HS
                turned = jnp.where(
                    lane < HS // 8,
                    -pltpu.roll(x, GW - HS // 8, 1),
                    pltpu.roll(x, HS // 8, 1),
                )
                x = x * cosine[rows, :] + turned * sine[rows, :]
            outs[spot][rows, :] = x.astype(BF16)
        return carry

    lax.fori_loop(0, total.shape[0] // tile, body, 0)


def project(normed, pieces, order, bias, tables, bundle):
    rows, features = normed.shape
    arrays, plan = [], []
    for piece in pieces:
        parts = []
        for array, first, width in piece:
            arrays.append(array)
            parts.append((len(arrays) - 1, first, width))
        plan.append(parts)
    depth = arrays[0].shape[0]
    columns = len(bundle) * GW
    out = jax.ShapeDtypeStruct((rows, GW), BF16)
    vmem = pl.BlockSpec(memory_space=pltpu.VMEM)
    anywhere = pl.BlockSpec(memory_space=pl.ANY)
    return pl.pallas_call(
        functools.partial(qkv_kernel, plan, bundle),
        out_shape=[out] * len(bundle),
        in_specs=[pl.BlockSpec(memory_space=pltpu.SMEM)]
        + [anywhere] * (len(arrays) + 1)
        + [vmem] * 3,
        out_specs=[vmem] * len(bundle),
        scratch_shapes=[
            pltpu.VMEM((rows, columns), F32),
            pltpu.VMEM((rows, features), BF16),
            pltpu.VMEM((features, columns), BF16),
            pltpu.SemaphoreType.DMA((len(plan),)),
            pltpu.SemaphoreType.DMA((len(plan), max(len(parts) for parts in plan))),
        ],
        compiler_params=params(),
        cost_estimate=LIGHT,
        name="project",
    )(order, normed, *arrays, bias, *tables)


def prefix_kernel(blocks, starts, lengths, *refs):
    queries = refs[:blocks]
    keys, values = refs[blocks : blocks + 2]
    outs = refs[blocks + 2 : 2 * blocks + 2]
    totals = refs[2 * blocks + 2]
    slot = pl.program_id(0)
    slots = pl.num_programs(0)
    rows = queries[0].shape[0]

    @pl.when(slot == 0)
    def _():
        totals[...] = jnp.zeros_like(totals)

    begin, size, offset = [], [], []
    count = 0
    for b in range(blocks):
        begin.append(starts[slot * blocks + b])
        size.append(lengths[slot * blocks + b])
        offset.append(count)
        count = count + size[b]

    def tile(base, height):
        down = lax.broadcasted_iota(jnp.int32, (height, 1), 0) + base
        across = lax.broadcasted_iota(jnp.int32, (1, height), 1) + base

        def sources(place, b):
            within = place - offset[b]
            return jnp.where((within >= 0) & (within < size[b]), within + begin[b], -1)

        picked = None
        for b in range(blocks):
            spread = lax.broadcasted_iota(jnp.int32, (height, rows), 1)
            one_hot = jnp.where(spread == sources(down, b), 1.0, 0.0).astype(BF16)
            part = jnp.dot(one_hot, queries[b][...], preferred_element_type=F32)
            picked = part if picked is None else picked + part
        picked = picked.astype(BF16)
        merged = [jnp.zeros((height, 128), F32) for _ in range(GW // 128)]
        extra = jnp.zeros((height, PACK), F32)
        place = lax.broadcasted_iota(jnp.int32, (height, PACK), 1)
        for k, (first, width) in enumerate(windows()):
            lanes = slice(first, first + width)
            mask = head_mask(k, first, (height, width))
            query = jnp.where(mask, picked[:, lanes], jnp.zeros((), BF16))
            scores = lax.dot_general(
                query,
                keys[0, :, lanes],
                (((1,), (1,)), ((), ())),
                preferred_element_type=F32,
            )
            peak = jnp.max(scores, axis=1, keepdims=True)
            weights = jnp.exp2((scores - peak) * (SCALE * LOG2E))
            mass = jnp.sum(weights, axis=1, keepdims=True)
            blended = jnp.dot(
                weights.astype(BF16), values[0, :, lanes], preferred_element_type=F32
            )
            blended = blended * (1.0 / mass)
            for w in range(width // 128):
                at = first // 128 + w
                cut = slice(w * 128, w * 128 + 128)
                merged[at] = jnp.where(mask[:, cut], blended[:, cut], merged[at])
            level = peak * SCALE + jnp.log(mass)
            high = level.astype(BF16).astype(F32)
            middle = (level - high).astype(BF16).astype(F32)
            low = level - high - middle
            for n, term in enumerate((high, middle, low)):
                extra = jnp.where(place == 32 * n + k, term, extra)
        packed = jnp.concatenate(merged + [extra], axis=1).astype(BF16)
        for b in range(blocks):
            spread = lax.broadcasted_iota(jnp.int32, (rows, height), 0)
            one_hot = jnp.where(spread == sources(across, b), 1.0, 0.0).astype(BF16)
            totals[b] += jnp.dot(one_hot, packed, preferred_element_type=F32)

    large = 256
    small = 128
    full = lax.div(count, large)
    rest = count - full * large

    def body(j, carry):
        tile(j * large, large)
        return carry

    lax.fori_loop(0, full + jnp.where(rest > small, 1, 0), body, 0)

    @pl.when((rest > 0) & (rest <= small))
    def _():
        tile(full * large, small)

    @pl.when(slot == slots - 1)
    def _():
        for b in range(blocks):
            outs[b][...] = totals[b].astype(BF16)


def prefix_attention(group, queries, cache, starts, lengths):
    blocks = len(queries)
    rows = queries[0].shape[0]
    slots, length, _ = cache[0].shape
    width = GW + PACK
    whole = lambda s, starts, lengths: (0, 0)
    block = pl.BlockSpec((1, length, GW), lambda s, starts, lengths: (s, 0, group))
    return pl.pallas_call(
        functools.partial(prefix_kernel, blocks),
        out_shape=[jax.ShapeDtypeStruct((rows, width), BF16)] * blocks,
        grid_spec=pltpu.PrefetchScalarGridSpec(
            num_scalar_prefetch=2,
            grid=(slots,),
            in_specs=[pl.BlockSpec((rows, GW), whole)] * blocks + [block] * 2,
            out_specs=[pl.BlockSpec((rows, width), whole)] * blocks,
            scratch_shapes=[pltpu.VMEM((blocks, rows, width), F32)],
        ),
        compiler_params=params(),
        cost_estimate=LIGHT,
        name="prefix",
    )(starts, lengths, *queries, *cache)


def suffix_kernel(row_start, queries, keys, values, out, levels):
    rows = queries.shape[0]
    tile = 128
    for i in range(rows // tile):
        at = slice(i * tile, (i + 1) * tile)
        wide = (i + 1) * tile
        row = lax.broadcasted_iota(jnp.int32, (tile, wide), 0) + i * tile
        column = lax.broadcasted_iota(jnp.int32, (tile, wide), 1)
        allowed = (column <= row) & (column >= row_start[at, :])
        merged = [jnp.zeros((tile, 128), F32) for _ in range(GW // 128)]
        level_row = jnp.zeros((tile, PACK), F32)
        place = lax.broadcasted_iota(jnp.int32, (tile, PACK), 1)
        for k, (first, width) in enumerate(windows()):
            lanes = slice(first, first + width)
            mask = head_mask(k, first, (tile, width))
            query = jnp.where(mask, queries[at, lanes], jnp.zeros((), BF16))
            scores = lax.dot_general(
                query,
                keys[:wide, lanes],
                (((1,), (1,)), ((), ())),
                preferred_element_type=F32,
            )
            scores = jnp.where(allowed, scores, -jnp.inf)
            peak = jnp.max(scores, axis=1, keepdims=True)
            weights = jnp.exp2((scores - peak) * (SCALE * LOG2E))
            mass = jnp.sum(weights, axis=1, keepdims=True)
            blended = jnp.dot(
                weights.astype(BF16), values[:wide, lanes], preferred_element_type=F32
            )
            blended = blended * (1.0 / mass)
            for w in range(width // 128):
                spot = first // 128 + w
                cut = slice(w * 128, w * 128 + 128)
                merged[spot] = jnp.where(mask[:, cut], blended[:, cut], merged[spot])
            level_row = jnp.where(place == k, peak * SCALE + jnp.log(mass), level_row)
        out[at, :] = jnp.concatenate(merged, axis=1)
        levels[at, :] = level_row


def suffix_attention(row_start, queries, keys, values):
    rows = queries.shape[0]
    return pl.pallas_call(
        suffix_kernel,
        out_shape=(
            jax.ShapeDtypeStruct((rows, GW), F32),
            jax.ShapeDtypeStruct((rows, PACK), F32),
        ),
        compiler_params=params(),
        cost_estimate=LIGHT,
        name="suffix",
    )(row_start, queries, keys, values)


def merge_kernel(blocks, *refs):
    parts = refs[:blocks]
    suffix, levels, out = refs[blocks:]
    rows = suffix.shape[0]
    tile = 128
    for i in range(rows // tile):
        at = slice(i * tile, (i + 1) * tile)
        prefix = parts[0][at, :].astype(F32)
        for b in range(1, blocks):
            prefix = prefix + parts[b][at, :].astype(F32)
        terms = prefix[:, GW:]
        pre = terms + pltpu.roll(terms, PACK - 32, 1) + pltpu.roll(terms, PACK - 64, 1)
        suf = levels[at, :]
        top = jnp.maximum(pre, suf)
        pre = jnp.exp(pre - top)
        suf = jnp.exp(suf - top)
        shares = pre / (pre + suf)
        spread = jnp.zeros((tile, GW), F32)
        for k in range(GROUP_HEADS):
            spread = jnp.where(head_mask(k, 0, (tile, GW)), shares[:, k : k + 1], spread)
        out[at, :] = (spread * prefix[:, :GW] + (1.0 - spread) * suffix[at, :]).astype(BF16)


def merge(parts, suffix, levels):
    rows = suffix.shape[0]
    return pl.pallas_call(
        functools.partial(merge_kernel, len(parts)),
        out_shape=jax.ShapeDtypeStruct((rows, GW), BF16),
        compiler_params=params(),
        cost_estimate=LIGHT,
        name="merge",
    )(*parts, suffix, levels)


def output_kernel(groups, lines, place, *refs):
    attention = refs[: 2 * groups]
    own, landed, crossed, out, held, joined, sems = refs[2 * groups :]
    at = pl.program_id(0)
    rows, share = out.shape[1:]
    depth = own.shape[0]
    half = lines // 2
    side, core = place[0], place[1]

    def own_copy(a):
        lanes = pl.ds(pl.multiple_of((2 * a + side) * share, 128), share)
        return pltpu.make_async_copy(
            own.at[:, lanes], held.at[a, pl.ds(0, depth)], sems.at[2 * a]
        )

    def other_copy(a):
        source = landed if a < half else crossed
        spot = lax.rem(a + core * half, lines)
        lanes = pl.ds((a % half) * share, share)
        return pltpu.make_async_copy(
            source.at[:, lanes], held.at[spot, pl.ds(depth, depth)], sems.at[2 * a + 1]
        )

    @pl.when(at == 0)
    def _():
        for a in range(lines):
            own_copy(a).start()
            other_copy(a).start()
        for n in range(2 * groups):
            joined[:, n * GW : (n + 1) * GW] = attention[n][...]

    own_copy(at).wait()
    sent = lax.rem(at + core * half, lines)
    pltpu.make_async_copy(
        landed.at[:, pl.ds(0, share)],
        held.at[at, pl.ds(depth, depth)],
        sems.at[2 * sent + 1],
    ).wait()
    out[0] = jnp.dot(joined[...], held[at], preferred_element_type=F32)


def output_projection(place, attention, own, landed, crossed, lines):
    rows = attention[0].shape[0]
    depth, features = own.shape
    share = features // (2 * lines)
    vmem = pl.BlockSpec((rows, GW), lambda a, place: (0, 0))
    anywhere = pl.BlockSpec(memory_space=pl.ANY)
    return pl.pallas_call(
        functools.partial(output_kernel, len(attention) // 2, lines),
        out_shape=jax.ShapeDtypeStruct((lines, rows, share), F32),
        grid_spec=pltpu.PrefetchScalarGridSpec(
            num_scalar_prefetch=1,
            grid=(lines,),
            in_specs=[vmem] * len(attention) + [anywhere] * 3,
            out_specs=pl.BlockSpec((1, rows, share), lambda a, place: (a, 0, 0)),
            scratch_shapes=[
                pltpu.VMEM((lines, 2 * depth, share), BF16),
                pltpu.VMEM((rows, 2 * depth), BF16),
                pltpu.SemaphoreType.DMA((2 * lines,)),
            ],
        ),
        compiler_params=params(),
        cost_estimate=LIGHT,
        name="output",
    )(place, *attention, own, landed, crossed)


def on_device(
    hidden_states,
    norm_gain,
    norm_bias,
    qkv_weight,
    qkv_bias,
    dense_weight,
    dense_bias,
    prefix_keys,
    prefix_values,
    suffix_len,
    request_order,
    group_slot,
):
    rows, share = hidden_states.shape
    held, prefix_length, local_width = prefix_keys.shape
    groups_local = local_width // GW
    tok_size = lax.axis_size("tok")
    head_size = lax.axis_size("head")
    chips = tok_size // 2
    lines = head_size // 2
    group_count = held * tok_size
    tok = lax.axis_index("tok")
    head = lax.axis_index("head")
    core, chip = tok % 2, tok // 2
    side, line = head % 2, head // 2

    def to_core(x):
        return lax.ppermute(x, "tok", [(t, t ^ 1) for t in range(tok_size)])

    def to_chip(x, shift):
        return lax.ppermute(
            x,
            "tok",
            [(t, (t // 2 + shift) % chips * 2 + t % 2) for t in range(tok_size)],
        )

    def to_side(x):
        return lax.ppermute(x, "head", [(h, h ^ 1) for h in range(head_size)])

    def after(x, *others):
        return lax.optimization_barrier((x, others))[0]

    layout = jnp.stack([suffix_len[0], request_order[0]])
    layouts = [layout] + [to_chip(layout, shift) for shift in range(1, chips)]
    (first,) = part_by_part(qkv_weight, 0, ((0, 3 * GW),))
    first, layouts = lax.optimization_barrier((first, layouts))

    full_rows = lax.all_gather(hidden_states, "head", axis=1, tiled=True)
    pairs = [[2 * n, 2 * n + 1] for n in range(chips)]
    cache = [
        lax.all_gather(after(one, layouts), "tok", axis=0, tiled=True, axis_index_groups=pairs)
        for one in (prefix_keys, prefix_values)
    ]
    arriving = [to_chip(first, shift) for shift in range(1, chips)]

    columns = 3 * GW
    order = [tok, tok ^ 1]
    for shift in range(1, chips):
        source = (chip + chips - shift) % chips * 2 + core
        order += [source, source ^ 1]
    order = jnp.stack(order).astype(jnp.int32)
    source, _ = lax.optimization_barrier((qkv_weight, layouts))
    cuts = ((0, columns), (0, 2 * GW), (2 * GW, columns))
    later = [part_by_part(source, g, cuts) for g in range(1, groups_local)]
    lengths = suffix_len[0]
    starts, row_start, within = shard_layout(lengths, request_order[0], rows)
    labels = jnp.arange(group_count, dtype=jnp.int32)
    slot_match = (group_slot[:, None] == labels[None, :]).astype(jnp.int32)

    def served_spans(one):
        firsts = shard_layout(one[0], one[1], rows)[0]
        spans = jnp.stack(
            [
                jnp.sum(firsts[:, None] * slot_match, axis=0),
                jnp.sum(one[0][:, None] * slot_match, axis=0),
            ]
        )
        return lax.dynamic_slice(spans, (0, chip * 2 * held), (2, 2 * held))

    served = jnp.stack([served_spans(one) for one in layouts], axis=2)
    tables = rotary_tables(prefix_length + within)
    bias = qkv_bias.astype(F32).reshape(groups_local, GROUP_HEADS, 3, HS)
    bias = jnp.transpose(bias, (0, 2, 1, 3)).reshape(groups_local, 1, columns)
    bias = [
        [bias[g]] if g == 0 else [bias[g][:, : 2 * GW], bias[g][:, 2 * GW :]]
        for g in range(groups_local)
    ]

    half = lines // 2
    outgoing = jnp.concatenate(
        [
            lax.dynamic_slice(
                dense_weight,
                (0, (2 * (core * half + a) + 1 - side) * share),
                (dense_weight.shape[0], share),
            )
            for a in range(half)
        ],
        axis=1,
    )
    ready = (
        served[0].reshape(-1),
        served[1].reshape(-1),
        tables,
        bias,
        order,
        row_start[:, None],
        jnp.stack([side, core]).astype(jnp.int32),
        outgoing,
        later,
    )
    arriving, ready = lax.optimization_barrier((arriving, ready))
    span_start, span_length, tables, bias, order, row_start, place, outgoing, later = ready

    def send(mine):
        return [to_chip(mine, shift) for shift in range(1, chips)]

    def exchange(queries):
        return [queries] + [to_chip(queries, shift) for shift in range(1, chips)]

    def pieces_of(own, arrived, first, width):
        pieces = [[(one, first, width)] for one in own]
        for n in range(chips - 1):
            for which in range(2):
                pieces.append([(part[n][which], 0, part[n][which].shape[1]) for part in arrived])
        return pieces

    def crossing(arrived):
        return [(one, to_core(one)) for one in arrived]

    coming = [send(after(one[1], arriving)) for one in later]
    first_pieces = pieces_of((first, to_core(first)), [crossing(arriving)], 0, columns)
    normed = layer_norm(full_rows, norm_gain, norm_bias)
    landed = to_side(after(outgoing, full_rows))
    own = [(one[0], to_core(after(one[0], arriving))) for one in later]
    heads = [project(normed, first_pieces, order, bias[0][0], tables, (0, 1, 2))]
    asked = [exchange(heads[0][0])]
    suffixes = [suffix_attention(row_start, *heads[0])]
    settled = suffixes[0]
    for g in range(1, groups_local):
        arrived = crossing(after(coming[g - 1], settled))
        pair = project(
            normed, pieces_of(own[g - 1], [arrived], 0, 2 * GW), order, bias[g][0], tables, (0, 1)
        )
        heads.append(pair)
        asked.append(exchange(pair[0]))
        settled = pair
    values_coming = [send(after(one[2], asked[0][1:])) for one in later]
    asked[0] = after(asked[0], settled)
    returned = []
    for g in range(groups_local):
        if g > 0:
            asked[g] = after(asked[g], answers)
        answers = prefix_attention(g, asked[g], cache, span_start, span_length)
        returned.append([answers[0]] + [to_chip(answers[s], chips - s) for s in range(1, chips)])
    crossed = to_core(after(landed, answers))
    for g in range(1, groups_local):
        arrived = crossing(after(values_coming[g - 1], answers))
        (values,) = project(
            normed, pieces_of(own[g - 1], [arrived], 2 * GW, GW), order, bias[g][1], tables, (2,)
        )
        suffixes.append(suffix_attention(row_start, heads[g][0], heads[g][1], values))
    attention_own, attention_side = [], []
    for g in range(groups_local):
        attention = merge(returned[g], *suffixes[g])
        attention_own.append(attention)
        attention_side.append(to_side(attention))
    partial = output_projection(
        place, attention_own + attention_side, dense_weight, landed, crossed, lines
    )

    last = lines - 1
    cuts = 2
    height = rows // cuts

    def chunk(place, cut):
        place = jnp.clip(place, 0, last)
        return lax.dynamic_slice(
            partial, (place, cut * height, 0), (1, height, share)
        ).reshape(height, share)

    passing = [None] * cuts
    for step in range(last):
        up_pairs = [(h, h + 2) for h in range(head_size) if h // 2 <= step and h // 2 < last]
        down_pairs = [(h, h - 2) for h in range(head_size) if last - h // 2 <= step and h // 2 > 0]
        for cut in range(cuts):
            up = chunk(last + line - step, cut)
            down = chunk(line - last + step, cut)
            if passing[cut] is not None:
                if cut > 0:
                    passing[cut], sent = lax.optimization_barrier((passing[cut], sent))
                up = up + passing[cut][0].astype(F32)
                down = down + passing[cut][1].astype(F32)
            up, down = lax.optimization_barrier((up.astype(BF16), down.astype(BF16)))
            sent = up
            passing[cut] = lax.optimization_barrier(
                (lax.ppermute(up, "head", up_pairs), lax.ppermute(down, "head", down_pairs))
            )
    base = hidden_states.astype(F32) + dense_bias.astype(F32)
    done = [
        base[cut * height : (cut + 1) * height]
        + (chunk(line, cut) + passing[cut][0].astype(F32) + passing[cut][1].astype(F32))
        for cut in range(cuts)
    ]
    return jnp.concatenate(done, axis=0).astype(BF16)


def solution(mesh):
    placed = (
        P("tok", "head"),
        P(),
        P(),
        P("tok", "head"),
        P("head"),
        P("head", None),
        P("head"),
        P("tok", None, "head"),
        P("tok", None, "head"),
        P("tok", None),
        P("tok", None),
        P(),
    )
    return jax.shard_map(
        on_device, mesh=mesh, in_specs=placed, out_specs=P("tok", "head"), check_vma=False
    )
```

```python
import functools
import math

import jax
import jax.numpy as jnp
from jax import lax
from jax.experimental import pallas as pl
from jax.experimental.pallas import tpu as pltpu
from jax.sharding import PartitionSpec as P

HS = 96
GROUP_HEADS = 4
GW = GROUP_HEADS * HS
PACK = 128
F32 = jnp.float32
BF16 = jnp.bfloat16
VMEM_LIMIT = 56 * 1024 * 1024
SCALE = 1.0 / math.sqrt(HS)
LOG2E = math.log2(math.e)
LIGHT = pl.CostEstimate(flops=1000, bytes_accessed=1000, transcendentals=0)


def windows():
    found = []
    for k in range(GROUP_HEADS):
        first = k * HS // 128 * 128
        last = -(-(k * HS + HS) // 128) * 128
        found.append((first, last - first))
    return found


def head_mask(k, first, shape):
    lane = lax.broadcasted_iota(jnp.int32, shape, 1) + first
    return (lane >= k * HS) & (lane < (k + 1) * HS)


def params():
    return pltpu.CompilerParams(vmem_limit_bytes=VMEM_LIMIT)


def norm_kernel(count, chunks, places, *refs):
    blocks = refs[:count]
    gain, shift, out, held, ready, sems, out_sems = refs[count:]
    share = blocks[0].shape[1]
    height = held.shape[0] // chunks
    tile = 32

    def copy(j, chunk):
        lanes = pl.ds(pl.multiple_of(places[j] * share, 128), share)
        rows = pl.ds(chunk * height, height)
        return pltpu.make_async_copy(
            blocks[j].at[rows, :], held.at[rows, lanes], sems.at[j, chunk]
        )

    def out_copy(chunk):
        rows = pl.ds(chunk * height, height)
        return pltpu.make_async_copy(ready.at[rows, :], out.at[rows, :], out_sems.at[chunk])

    for chunk in range(chunks):
        for j in range(count):

            @pl.when(places[j] >= 0)
            def _(j=j, chunk=chunk):
                copy(j, chunk).start()

    for chunk in range(chunks):
        for j in range(count):

            @pl.when(places[j] >= 0)
            def _(j=j, chunk=chunk):
                copy(j, chunk).wait()

        def body(i, carry, chunk=chunk):
            rows = pl.ds(pl.multiple_of(chunk * height + i * tile, tile), tile)
            widened = held[rows, :].astype(F32)
            center = jnp.mean(widened, axis=-1, keepdims=True)
            moved = widened - center
            spread = jnp.mean(jnp.square(moved), axis=-1, keepdims=True)
            scaled = moved * lax.rsqrt(spread + 1e-05) * gain[...] + shift[...]
            ready[rows, :] = scaled.astype(BF16)
            return carry

        lax.fori_loop(0, height // tile, body, 0)
        out_copy(chunk).start()
    for chunk in range(chunks):
        out_copy(chunk).wait()


def layer_norm(blocks, places, gain, shift):
    rows = blocks[0].shape[0]
    features = gain.shape[0]
    count = len(blocks)
    chunks = 4
    vmem = pl.BlockSpec(memory_space=pltpu.VMEM)
    return pl.pallas_call(
        functools.partial(norm_kernel, count, chunks),
        out_shape=jax.ShapeDtypeStruct((rows, features), BF16),
        in_specs=[pl.BlockSpec(memory_space=pltpu.SMEM)]
        + [pl.BlockSpec(memory_space=pl.ANY)] * count
        + [vmem] * 2,
        out_specs=pl.BlockSpec(memory_space=pl.ANY),
        scratch_shapes=[
            pltpu.VMEM((rows, features), BF16),
            pltpu.VMEM((rows, features), BF16),
            pltpu.SemaphoreType.DMA((count, chunks)),
            pltpu.SemaphoreType.DMA((chunks,)),
        ],
        compiler_params=params(),
        cost_estimate=LIGHT,
        name="norm",
    )(places, *blocks, gain[None, :], shift[None, :])


def shard_layout(lengths, ordering, row_count):
    group_count = lengths.shape[0]
    labels = jnp.arange(group_count, dtype=jnp.int32)
    chosen = (ordering[:, None] == labels[None, :]).astype(jnp.int32)
    ranking = jnp.sum(labels[:, None] * chosen, axis=0)
    earlier = (ranking[None, :] < ranking[:, None]).astype(jnp.int32)
    starts = jnp.sum(earlier * lengths[None, :], axis=1)
    places = jnp.arange(row_count, dtype=jnp.int32)
    member = (
        (places[:, None] >= starts[None, :]) & (places[:, None] < (starts + lengths)[None, :])
    ).astype(jnp.int32)
    row_start = jnp.sum(member * starts[None, :], axis=1)
    return starts, row_start, places - row_start


def rotary_tables(positions):
    rot = HS // 4
    half = rot // 2
    inverse = 10000.0 ** (-(jnp.arange(half, dtype=F32) * 2.0) / rot)
    lanes = jnp.concatenate([inverse, inverse, jnp.zeros((HS - rot,), F32)])
    lanes = jnp.tile(lanes, GROUP_HEADS)
    angles = positions.astype(F32)[:, None] * lanes[None, :]
    return [jnp.cos(angles), jnp.sin(angles)]


def part_kernel(bundles, wide, *outs):
    columns = wide[...]
    for c in range(3):
        merged = [None] * (GW // 128)
        for k, (first, width) in enumerate(windows()):
            source = 2 * HS * k + HS * c + first
            cut = columns[:, source : source + width]
            mask = head_mask(k, first, cut.shape)
            for w in range(width // 128):
                at = first // 128 + w
                lanes = slice(w * 128, w * 128 + 128)
                if merged[at] is None:
                    merged[at] = cut[:, lanes]
                else:
                    merged[at] = jnp.where(mask[:, lanes], cut[:, lanes], merged[at])
        for out, (begin, end) in zip(outs, bundles):
            for at, piece in enumerate(merged):
                first = c * GW + at * 128
                if begin <= first < end:
                    out[:, first - begin : first - begin + 128] = piece


def part_by_part(weight, group, bundles):
    rows = weight.shape[0]
    tile = 128
    return pl.pallas_call(
        functools.partial(part_kernel, bundles),
        out_shape=[jax.ShapeDtypeStruct((rows, end - begin), BF16) for begin, end in bundles],
        grid=(rows // tile,),
        in_specs=[pl.BlockSpec((tile, 3 * GW), lambda i: (i, group))],
        out_specs=[pl.BlockSpec((tile, end - begin), lambda i: (i, 0)) for begin, end in bundles],
        compiler_params=params(),
        cost_estimate=LIGHT,
        name="parts",
    )(weight)


def qkv_kernel(pieces, bundle, order, normed, *refs):
    count = 1 + max(part[0] for piece in pieces for part in piece)
    weights = refs[:count]
    bias, cosine, sine = refs[count : count + 3]
    outs = refs[count + 3 : count + 3 + len(bundle)]
    total, held_rows, held_weights, row_sems, weight_sems = refs[count + 3 + len(bundle) :]
    depth = weights[0].shape[0]

    def row_copy(j):
        lanes = pl.ds(pl.multiple_of(order[j] * depth, 128), depth)
        return pltpu.make_async_copy(
            normed.at[:, lanes], held_rows.at[:, pl.ds(j * depth, depth)], row_sems.at[j]
        )

    def weight_copies(j):
        found, at = [], 0
        for n, (source, first, width) in enumerate(pieces[j]):
            found.append(
                pltpu.make_async_copy(
                    weights[source].at[:, pl.ds(first, width)],
                    held_weights.at[pl.ds(j * depth, depth), pl.ds(at, width)],
                    weight_sems.at[j, n],
                )
            )
            at += width
        return found

    for j in range(len(pieces)):
        row_copy(j).start()
        for one in weight_copies(j):
            one.start()
    halves = 2
    each = len(pieces) // halves
    height = total.shape[0] // 2
    for n in range(halves):
        for j in range(n * each, (n + 1) * each):
            row_copy(j).wait()
            for one in weight_copies(j):
                one.wait()
        inner = slice(n * each * depth, (n + 1) * each * depth)
        for m in range(2):
            rows = slice(m * height, (m + 1) * height)
            part = jnp.dot(
                held_rows[rows, inner], held_weights[inner, :], preferred_element_type=F32
            )
            if n == 0:
                total[rows, :] = part
            else:
                total[rows, :] += part

    tile = 64

    def body(i, carry):
        rows = pl.ds(pl.multiple_of(i * tile, tile), tile)
        for spot, c in enumerate(bundle):
            lanes = slice(spot * GW, (spot + 1) * GW)
            x = total[rows, lanes] + bias[:, lanes]
            if c < 2:
                lane = lax.broadcasted_iota(jnp.int32, x.shape, 1) % HS
                turned = jnp.where(
                    lane < HS // 8,
                    -pltpu.roll(x, GW - HS // 8, 1),
                    pltpu.roll(x, HS // 8, 1),
                )
                x = x * cosine[rows, :] + turned * sine[rows, :]
            outs[spot][rows, :] = x.astype(BF16)
        return carry

    lax.fori_loop(0, total.shape[0] // tile, body, 0)


def project(normed, pieces, order, bias, tables, bundle):
    rows, features = normed.shape
    arrays, plan = [], []
    for piece in pieces:
        parts = []
        for array, first, width in piece:
            arrays.append(array)
            parts.append((len(arrays) - 1, first, width))
        plan.append(parts)
    depth = arrays[0].shape[0]
    columns = len(bundle) * GW
    out = jax.ShapeDtypeStruct((rows, GW), BF16)
    vmem = pl.BlockSpec(memory_space=pltpu.VMEM)
    anywhere = pl.BlockSpec(memory_space=pl.ANY)
    return pl.pallas_call(
        functools.partial(qkv_kernel, plan, bundle),
        out_shape=[out] * len(bundle),
        in_specs=[pl.BlockSpec(memory_space=pltpu.SMEM)]
        + [anywhere] * (len(arrays) + 1)
        + [vmem] * 3,
        out_specs=[vmem] * len(bundle),
        scratch_shapes=[
            pltpu.VMEM((rows, columns), F32),
            pltpu.VMEM((rows, features), BF16),
            pltpu.VMEM((features, columns), BF16),
            pltpu.SemaphoreType.DMA((len(plan),)),
            pltpu.SemaphoreType.DMA((len(plan), max(len(parts) for parts in plan))),
        ],
        compiler_params=params(),
        cost_estimate=LIGHT,
        name="project",
    )(order, normed, *arrays, bias, *tables)


def prefix_kernel(blocks, starts, lengths, *refs):
    queries = refs[:blocks]
    k_own, k_other, v_own, v_other = refs[blocks : blocks + 4]
    outs = refs[blocks + 4 : 2 * blocks + 4]
    totals = refs[2 * blocks + 4]
    slot = pl.program_id(0)
    slots = pl.num_programs(0)
    rows = queries[0].shape[0]

    @pl.when(slot == 0)
    def _():
        totals[...] = jnp.zeros_like(totals)

    begin, size, offset = [], [], []
    count = 0
    for b in range(blocks):
        begin.append(starts[slot * blocks + b])
        size.append(lengths[slot * blocks + b])
        offset.append(count)
        count = count + size[b]

    def serve(keys, values):
        def tile(base, height):
            down = lax.broadcasted_iota(jnp.int32, (height, 1), 0) + base
            across = lax.broadcasted_iota(jnp.int32, (1, height), 1) + base

            def sources(place, b):
                within = place - offset[b]
                return jnp.where((within >= 0) & (within < size[b]), within + begin[b], -1)

            picked = None
            for b in range(blocks):
                spread = lax.broadcasted_iota(jnp.int32, (height, rows), 1)
                one_hot = jnp.where(spread == sources(down, b), 1.0, 0.0).astype(BF16)
                part = jnp.dot(one_hot, queries[b][...], preferred_element_type=F32)
                picked = part if picked is None else picked + part
            picked = picked.astype(BF16)
            merged = [jnp.zeros((height, 128), F32) for _ in range(GW // 128)]
            extra = jnp.zeros((height, PACK), F32)
            place = lax.broadcasted_iota(jnp.int32, (height, PACK), 1)
            for k, (first, width) in enumerate(windows()):
                lanes = slice(first, first + width)
                mask = head_mask(k, first, (height, width))
                query = jnp.where(mask, picked[:, lanes], jnp.zeros((), BF16))
                scores = lax.dot_general(
                    query,
                    keys[0, :, lanes],
                    (((1,), (1,)), ((), ())),
                    preferred_element_type=F32,
                )
                peak = jnp.max(scores, axis=1, keepdims=True)
                weights = jnp.exp2((scores - peak) * (SCALE * LOG2E))
                mass = jnp.sum(weights, axis=1, keepdims=True)
                blended = jnp.dot(
                    weights.astype(BF16), values[0, :, lanes], preferred_element_type=F32
                )
                blended = blended * (1.0 / mass)
                for w in range(width // 128):
                    at = first // 128 + w
                    cut = slice(w * 128, w * 128 + 128)
                    merged[at] = jnp.where(mask[:, cut], blended[:, cut], merged[at])
                level = peak * SCALE + jnp.log(mass)
                high = level.astype(BF16).astype(F32)
                middle = (level - high).astype(BF16).astype(F32)
                low = level - high - middle
                for n, term in enumerate((high, middle, low)):
                    extra = jnp.where(place == 32 * n + k, term, extra)
            packed = jnp.concatenate(merged + [extra], axis=1).astype(BF16)
            for b in range(blocks):
                spread = lax.broadcasted_iota(jnp.int32, (rows, height), 0)
                one_hot = jnp.where(spread == sources(across, b), 1.0, 0.0).astype(BF16)
                totals[b] += jnp.dot(one_hot, packed, preferred_element_type=F32)

        large = 256
        small = 128
        full = lax.div(count, large)
        rest = count - full * large

        def body(j, carry):
            tile(j * large, large)
            return carry

        lax.fori_loop(0, full + jnp.where(rest > small, 1, 0), body, 0)

        @pl.when((rest > 0) & (rest <= small))
        def _():
            tile(full * large, small)

    half = slots // 2

    @pl.when(slot < half)
    def _():
        serve(k_own, v_own)

    @pl.when(slot >= half)
    def _():
        serve(k_other, v_other)

    @pl.when(slot == slots - 1)
    def _():
        for b in range(blocks):
            outs[b][...] = totals[b].astype(BF16)


def prefix_attention(group, queries, cache, starts, lengths):
    blocks = len(queries)
    rows = queries[0].shape[0]
    held, length, _ = cache[0].shape
    width = GW + PACK
    whole = lambda s, starts, lengths: (0, 0)
    own = lambda s, starts, lengths: (jnp.minimum(s, held - 1), 0, group)
    other = lambda s, starts, lengths: (jnp.maximum(s - held, 0), 0, group)
    block = (1, length, GW)
    return pl.pallas_call(
        functools.partial(prefix_kernel, blocks),
        out_shape=[jax.ShapeDtypeStruct((rows, width), BF16)] * blocks,
        grid_spec=pltpu.PrefetchScalarGridSpec(
            num_scalar_prefetch=2,
            grid=(2 * held,),
            in_specs=[pl.BlockSpec((rows, GW), whole)] * blocks
            + [pl.BlockSpec(block, own), pl.BlockSpec(block, other)] * 2,
            out_specs=[pl.BlockSpec((rows, width), whole)] * blocks,
            scratch_shapes=[pltpu.VMEM((blocks, rows, width), F32)],
        ),
        compiler_params=params(),
        cost_estimate=LIGHT,
        name="prefix",
    )(starts, lengths, *queries, *cache)


def suffix_kernel(row_start, queries, keys, values, out, levels):
    rows = queries.shape[0]
    tile = 128
    for i in range(rows // tile):
        at = slice(i * tile, (i + 1) * tile)
        wide = (i + 1) * tile
        row = lax.broadcasted_iota(jnp.int32, (tile, wide), 0) + i * tile
        column = lax.broadcasted_iota(jnp.int32, (tile, wide), 1)
        allowed = (column <= row) & (column >= row_start[at, :])
        merged = [jnp.zeros((tile, 128), F32) for _ in range(GW // 128)]
        level_row = jnp.zeros((tile, PACK), F32)
        place = lax.broadcasted_iota(jnp.int32, (tile, PACK), 1)
        for k, (first, width) in enumerate(windows()):
            lanes = slice(first, first + width)
            mask = head_mask(k, first, (tile, width))
            query = jnp.where(mask, queries[at, lanes], jnp.zeros((), BF16))
            scores = lax.dot_general(
                query,
                keys[:wide, lanes],
                (((1,), (1,)), ((), ())),
                preferred_element_type=F32,
            )
            scores = jnp.where(allowed, scores, -jnp.inf)
            peak = jnp.max(scores, axis=1, keepdims=True)
            weights = jnp.exp2((scores - peak) * (SCALE * LOG2E))
            mass = jnp.sum(weights, axis=1, keepdims=True)
            blended = jnp.dot(
                weights.astype(BF16), values[:wide, lanes], preferred_element_type=F32
            )
            blended = blended * (1.0 / mass)
            for w in range(width // 128):
                spot = first // 128 + w
                cut = slice(w * 128, w * 128 + 128)
                merged[spot] = jnp.where(mask[:, cut], blended[:, cut], merged[spot])
            level_row = jnp.where(place == k, peak * SCALE + jnp.log(mass), level_row)
        out[at, :] = jnp.concatenate(merged, axis=1)
        levels[at, :] = level_row


def suffix_attention(row_start, queries, keys, values):
    rows = queries.shape[0]
    return pl.pallas_call(
        suffix_kernel,
        out_shape=(
            jax.ShapeDtypeStruct((rows, GW), F32),
            jax.ShapeDtypeStruct((rows, PACK), F32),
        ),
        compiler_params=params(),
        cost_estimate=LIGHT,
        name="suffix",
    )(row_start, queries, keys, values)


def merge_kernel(blocks, *refs):
    parts = refs[:blocks]
    suffix, levels, out = refs[blocks:]
    rows = suffix.shape[0]
    tile = 128
    for i in range(rows // tile):
        at = slice(i * tile, (i + 1) * tile)
        prefix = parts[0][at, :].astype(F32)
        for b in range(1, blocks):
            prefix = prefix + parts[b][at, :].astype(F32)
        terms = prefix[:, GW:]
        pre = terms + pltpu.roll(terms, PACK - 32, 1) + pltpu.roll(terms, PACK - 64, 1)
        suf = levels[at, :]
        top = jnp.maximum(pre, suf)
        pre = jnp.exp(pre - top)
        suf = jnp.exp(suf - top)
        shares = pre / (pre + suf)
        spread = jnp.zeros((tile, GW), F32)
        for k in range(GROUP_HEADS):
            spread = jnp.where(head_mask(k, 0, (tile, GW)), shares[:, k : k + 1], spread)
        out[at, :] = (spread * prefix[:, :GW] + (1.0 - spread) * suffix[at, :]).astype(BF16)


def merge(parts, suffix, levels):
    rows = suffix.shape[0]
    return pl.pallas_call(
        functools.partial(merge_kernel, len(parts)),
        out_shape=jax.ShapeDtypeStruct((rows, GW), BF16),
        compiler_params=params(),
        cost_estimate=LIGHT,
        name="merge",
    )(*parts, suffix, levels)


def output_kernel(groups, lines, place, *refs):
    attention = refs[: 2 * groups]
    own, landed, crossed, out, held, joined, sems = refs[2 * groups :]
    at = pl.program_id(0)
    rows, share = out.shape[1:]
    depth = own.shape[0]
    half = lines // 2
    side, core = place[0], place[1]

    def own_copy(a):
        lanes = pl.ds(pl.multiple_of((2 * a + side) * share, 128), share)
        return pltpu.make_async_copy(
            own.at[:, lanes], held.at[a, pl.ds(0, depth)], sems.at[2 * a]
        )

    def other_copy(a):
        source = landed if a < half else crossed
        spot = lax.rem(a + core * half, lines)
        lanes = pl.ds((a % half) * share, share)
        return pltpu.make_async_copy(
            source.at[:, lanes], held.at[spot, pl.ds(depth, depth)], sems.at[2 * a + 1]
        )

    @pl.when(at == 0)
    def _():
        for a in range(lines):
            own_copy(a).start()
            other_copy(a).start()
        for n in range(2 * groups):
            joined[:, n * GW : (n + 1) * GW] = attention[n][...]

    own_copy(at).wait()
    sent = lax.rem(at + core * half, lines)
    pltpu.make_async_copy(
        landed.at[:, pl.ds(0, share)],
        held.at[at, pl.ds(depth, depth)],
        sems.at[2 * sent + 1],
    ).wait()
    out[0] = jnp.dot(joined[...], held[at], preferred_element_type=F32)


def output_projection(place, attention, own, landed, crossed, lines):
    rows = attention[0].shape[0]
    depth, features = own.shape
    share = features // (2 * lines)
    vmem = pl.BlockSpec((rows, GW), lambda a, place: (0, 0))
    anywhere = pl.BlockSpec(memory_space=pl.ANY)
    return pl.pallas_call(
        functools.partial(output_kernel, len(attention) // 2, lines),
        out_shape=jax.ShapeDtypeStruct((lines, rows, share), F32),
        grid_spec=pltpu.PrefetchScalarGridSpec(
            num_scalar_prefetch=1,
            grid=(lines,),
            in_specs=[vmem] * len(attention) + [anywhere] * 3,
            out_specs=pl.BlockSpec((1, rows, share), lambda a, place: (a, 0, 0)),
            scratch_shapes=[
                pltpu.VMEM((lines, 2 * depth, share), BF16),
                pltpu.VMEM((rows, 2 * depth), BF16),
                pltpu.SemaphoreType.DMA((2 * lines,)),
            ],
        ),
        compiler_params=params(),
        cost_estimate=LIGHT,
        name="output",
    )(place, *attention, own, landed, crossed)


def on_device(
    hidden_states,
    norm_gain,
    norm_bias,
    qkv_weight,
    qkv_bias,
    dense_weight,
    dense_bias,
    prefix_keys,
    prefix_values,
    suffix_len,
    request_order,
    group_slot,
):
    rows, share = hidden_states.shape
    held, prefix_length, local_width = prefix_keys.shape
    groups_local = local_width // GW
    tok_size = lax.axis_size("tok")
    head_size = lax.axis_size("head")
    chips = tok_size // 2
    lines = head_size // 2
    group_count = held * tok_size
    tok = lax.axis_index("tok")
    head = lax.axis_index("head")
    core, chip = tok % 2, tok // 2
    side, line = head % 2, head // 2

    def to_core(x):
        return lax.ppermute(x, "tok", [(t, t ^ 1) for t in range(tok_size)])

    def to_chip(x, shift):
        return lax.ppermute(
            x,
            "tok",
            [(t, (t // 2 + shift) % chips * 2 + t % 2) for t in range(tok_size)],
        )

    def to_side(x):
        return lax.ppermute(x, "head", [(h, h ^ 1) for h in range(head_size)])

    def after(x, *others):
        return lax.optimization_barrier((x, others))[0]

    layout = jnp.stack([suffix_len[0], request_order[0]])
    layouts = [layout] + [to_chip(layout, shift) for shift in range(1, chips)]
    (first,) = part_by_part(qkv_weight, 0, ((0, 3 * GW),))
    first, layouts = lax.optimization_barrier((first, layouts))

    last = lines - 1

    def to_side_from(x, lowest, highest):
        return lax.ppermute(
            x, "head", [(h, h ^ 1) for h in range(head_size) if lowest <= h // 2 <= highest]
        )

    across = to_side(hidden_states)
    blocks = [hidden_states, across]
    places = [head, head ^ 1]
    arriving = [to_chip(first, shift) for shift in range(1, chips)]
    up = down = hidden_states
    settled = across
    for step in range(last):
        if step > 0:
            up, down, settled, first = lax.optimization_barrier((up, down, settled, first))
            blocks[4 * step - 5 if step > 1 else 1] = settled
        up = lax.ppermute(
            up, "head", [(h, h + 2) for h in range(head_size) if step <= h // 2 < last]
        )
        down = lax.ppermute(
            down, "head", [(h, h - 2) for h in range(head_size) if 0 < h // 2 <= last - step]
        )
        settled = across if step == 0 else blocks[4 * step - 1]
        blocks += [up, to_side_from(up, step + 1, last)]
        blocks += [down, to_side_from(down, 0, last - 1 - step)]
        for there, valid in (
            (line - 1 - step, line >= step + 1),
            (line + 1 + step, line + 1 + step <= last),
        ):
            places += [
                jnp.where(valid, 2 * there + side, -1),
                jnp.where(valid, 2 * there + 1 - side, -1),
            ]
    places = jnp.stack(places).astype(jnp.int32)

    columns = 3 * GW
    order = [tok, tok ^ 1]
    for shift in range(1, chips):
        source = (chip + chips - shift) % chips * 2 + core
        order += [source, source ^ 1]
    order = jnp.stack(order).astype(jnp.int32)
    source, _ = lax.optimization_barrier((qkv_weight, layouts))
    cuts = ((0, columns), (0, 2 * GW), (2 * GW, columns))
    later = [part_by_part(source, g, cuts) for g in range(1, groups_local)]
    lengths = suffix_len[0]
    starts, row_start, within = shard_layout(lengths, request_order[0], rows)
    labels = jnp.arange(group_count, dtype=jnp.int32)
    slot_match = (group_slot[:, None] == labels[None, :]).astype(jnp.int32)

    def served_spans(one):
        firsts = shard_layout(one[0], one[1], rows)[0]
        spans = jnp.stack(
            [
                jnp.sum(firsts[:, None] * slot_match, axis=0),
                jnp.sum(one[0][:, None] * slot_match, axis=0),
            ]
        )
        return jnp.concatenate(
            [
                lax.dynamic_slice(spans, (0, tok * held), (2, held)),
                lax.dynamic_slice(spans, (0, (tok ^ 1) * held), (2, held)),
            ],
            axis=1,
        )

    served = jnp.stack([served_spans(one) for one in layouts], axis=2)
    tables = rotary_tables(prefix_length + within)
    bias = qkv_bias.astype(F32).reshape(groups_local, GROUP_HEADS, 3, HS)
    bias = jnp.transpose(bias, (0, 2, 1, 3)).reshape(groups_local, 1, columns)
    bias = [
        [bias[g]] if g == 0 else [bias[g][:, : 2 * GW], bias[g][:, 2 * GW :]]
        for g in range(groups_local)
    ]

    half = lines // 2
    outgoing = jnp.concatenate(
        [
            lax.dynamic_slice(
                dense_weight,
                (0, (2 * (core * half + a) + 1 - side) * share),
                (dense_weight.shape[0], share),
            )
            for a in range(half)
        ],
        axis=1,
    )
    ready = (
        served[0].reshape(-1),
        served[1].reshape(-1),
        tables,
        bias,
        order,
        row_start[:, None],
        jnp.stack([side, core]).astype(jnp.int32),
        outgoing,
        later,
        places,
        blocks,
    )
    arriving, ready = lax.optimization_barrier((arriving, ready))
    span_start, span_length, tables, bias, order, row_start, place, outgoing, later = ready[:9]
    places, blocks = ready[9:]

    def send(mine):
        return [to_chip(mine, shift) for shift in range(1, chips)]

    def exchange(queries):
        return [queries] + [to_chip(queries, shift) for shift in range(1, chips)]

    def pieces_of(own, arrived, first, width):
        pieces = [[(one, first, width)] for one in own]
        for n in range(chips - 1):
            for which in range(2):
                pieces.append([(part[n][which], 0, part[n][which].shape[1]) for part in arrived])
        return pieces

    def crossing(arrived):
        return [(one, to_core(one)) for one in arrived]

    coming = [send(after(one[1], arriving)) for one in later]
    first_pieces = pieces_of((first, to_core(first)), [crossing(arriving)], 0, columns)
    normed = layer_norm(blocks, places, norm_gain, norm_bias)
    landed = to_side(after(outgoing, normed))
    cache = [prefix_keys, to_core(after(prefix_keys, arriving))]
    cache += [prefix_values, to_core(after(prefix_values, arriving))]
    own = [(one[0], to_core(after(one[0], normed))) for one in later]
    heads = [project(normed, first_pieces, order, bias[0][0], tables, (0, 1, 2))]
    asked = [exchange(heads[0][0])]
    suffixes = [suffix_attention(row_start, *heads[0])]
    settled = suffixes[0]
    for g in range(1, groups_local):
        arrived = crossing(after(coming[g - 1], settled))
        pair = project(
            normed, pieces_of(own[g - 1], [arrived], 0, 2 * GW), order, bias[g][0], tables, (0, 1)
        )
        heads.append(pair)
        asked.append(exchange(pair[0]))
        settled = pair
    values_coming = [send(after(one[2], coming)) for one in later]
    asked[0] = after(asked[0], settled)
    returned = []
    for g in range(groups_local):
        if g > 0:
            asked[g] = after(asked[g], answers)
        answers = prefix_attention(g, asked[g], cache, span_start, span_length)
        returned.append([answers[0]] + [to_chip(answers[s], chips - s) for s in range(1, chips)])
    crossed = to_core(after(landed, answers))
    for g in range(1, groups_local):
        arrived = crossing(after(values_coming[g - 1], answers))
        (values,) = project(
            normed, pieces_of(own[g - 1], [arrived], 2 * GW, GW), order, bias[g][1], tables, (2,)
        )
        suffixes.append(suffix_attention(row_start, heads[g][0], heads[g][1], values))
    attention_own, attention_side = [], []
    for g in range(groups_local):
        attention = merge(after(returned[g], suffixes[-1]), *suffixes[g])
        attention_own.append(attention)
        attention_side.append(to_side(attention))
    partial = output_projection(
        place, attention_own + attention_side, dense_weight, landed, crossed, lines
    )

    cuts = 2
    height = rows // cuts

    def chunk(place, cut):
        place = jnp.clip(place, 0, last)
        return lax.dynamic_slice(
            partial, (place, cut * height, 0), (1, height, share)
        ).reshape(height, share)

    passing = [None] * cuts
    for step in range(last):
        up_pairs = [(h, h + 2) for h in range(head_size) if h // 2 <= step and h // 2 < last]
        down_pairs = [(h, h - 2) for h in range(head_size) if last - h // 2 <= step and h // 2 > 0]
        for cut in range(cuts):
            up = chunk(last + line - step, cut)
            down = chunk(line - last + step, cut)
            if passing[cut] is not None:
                if cut > 0:
                    passing[cut], sent = lax.optimization_barrier((passing[cut], sent))
                up = up + passing[cut][0].astype(F32)
                down = down + passing[cut][1].astype(F32)
            up, down = lax.optimization_barrier((up.astype(BF16), down.astype(BF16)))
            sent = up
            passing[cut] = lax.optimization_barrier(
                (lax.ppermute(up, "head", up_pairs), lax.ppermute(down, "head", down_pairs))
            )
    base = hidden_states.astype(F32) + dense_bias.astype(F32)
    done = [
        base[cut * height : (cut + 1) * height]
        + (chunk(line, cut) + passing[cut][0].astype(F32) + passing[cut][1].astype(F32))
        for cut in range(cuts)
    ]
    return jnp.concatenate(done, axis=0).astype(BF16)


def solution(mesh):
    placed = (
        P("tok", "head"),
        P(),
        P(),
        P("tok", "head"),
        P("head"),
        P("head", None),
        P("head"),
        P("tok", None, "head"),
        P("tok", None, "head"),
        P("tok", None),
        P("tok", None),
        P(),
    )
    return jax.shard_map(
        on_device, mesh=mesh, in_specs=placed, out_specs=P("tok", "head"), check_vma=False
    )
```

```python
import functools
import math

import jax
import jax.numpy as jnp
from jax import lax
from jax.experimental import pallas as pl
from jax.experimental.pallas import tpu as pltpu
from jax.sharding import PartitionSpec as P

HS = 96
GROUP_HEADS = 4
GW = GROUP_HEADS * HS
PACK = 128
F32 = jnp.float32
BF16 = jnp.bfloat16
VMEM_LIMIT = 56 * 1024 * 1024
SCALE = 1.0 / math.sqrt(HS)
LOG2E = math.log2(math.e)
LIGHT = pl.CostEstimate(flops=1000, bytes_accessed=1000, transcendentals=0)


def windows():
    found = []
    for k in range(GROUP_HEADS):
        first = k * HS // 128 * 128
        last = -(-(k * HS + HS) // 128) * 128
        found.append((first, last - first))
    return found


def head_mask(k, first, shape):
    lane = lax.broadcasted_iota(jnp.int32, shape, 1) + first
    return (lane >= k * HS) & (lane < (k + 1) * HS)


def params():
    return pltpu.CompilerParams(vmem_limit_bytes=VMEM_LIMIT)


def norm_kernel(count, chunks, places, *refs):
    blocks = refs[:count]
    gain, shift, out, held, ready, sems, out_sems = refs[count:]
    share = blocks[0].shape[1]
    height = held.shape[0] // chunks
    tile = 32

    def copy(j, chunk):
        lanes = pl.ds(pl.multiple_of(places[j] * share, 128), share)
        rows = pl.ds(chunk * height, height)
        return pltpu.make_async_copy(
            blocks[j].at[rows, :], held.at[rows, lanes], sems.at[j, chunk]
        )

    def out_copy(chunk):
        rows = pl.ds(chunk * height, height)
        return pltpu.make_async_copy(ready.at[rows, :], out.at[rows, :], out_sems.at[chunk])

    for chunk in range(chunks):
        for j in range(count):

            @pl.when(places[j] >= 0)
            def _(j=j, chunk=chunk):
                copy(j, chunk).start()

    for chunk in range(chunks):
        for j in range(count):

            @pl.when(places[j] >= 0)
            def _(j=j, chunk=chunk):
                copy(j, chunk).wait()

        def body(i, carry, chunk=chunk):
            rows = pl.ds(pl.multiple_of(chunk * height + i * tile, tile), tile)
            widened = held[rows, :].astype(F32)
            center = jnp.mean(widened, axis=-1, keepdims=True)
            moved = widened - center
            spread = jnp.mean(jnp.square(moved), axis=-1, keepdims=True)
            scaled = moved * lax.rsqrt(spread + 1e-05) * gain[...] + shift[...]
            ready[rows, :] = scaled.astype(BF16)
            return carry

        lax.fori_loop(0, height // tile, body, 0)
        out_copy(chunk).start()
    for chunk in range(chunks):
        out_copy(chunk).wait()


def layer_norm(blocks, places, gain, shift):
    rows = blocks[0].shape[0]
    features = gain.shape[0]
    count = len(blocks)
    chunks = 4
    vmem = pl.BlockSpec(memory_space=pltpu.VMEM)
    return pl.pallas_call(
        functools.partial(norm_kernel, count, chunks),
        out_shape=jax.ShapeDtypeStruct((rows, features), BF16),
        in_specs=[pl.BlockSpec(memory_space=pltpu.SMEM)]
        + [pl.BlockSpec(memory_space=pl.ANY)] * count
        + [vmem] * 2,
        out_specs=pl.BlockSpec(memory_space=pl.ANY),
        scratch_shapes=[
            pltpu.VMEM((rows, features), BF16),
            pltpu.VMEM((rows, features), BF16),
            pltpu.SemaphoreType.DMA((count, chunks)),
            pltpu.SemaphoreType.DMA((chunks,)),
        ],
        compiler_params=params(),
        cost_estimate=LIGHT,
        name="norm",
    )(places, *blocks, gain[None, :], shift[None, :])


def shard_layout(lengths, ordering, row_count):
    group_count = lengths.shape[0]
    labels = jnp.arange(group_count, dtype=jnp.int32)
    chosen = (ordering[:, None] == labels[None, :]).astype(jnp.int32)
    ranking = jnp.sum(labels[:, None] * chosen, axis=0)
    earlier = (ranking[None, :] < ranking[:, None]).astype(jnp.int32)
    starts = jnp.sum(earlier * lengths[None, :], axis=1)
    places = jnp.arange(row_count, dtype=jnp.int32)
    member = (
        (places[:, None] >= starts[None, :]) & (places[:, None] < (starts + lengths)[None, :])
    ).astype(jnp.int32)
    row_start = jnp.sum(member * starts[None, :], axis=1)
    return starts, row_start, places - row_start


def rotary_tables(positions):
    rot = HS // 4
    half = rot // 2
    inverse = 10000.0 ** (-(jnp.arange(half, dtype=F32) * 2.0) / rot)
    lanes = jnp.concatenate([inverse, inverse, jnp.zeros((HS - rot,), F32)])
    lanes = jnp.tile(lanes, GROUP_HEADS)
    angles = positions.astype(F32)[:, None] * lanes[None, :]
    return [jnp.cos(angles), jnp.sin(angles)]


def part_kernel(bundles, wide, *outs):
    columns = wide[...]
    for c in range(3):
        merged = [None] * (GW // 128)
        for k, (first, width) in enumerate(windows()):
            source = 2 * HS * k + HS * c + first
            cut = columns[:, source : source + width]
            mask = head_mask(k, first, cut.shape)
            for w in range(width // 128):
                at = first // 128 + w
                lanes = slice(w * 128, w * 128 + 128)
                if merged[at] is None:
                    merged[at] = cut[:, lanes]
                else:
                    merged[at] = jnp.where(mask[:, lanes], cut[:, lanes], merged[at])
        for out, (begin, end) in zip(outs, bundles):
            for at, piece in enumerate(merged):
                first = c * GW + at * 128
                if begin <= first < end:
                    out[:, first - begin : first - begin + 128] = piece


def part_by_part(weight, group, bundles):
    rows = weight.shape[0]
    tile = 128
    return pl.pallas_call(
        functools.partial(part_kernel, bundles),
        out_shape=[jax.ShapeDtypeStruct((rows, end - begin), BF16) for begin, end in bundles],
        grid=(rows // tile,),
        in_specs=[pl.BlockSpec((tile, 3 * GW), lambda i: (i, group))],
        out_specs=[pl.BlockSpec((tile, end - begin), lambda i: (i, 0)) for begin, end in bundles],
        compiler_params=params(),
        cost_estimate=LIGHT,
        name="parts",
    )(weight)


def qkv_kernel(pieces, bundle, order, normed, *refs):
    count = 1 + max(part[0] for piece in pieces for part in piece)
    weights = refs[:count]
    bias, cosine, sine = refs[count : count + 3]
    outs = refs[count + 3 : count + 3 + len(bundle)]
    total, held_rows, held_weights, row_sems, weight_sems = refs[count + 3 + len(bundle) :]
    depth = weights[0].shape[0]

    def row_copy(j):
        lanes = pl.ds(pl.multiple_of(order[j] * depth, 128), depth)
        return pltpu.make_async_copy(
            normed.at[:, lanes], held_rows.at[:, pl.ds(j * depth, depth)], row_sems.at[j]
        )

    def weight_copies(j):
        found, at = [], 0
        for n, (source, first, width) in enumerate(pieces[j]):
            found.append(
                pltpu.make_async_copy(
                    weights[source].at[:, pl.ds(first, width)],
                    held_weights.at[pl.ds(j * depth, depth), pl.ds(at, width)],
                    weight_sems.at[j, n],
                )
            )
            at += width
        return found

    for j in range(len(pieces)):
        row_copy(j).start()
        for one in weight_copies(j):
            one.start()
    halves = 2
    each = len(pieces) // halves
    height = total.shape[0] // 2
    for n in range(halves):
        for j in range(n * each, (n + 1) * each):
            row_copy(j).wait()
            for one in weight_copies(j):
                one.wait()
        inner = slice(n * each * depth, (n + 1) * each * depth)
        for m in range(2):
            rows = slice(m * height, (m + 1) * height)
            part = jnp.dot(
                held_rows[rows, inner], held_weights[inner, :], preferred_element_type=F32
            )
            if n == 0:
                total[rows, :] = part
            else:
                total[rows, :] += part

    tile = 64

    def body(i, carry):
        rows = pl.ds(pl.multiple_of(i * tile, tile), tile)
        for spot, c in enumerate(bundle):
            lanes = slice(spot * GW, (spot + 1) * GW)
            x = total[rows, lanes] + bias[:, lanes]
            if c < 2:
                lane = lax.broadcasted_iota(jnp.int32, x.shape, 1) % HS
                turned = jnp.where(
                    lane < HS // 8,
                    -pltpu.roll(x, GW - HS // 8, 1),
                    pltpu.roll(x, HS // 8, 1),
                )
                x = x * cosine[rows, :] + turned * sine[rows, :]
            outs[spot][rows, :] = x.astype(BF16)
        return carry

    lax.fori_loop(0, total.shape[0] // tile, body, 0)


def project(normed, pieces, order, bias, tables, bundle):
    rows, features = normed.shape
    arrays, plan = [], []
    for piece in pieces:
        parts = []
        for array, first, width in piece:
            arrays.append(array)
            parts.append((len(arrays) - 1, first, width))
        plan.append(parts)
    depth = arrays[0].shape[0]
    columns = len(bundle) * GW
    out = jax.ShapeDtypeStruct((rows, GW), BF16)
    vmem = pl.BlockSpec(memory_space=pltpu.VMEM)
    anywhere = pl.BlockSpec(memory_space=pl.ANY)
    return pl.pallas_call(
        functools.partial(qkv_kernel, plan, bundle),
        out_shape=[out] * len(bundle),
        in_specs=[pl.BlockSpec(memory_space=pltpu.SMEM)]
        + [anywhere] * (len(arrays) + 1)
        + [vmem] * 3,
        out_specs=[vmem] * len(bundle),
        scratch_shapes=[
            pltpu.VMEM((rows, columns), F32),
            pltpu.VMEM((rows, features), BF16),
            pltpu.VMEM((features, columns), BF16),
            pltpu.SemaphoreType.DMA((len(plan),)),
            pltpu.SemaphoreType.DMA((len(plan), max(len(parts) for parts in plan))),
        ],
        compiler_params=params(),
        cost_estimate=LIGHT,
        name="project",
    )(order, normed, *arrays, bias, *tables)


def prefix_kernel(blocks, starts, lengths, *refs):
    queries = refs[:blocks]
    k_own, k_other, v_own, v_other = refs[blocks : blocks + 4]
    outs = refs[blocks + 4 : 2 * blocks + 4]
    totals = refs[2 * blocks + 4]
    slot = pl.program_id(0)
    slots = pl.num_programs(0)
    rows = queries[0].shape[0]

    @pl.when(slot == 0)
    def _():
        totals[...] = jnp.zeros_like(totals)

    reach = min(256, rows)
    begin, size, offset, window = [], [], [], []
    count = 0
    for b in range(blocks):
        begin.append(starts[slot * blocks + b])
        first_row = jnp.minimum(lax.div(begin[b], 16) * 16, rows - reach)
        window.append(pl.multiple_of(first_row, 16))
        size.append(lengths[slot * blocks + b])
        offset.append(count)
        count = count + size[b]

    def serve(keys, values):
        def tile(base, height):
            down = lax.broadcasted_iota(jnp.int32, (height, 1), 0) + base
            across = lax.broadcasted_iota(jnp.int32, (1, height), 1) + base

            def sources(place, b):
                within = place - offset[b]
                return jnp.where(
                    (within >= 0) & (within < size[b]), within + begin[b] - window[b], -1
                )

            picked = None
            for b in range(blocks):
                spread = lax.broadcasted_iota(jnp.int32, (height, reach), 1)
                one_hot = jnp.where(spread == sources(down, b), 1.0, 0.0).astype(BF16)
                part = jnp.dot(
                    one_hot, queries[b][pl.ds(window[b], reach), :], preferred_element_type=F32
                )
                picked = part if picked is None else picked + part
            picked = picked.astype(BF16)
            merged = [jnp.zeros((height, 128), F32) for _ in range(GW // 128)]
            extra = jnp.zeros((height, PACK), F32)
            place = lax.broadcasted_iota(jnp.int32, (height, PACK), 1)
            for k, (first, width) in enumerate(windows()):
                lanes = slice(first, first + width)
                mask = head_mask(k, first, (height, width))
                query = jnp.where(mask, picked[:, lanes], jnp.zeros((), BF16))
                scores = lax.dot_general(
                    query,
                    keys[0, :, lanes],
                    (((1,), (1,)), ((), ())),
                    preferred_element_type=F32,
                )
                peak = jnp.max(scores, axis=1, keepdims=True)
                weights = jnp.exp2((scores - peak) * (SCALE * LOG2E))
                mass = jnp.sum(weights, axis=1, keepdims=True)
                blended = jnp.dot(
                    weights.astype(BF16), values[0, :, lanes], preferred_element_type=F32
                )
                blended = blended * (1.0 / mass)
                for w in range(width // 128):
                    at = first // 128 + w
                    cut = slice(w * 128, w * 128 + 128)
                    merged[at] = jnp.where(mask[:, cut], blended[:, cut], merged[at])
                level = peak * SCALE + jnp.log(mass)
                high = level.astype(BF16).astype(F32)
                middle = (level - high).astype(BF16).astype(F32)
                low = level - high - middle
                for n, term in enumerate((high, middle, low)):
                    extra = jnp.where(place == 32 * n + k, term, extra)
            packed = jnp.concatenate(merged + [extra], axis=1).astype(BF16)
            for b in range(blocks):
                spread = lax.broadcasted_iota(jnp.int32, (reach, height), 0)
                one_hot = jnp.where(spread == sources(across, b), 1.0, 0.0).astype(BF16)
                totals[b, pl.ds(window[b], reach), :] += jnp.dot(
                    one_hot, packed, preferred_element_type=F32
                )

        large = 256
        small = 128
        full = lax.div(count, large)
        rest = count - full * large

        def body(j, carry):
            tile(j * large, large)
            return carry

        lax.fori_loop(0, full + jnp.where(rest > small, 1, 0), body, 0)

        @pl.when((rest > 0) & (rest <= small))
        def _():
            tile(full * large, small)

    half = slots // 2

    @pl.when(slot < half)
    def _():
        serve(k_own, v_own)

    @pl.when(slot >= half)
    def _():
        serve(k_other, v_other)

    @pl.when(slot == slots - 1)
    def _():
        for b in range(blocks):
            outs[b][...] = totals[b].astype(BF16)


def prefix_attention(group, queries, cache, starts, lengths):
    blocks = len(queries)
    rows = queries[0].shape[0]
    held, length, _ = cache[0].shape
    width = GW + PACK
    whole = lambda s, starts, lengths: (0, 0)
    own = lambda s, starts, lengths: (jnp.minimum(s, held - 1), 0, group)
    other = lambda s, starts, lengths: (jnp.maximum(s - held, 0), 0, group)
    block = (1, length, GW)
    return pl.pallas_call(
        functools.partial(prefix_kernel, blocks),
        out_shape=[jax.ShapeDtypeStruct((rows, width), BF16)] * blocks,
        grid_spec=pltpu.PrefetchScalarGridSpec(
            num_scalar_prefetch=2,
            grid=(2 * held,),
            in_specs=[pl.BlockSpec((rows, GW), whole)] * blocks
            + [pl.BlockSpec(block, own), pl.BlockSpec(block, other)] * 2,
            out_specs=[pl.BlockSpec((rows, width), whole)] * blocks,
            scratch_shapes=[pltpu.VMEM((blocks, rows, width), F32)],
        ),
        compiler_params=params(),
        cost_estimate=LIGHT,
        name="prefix",
    )(starts, lengths, *queries, *cache)


def suffix_kernel(row_start, queries, keys, values, out, levels):
    rows = queries.shape[0]
    tile = 128
    for i in range(rows // tile):
        at = slice(i * tile, (i + 1) * tile)
        wide = (i + 1) * tile
        row = lax.broadcasted_iota(jnp.int32, (tile, wide), 0) + i * tile
        column = lax.broadcasted_iota(jnp.int32, (tile, wide), 1)
        allowed = (column <= row) & (column >= row_start[at, :])
        merged = [jnp.zeros((tile, 128), F32) for _ in range(GW // 128)]
        level_row = jnp.zeros((tile, PACK), F32)
        place = lax.broadcasted_iota(jnp.int32, (tile, PACK), 1)
        for k, (first, width) in enumerate(windows()):
            lanes = slice(first, first + width)
            mask = head_mask(k, first, (tile, width))
            query = jnp.where(mask, queries[at, lanes], jnp.zeros((), BF16))
            scores = lax.dot_general(
                query,
                keys[:wide, lanes],
                (((1,), (1,)), ((), ())),
                preferred_element_type=F32,
            )
            scores = jnp.where(allowed, scores, -jnp.inf)
            peak = jnp.max(scores, axis=1, keepdims=True)
            weights = jnp.exp2((scores - peak) * (SCALE * LOG2E))
            mass = jnp.sum(weights, axis=1, keepdims=True)
            blended = jnp.dot(
                weights.astype(BF16), values[:wide, lanes], preferred_element_type=F32
            )
            blended = blended * (1.0 / mass)
            for w in range(width // 128):
                spot = first // 128 + w
                cut = slice(w * 128, w * 128 + 128)
                merged[spot] = jnp.where(mask[:, cut], blended[:, cut], merged[spot])
            level_row = jnp.where(place == k, peak * SCALE + jnp.log(mass), level_row)
        out[at, :] = jnp.concatenate(merged, axis=1)
        levels[at, :] = level_row


def suffix_attention(row_start, queries, keys, values):
    rows = queries.shape[0]
    return pl.pallas_call(
        suffix_kernel,
        out_shape=(
            jax.ShapeDtypeStruct((rows, GW), F32),
            jax.ShapeDtypeStruct((rows, PACK), F32),
        ),
        compiler_params=params(),
        cost_estimate=LIGHT,
        name="suffix",
    )(row_start, queries, keys, values)


def merge_kernel(blocks, *refs):
    parts = refs[:blocks]
    suffix, levels, out = refs[blocks:]
    rows = suffix.shape[0]
    tile = 128
    for i in range(rows // tile):
        at = slice(i * tile, (i + 1) * tile)
        prefix = parts[0][at, :].astype(F32)
        for b in range(1, blocks):
            prefix = prefix + parts[b][at, :].astype(F32)
        terms = prefix[:, GW:]
        pre = terms + pltpu.roll(terms, PACK - 32, 1) + pltpu.roll(terms, PACK - 64, 1)
        suf = levels[at, :]
        top = jnp.maximum(pre, suf)
        pre = jnp.exp(pre - top)
        suf = jnp.exp(suf - top)
        shares = pre / (pre + suf)
        spread = jnp.zeros((tile, GW), F32)
        for k in range(GROUP_HEADS):
            spread = jnp.where(head_mask(k, 0, (tile, GW)), shares[:, k : k + 1], spread)
        out[at, :] = (spread * prefix[:, :GW] + (1.0 - spread) * suffix[at, :]).astype(BF16)


def merge(parts, suffix, levels):
    rows = suffix.shape[0]
    return pl.pallas_call(
        functools.partial(merge_kernel, len(parts)),
        out_shape=jax.ShapeDtypeStruct((rows, GW), BF16),
        compiler_params=params(),
        cost_estimate=LIGHT,
        name="merge",
    )(*parts, suffix, levels)


def output_kernel(groups, lines, place, *refs):
    attention = refs[: 2 * groups]
    own, landed, crossed, out, held, joined, sems = refs[2 * groups :]
    at = pl.program_id(0)
    rows, share = out.shape[1:]
    depth = own.shape[0]
    half = lines // 2
    side, core = place[0], place[1]

    def own_copy(a):
        lanes = pl.ds(pl.multiple_of((2 * a + side) * share, 128), share)
        return pltpu.make_async_copy(
            own.at[:, lanes], held.at[a, pl.ds(0, depth)], sems.at[2 * a]
        )

    def other_copy(a):
        source = landed if a < half else crossed
        spot = lax.rem(a + core * half, lines)
        lanes = pl.ds((a % half) * share, share)
        return pltpu.make_async_copy(
            source.at[:, lanes], held.at[spot, pl.ds(depth, depth)], sems.at[2 * a + 1]
        )

    @pl.when(at == 0)
    def _():
        for a in range(lines):
            own_copy(a).start()
            other_copy(a).start()
        for n in range(2 * groups):
            joined[:, n * GW : (n + 1) * GW] = attention[n][...]

    own_copy(at).wait()
    sent = lax.rem(at + core * half, lines)
    pltpu.make_async_copy(
        landed.at[:, pl.ds(0, share)],
        held.at[at, pl.ds(depth, depth)],
        sems.at[2 * sent + 1],
    ).wait()
    out[0] = jnp.dot(joined[...], held[at], preferred_element_type=F32)


def output_projection(place, attention, own, landed, crossed, lines):
    rows = attention[0].shape[0]
    depth, features = own.shape
    share = features // (2 * lines)
    vmem = pl.BlockSpec((rows, GW), lambda a, place: (0, 0))
    anywhere = pl.BlockSpec(memory_space=pl.ANY)
    return pl.pallas_call(
        functools.partial(output_kernel, len(attention) // 2, lines),
        out_shape=jax.ShapeDtypeStruct((lines, rows, share), F32),
        grid_spec=pltpu.PrefetchScalarGridSpec(
            num_scalar_prefetch=1,
            grid=(lines,),
            in_specs=[vmem] * len(attention) + [anywhere] * 3,
            out_specs=pl.BlockSpec((1, rows, share), lambda a, place: (a, 0, 0)),
            scratch_shapes=[
                pltpu.VMEM((lines, 2 * depth, share), BF16),
                pltpu.VMEM((rows, 2 * depth), BF16),
                pltpu.SemaphoreType.DMA((2 * lines,)),
            ],
        ),
        compiler_params=params(),
        cost_estimate=LIGHT,
        name="output",
    )(place, *attention, own, landed, crossed)


def on_device(
    hidden_states,
    norm_gain,
    norm_bias,
    qkv_weight,
    qkv_bias,
    dense_weight,
    dense_bias,
    prefix_keys,
    prefix_values,
    suffix_len,
    request_order,
    group_slot,
):
    rows, share = hidden_states.shape
    held, prefix_length, local_width = prefix_keys.shape
    groups_local = local_width // GW
    tok_size = lax.axis_size("tok")
    head_size = lax.axis_size("head")
    chips = tok_size // 2
    lines = head_size // 2
    group_count = held * tok_size
    tok = lax.axis_index("tok")
    head = lax.axis_index("head")
    core, chip = tok % 2, tok // 2
    side, line = head % 2, head // 2

    def to_core(x):
        return lax.ppermute(x, "tok", [(t, t ^ 1) for t in range(tok_size)])

    def to_chip(x, shift):
        return lax.ppermute(
            x,
            "tok",
            [(t, (t // 2 + shift) % chips * 2 + t % 2) for t in range(tok_size)],
        )

    def to_side(x):
        return lax.ppermute(x, "head", [(h, h ^ 1) for h in range(head_size)])

    def after(x, *others):
        return lax.optimization_barrier((x, others))[0]

    layout = jnp.stack([suffix_len[0], request_order[0]])
    layouts = [layout] + [to_chip(layout, shift) for shift in range(1, chips)]
    (first,) = part_by_part(qkv_weight, 0, ((0, 3 * GW),))
    first, layouts = lax.optimization_barrier((first, layouts))

    last = lines - 1

    def to_side_from(x, lowest, highest):
        return lax.ppermute(
            x, "head", [(h, h ^ 1) for h in range(head_size) if lowest <= h // 2 <= highest]
        )

    columns = 3 * GW
    source, _ = lax.optimization_barrier((qkv_weight, layouts))
    cuts = ((0, columns), (0, 2 * GW), (2 * GW, columns))
    later = [part_by_part(source, g, cuts) for g in range(1, groups_local)]
    across = to_side(hidden_states)
    blocks = [hidden_states, across]
    places = [head, head ^ 1]
    arriving = [to_chip(first, shift) for shift in range(1, chips)]
    up = down = hidden_states
    settled = across
    for step in range(last):
        if step > 0:
            up, down, settled, first, later = lax.optimization_barrier(
                (up, down, settled, first, later)
            )
            blocks[1 if step == 1 else tied] = settled
        up = lax.ppermute(
            up, "head", [(h, h + 2) for h in range(head_size) if step <= h // 2 < last]
        )
        down = lax.ppermute(
            down, "head", [(h, h - 2) for h in range(head_size) if 0 < h // 2 <= last - step]
        )
        from_below, from_above = line >= step + 1, line + 1 + step <= last
        below, above = line - 1 - step, line + 1 + step
        blocks += [up, down]
        places += [
            jnp.where(from_below, 2 * below + side, -1),
            jnp.where(from_above, 2 * above + side, -1),
        ]
        marked = len(blocks)
        if 2 * step + 1 < last:
            blocks += [to_side_from(up, step + 1, last), to_side_from(down, 0, last - 1 - step)]
            places += [
                jnp.where(from_below, 2 * below + 1 - side, -1),
                jnp.where(from_above, 2 * above + 1 - side, -1),
            ]
        else:
            here = after(jnp.where(from_below, up, down), blocks[-3])
            lines_with = [h for h in range(head_size) if h // 2 >= step + 1 or h // 2 <= last - 1 - step]
            blocks.append(lax.ppermute(here, "head", [(h, h ^ 1) for h in lines_with]))
            there = jnp.where(from_below, below, above)
            places.append(jnp.where(from_below | from_above, 2 * there + 1 - side, -1))
        if step > 0:
            tied, settled = previous, blocks[previous]
        previous = marked
    places = jnp.stack(places).astype(jnp.int32)

    order = [tok, tok ^ 1]
    for shift in range(1, chips):
        source = (chip + chips - shift) % chips * 2 + core
        order += [source, source ^ 1]
    order = jnp.stack(order).astype(jnp.int32)
    lengths = suffix_len[0]
    starts, row_start, within = shard_layout(lengths, request_order[0], rows)
    labels = jnp.arange(group_count, dtype=jnp.int32)
    slot_match = (group_slot[:, None] == labels[None, :]).astype(jnp.int32)

    def served_spans(one):
        firsts = shard_layout(one[0], one[1], rows)[0]
        spans = jnp.stack(
            [
                jnp.sum(firsts[:, None] * slot_match, axis=0),
                jnp.sum(one[0][:, None] * slot_match, axis=0),
            ]
        )
        return jnp.concatenate(
            [
                lax.dynamic_slice(spans, (0, tok * held), (2, held)),
                lax.dynamic_slice(spans, (0, (tok ^ 1) * held), (2, held)),
            ],
            axis=1,
        )

    served = jnp.stack([served_spans(one) for one in layouts], axis=2)
    tables = rotary_tables(prefix_length + within)
    bias = qkv_bias.astype(F32).reshape(groups_local, GROUP_HEADS, 3, HS)
    bias = jnp.transpose(bias, (0, 2, 1, 3)).reshape(groups_local, 1, columns)
    bias = [
        [bias[g]] if g == 0 else [bias[g][:, : 2 * GW], bias[g][:, 2 * GW :]]
        for g in range(groups_local)
    ]

    half = lines // 2
    outgoing = jnp.concatenate(
        [
            lax.dynamic_slice(
                dense_weight,
                (0, (2 * (core * half + a) + 1 - side) * share),
                (dense_weight.shape[0], share),
            )
            for a in range(half)
        ],
        axis=1,
    )
    ready = (
        served[0].reshape(-1),
        served[1].reshape(-1),
        tables,
        bias,
        order,
        row_start[:, None],
        jnp.stack([side, core]).astype(jnp.int32),
        outgoing,
        later,
        places,
        blocks,
    )
    arriving, ready = lax.optimization_barrier((arriving, ready))
    span_start, span_length, tables, bias, order, row_start, place, outgoing, later = ready[:9]
    places, blocks = ready[9:]

    def send(mine):
        return [to_chip(mine, shift) for shift in range(1, chips)]

    def exchange(queries):
        return [queries] + [to_chip(queries, shift) for shift in range(1, chips)]

    def pieces_of(own, arrived, first, width):
        pieces = [[(one, first, width)] for one in own]
        for n in range(chips - 1):
            for which in range(2):
                pieces.append([(part[n][which], 0, part[n][which].shape[1]) for part in arrived])
        return pieces

    def crossing(arrived):
        return [(one, to_core(one)) for one in arrived]

    coming = [send(after(one[1], arriving)) for one in later]
    first_pieces = pieces_of((first, to_core(first)), [crossing(arriving)], 0, columns)
    normed = layer_norm(blocks, places, norm_gain, norm_bias)
    landed = to_side(after(outgoing, normed))
    cache = [prefix_keys, to_core(after(prefix_keys, arriving))]
    cache += [prefix_values, to_core(after(prefix_values, arriving))]
    own = [(one[0], to_core(after(one[0], normed))) for one in later]
    heads = [project(normed, first_pieces, order, bias[0][0], tables, (0, 1, 2))]
    asked = [exchange(heads[0][0])]
    suffixes = [suffix_attention(row_start, *heads[0])]
    settled = suffixes[0]
    for g in range(1, groups_local):
        arrived = crossing(after(coming[g - 1], settled))
        pair = project(
            normed, pieces_of(own[g - 1], [arrived], 0, 2 * GW), order, bias[g][0], tables, (0, 1)
        )
        heads.append(pair)
        asked.append(exchange(pair[0]))
        settled = pair
    values_coming = [send(after(one[2], coming)) for one in later]
    asked[0] = after(asked[0], settled)
    returned = []
    for g in range(groups_local):
        if g > 0:
            asked[g] = after(asked[g], answers)
        answers = prefix_attention(g, asked[g], cache, span_start, span_length)
        returned.append([answers[0]] + [to_chip(answers[s], chips - s) for s in range(1, chips)])
    crossed = to_core(after(landed, answers))
    for g in range(1, groups_local):
        arrived = crossing(after(values_coming[g - 1], answers))
        (values,) = project(
            normed, pieces_of(own[g - 1], [arrived], 2 * GW, GW), order, bias[g][1], tables, (2,)
        )
        suffixes.append(suffix_attention(row_start, heads[g][0], heads[g][1], values))
    attention_own, attention_side = [], []
    for g in range(groups_local):
        attention = merge(after(returned[g], suffixes[-1]), *suffixes[g])
        attention_own.append(attention)
        attention_side.append(to_side(attention))
    partial = output_projection(
        place, attention_own + attention_side, dense_weight, landed, crossed, lines
    )

    cuts = 2
    height = rows // cuts

    def chunk(place, cut):
        place = jnp.clip(place, 0, last)
        return lax.dynamic_slice(
            partial, (place, cut * height, 0), (1, height, share)
        ).reshape(height, share)

    passing = [None] * cuts
    for step in range(last):
        up_pairs = [(h, h + 2) for h in range(head_size) if h // 2 <= step and h // 2 < last]
        down_pairs = [(h, h - 2) for h in range(head_size) if last - h // 2 <= step and h // 2 > 0]
        for cut in range(cuts):
            up = chunk(last + line - step, cut)
            down = chunk(line - last + step, cut)
            if passing[cut] is not None:
                if cut > 0:
                    passing[cut], sent = lax.optimization_barrier((passing[cut], sent))
                up = up + passing[cut][0].astype(F32)
                down = down + passing[cut][1].astype(F32)
            up, down = lax.optimization_barrier((up.astype(BF16), down.astype(BF16)))
            sent = up
            passing[cut] = lax.optimization_barrier(
                (lax.ppermute(up, "head", up_pairs), lax.ppermute(down, "head", down_pairs))
            )
    base = hidden_states.astype(F32) + dense_bias.astype(F32)
    done = [
        base[cut * height : (cut + 1) * height]
        + (chunk(line, cut) + passing[cut][0].astype(F32) + passing[cut][1].astype(F32))
        for cut in range(cuts)
    ]
    return jnp.concatenate(done, axis=0).astype(BF16)


def solution(mesh):
    placed = (
        P("tok", "head"),
        P(),
        P(),
        P("tok", "head"),
        P("head"),
        P("head", None),
        P("head"),
        P("tok", None, "head"),
        P("tok", None, "head"),
        P("tok", None),
        P("tok", None),
        P(),
    )
    return jax.shard_map(
        on_device, mesh=mesh, in_specs=placed, out_specs=P("tok", "head"), check_vma=False
    )
```

```python
import functools
import math

import jax
import jax.numpy as jnp
from jax import lax
from jax.experimental import pallas as pl
from jax.experimental.pallas import tpu as pltpu
from jax.sharding import PartitionSpec as P

HS = 96
GROUP_HEADS = 4
GW = GROUP_HEADS * HS
PACK = 128
F32 = jnp.float32
BF16 = jnp.bfloat16
VMEM_LIMIT = 56 * 1024 * 1024
SCALE = 1.0 / math.sqrt(HS)
LOG2E = math.log2(math.e)
LIGHT = pl.CostEstimate(flops=1000, bytes_accessed=1000, transcendentals=0)


def windows():
    found = []
    for k in range(GROUP_HEADS):
        first = k * HS // 128 * 128
        last = -(-(k * HS + HS) // 128) * 128
        found.append((first, last - first))
    return found


def head_mask(k, first, shape):
    lane = lax.broadcasted_iota(jnp.int32, shape, 1) + first
    return (lane >= k * HS) & (lane < (k + 1) * HS)


def params():
    return pltpu.CompilerParams(vmem_limit_bytes=VMEM_LIMIT)


def norm_kernel(count, chunks, places, *refs):
    blocks = refs[:count]
    gain, shift, out, held, ready, sems, out_sems = refs[count:]
    share = blocks[0].shape[1]
    height = held.shape[0] // chunks
    tile = 32

    def copy(j, chunk):
        lanes = pl.ds(pl.multiple_of(places[j] * share, 128), share)
        rows = pl.ds(chunk * height, height)
        return pltpu.make_async_copy(
            blocks[j].at[rows, :], held.at[rows, lanes], sems.at[j, chunk]
        )

    def out_copy(chunk):
        rows = pl.ds(chunk * height, height)
        return pltpu.make_async_copy(ready.at[rows, :], out.at[rows, :], out_sems.at[chunk])

    for chunk in range(chunks):
        for j in range(count):

            @pl.when(places[j] >= 0)
            def _(j=j, chunk=chunk):
                copy(j, chunk).start()

    for chunk in range(chunks):
        for j in range(count):

            @pl.when(places[j] >= 0)
            def _(j=j, chunk=chunk):
                copy(j, chunk).wait()

        def body(i, carry, chunk=chunk):
            rows = pl.ds(pl.multiple_of(chunk * height + i * tile, tile), tile)
            widened = held[rows, :].astype(F32)
            center = jnp.mean(widened, axis=-1, keepdims=True)
            moved = widened - center
            spread = jnp.mean(jnp.square(moved), axis=-1, keepdims=True)
            scaled = moved * lax.rsqrt(spread + 1e-05) * gain[...] + shift[...]
            ready[rows, :] = scaled.astype(BF16)
            return carry

        lax.fori_loop(0, height // tile, body, 0)
        out_copy(chunk).start()
    for chunk in range(chunks):
        out_copy(chunk).wait()


def layer_norm(blocks, places, gain, shift):
    rows = blocks[0].shape[0]
    features = gain.shape[0]
    count = len(blocks)
    chunks = 4
    vmem = pl.BlockSpec(memory_space=pltpu.VMEM)
    return pl.pallas_call(
        functools.partial(norm_kernel, count, chunks),
        out_shape=jax.ShapeDtypeStruct((rows, features), BF16),
        in_specs=[pl.BlockSpec(memory_space=pltpu.SMEM)]
        + [pl.BlockSpec(memory_space=pl.ANY)] * count
        + [vmem] * 2,
        out_specs=pl.BlockSpec(memory_space=pl.ANY),
        scratch_shapes=[
            pltpu.VMEM((rows, features), BF16),
            pltpu.VMEM((rows, features), BF16),
            pltpu.SemaphoreType.DMA((count, chunks)),
            pltpu.SemaphoreType.DMA((chunks,)),
        ],
        compiler_params=params(),
        cost_estimate=LIGHT,
        name="norm",
    )(places, *blocks, gain[None, :], shift[None, :])


def shard_layout(lengths, ordering, row_count):
    group_count = lengths.shape[0]
    labels = jnp.arange(group_count, dtype=jnp.int32)
    chosen = (ordering[:, None] == labels[None, :]).astype(jnp.int32)
    ranking = jnp.sum(labels[:, None] * chosen, axis=0)
    earlier = (ranking[None, :] < ranking[:, None]).astype(jnp.int32)
    starts = jnp.sum(earlier * lengths[None, :], axis=1)
    places = jnp.arange(row_count, dtype=jnp.int32)
    member = (
        (places[:, None] >= starts[None, :]) & (places[:, None] < (starts + lengths)[None, :])
    ).astype(jnp.int32)
    row_start = jnp.sum(member * starts[None, :], axis=1)
    return starts, row_start, places - row_start


def rotary_tables(positions):
    rot = HS // 4
    half = rot // 2
    inverse = 10000.0 ** (-(jnp.arange(half, dtype=F32) * 2.0) / rot)
    lanes = jnp.concatenate([inverse, inverse, jnp.zeros((HS - rot,), F32)])
    lanes = jnp.tile(lanes, GROUP_HEADS)
    angles = positions.astype(F32)[:, None] * lanes[None, :]
    return [jnp.cos(angles), jnp.sin(angles)]


def part_kernel(bundles, wide, *outs):
    columns = wide[...]
    for c in range(3):
        merged = [None] * (GW // 128)
        for k, (first, width) in enumerate(windows()):
            source = 2 * HS * k + HS * c + first
            cut = columns[:, source : source + width]
            mask = head_mask(k, first, cut.shape)
            for w in range(width // 128):
                at = first // 128 + w
                lanes = slice(w * 128, w * 128 + 128)
                if merged[at] is None:
                    merged[at] = cut[:, lanes]
                else:
                    merged[at] = jnp.where(mask[:, lanes], cut[:, lanes], merged[at])
        for out, (begin, end) in zip(outs, bundles):
            for at, piece in enumerate(merged):
                first = c * GW + at * 128
                if begin <= first < end:
                    out[:, first - begin : first - begin + 128] = piece


def part_by_part(weight, group, bundles):
    rows = weight.shape[0]
    tile = 128
    return pl.pallas_call(
        functools.partial(part_kernel, bundles),
        out_shape=[jax.ShapeDtypeStruct((rows, end - begin), BF16) for begin, end in bundles],
        grid=(rows // tile,),
        in_specs=[pl.BlockSpec((tile, 3 * GW), lambda i: (i, group))],
        out_specs=[pl.BlockSpec((tile, end - begin), lambda i: (i, 0)) for begin, end in bundles],
        compiler_params=params(),
        cost_estimate=LIGHT,
        name="parts",
    )(weight)


def qkv_kernel(pieces, bundle, order, normed, *refs):
    count = 1 + max(part[0] for piece in pieces for part in piece)
    weights = refs[:count]
    bias, cosine, sine = refs[count : count + 3]
    outs = refs[count + 3 : count + 3 + len(bundle)]
    total, held_rows, held_weights, row_sems, weight_sems = refs[count + 3 + len(bundle) :]
    depth = weights[0].shape[0]

    def row_copy(j):
        lanes = pl.ds(pl.multiple_of(order[j] * depth, 128), depth)
        return pltpu.make_async_copy(
            normed.at[:, lanes], held_rows.at[:, pl.ds(j * depth, depth)], row_sems.at[j]
        )

    def weight_copies(j):
        found, at = [], 0
        for n, (source, first, width) in enumerate(pieces[j]):
            found.append(
                pltpu.make_async_copy(
                    weights[source].at[:, pl.ds(first, width)],
                    held_weights.at[pl.ds(j * depth, depth), pl.ds(at, width)],
                    weight_sems.at[j, n],
                )
            )
            at += width
        return found

    for j in range(len(pieces)):
        row_copy(j).start()
        for one in weight_copies(j):
            one.start()
    halves = 2
    each = len(pieces) // halves
    height = total.shape[0] // 2
    for n in range(halves):
        for j in range(n * each, (n + 1) * each):
            row_copy(j).wait()
            for one in weight_copies(j):
                one.wait()
        inner = slice(n * each * depth, (n + 1) * each * depth)
        for m in range(2):
            rows = slice(m * height, (m + 1) * height)
            part = jnp.dot(
                held_rows[rows, inner], held_weights[inner, :], preferred_element_type=F32
            )
            if n == 0:
                total[rows, :] = part
            else:
                total[rows, :] += part

    tile = 64

    def body(i, carry):
        rows = pl.ds(pl.multiple_of(i * tile, tile), tile)
        for spot, c in enumerate(bundle):
            lanes = slice(spot * GW, (spot + 1) * GW)
            x = total[rows, lanes] + bias[:, lanes]
            if c < 2:
                lane = lax.broadcasted_iota(jnp.int32, x.shape, 1) % HS
                turned = jnp.where(
                    lane < HS // 8,
                    -pltpu.roll(x, GW - HS // 8, 1),
                    pltpu.roll(x, HS // 8, 1),
                )
                x = x * cosine[rows, :] + turned * sine[rows, :]
            outs[spot][rows, :] = x.astype(BF16)
        return carry

    lax.fori_loop(0, total.shape[0] // tile, body, 0)


def project(normed, pieces, order, bias, tables, bundle):
    rows, features = normed.shape
    arrays, plan = [], []
    for piece in pieces:
        parts = []
        for array, first, width in piece:
            arrays.append(array)
            parts.append((len(arrays) - 1, first, width))
        plan.append(parts)
    depth = arrays[0].shape[0]
    columns = len(bundle) * GW
    out = jax.ShapeDtypeStruct((rows, GW), BF16)
    vmem = pl.BlockSpec(memory_space=pltpu.VMEM)
    anywhere = pl.BlockSpec(memory_space=pl.ANY)
    return pl.pallas_call(
        functools.partial(qkv_kernel, plan, bundle),
        out_shape=[out] * len(bundle),
        in_specs=[pl.BlockSpec(memory_space=pltpu.SMEM)]
        + [anywhere] * (len(arrays) + 1)
        + [vmem] * 3,
        out_specs=[vmem] * len(bundle),
        scratch_shapes=[
            pltpu.VMEM((rows, columns), F32),
            pltpu.VMEM((rows, features), BF16),
            pltpu.VMEM((features, columns), BF16),
            pltpu.SemaphoreType.DMA((len(plan),)),
            pltpu.SemaphoreType.DMA((len(plan), max(len(parts) for parts in plan))),
        ],
        compiler_params=params(),
        cost_estimate=LIGHT,
        name="project",
    )(order, normed, *arrays, bias, *tables)


def prefix_kernel(blocks, starts, lengths, *refs):
    queries = refs[:blocks]
    k_own, k_other, v_own, v_other = refs[blocks : blocks + 4]
    outs = refs[blocks + 4 : 2 * blocks + 4]
    totals = refs[2 * blocks + 4]
    slot = pl.program_id(0)
    slots = pl.num_programs(0)
    rows = queries[0].shape[0]

    @pl.when(slot == 0)
    def _():
        totals[...] = jnp.zeros_like(totals)

    reach = min(256, rows)
    begin, size, offset, window = [], [], [], []
    count = 0
    for b in range(blocks):
        begin.append(starts[slot * blocks + b])
        first_row = jnp.minimum(lax.div(begin[b], 16) * 16, rows - reach)
        window.append(pl.multiple_of(first_row, 16))
        size.append(lengths[slot * blocks + b])
        offset.append(count)
        count = count + size[b]

    def serve(keys, values):
        def tile(base, height):
            down = lax.broadcasted_iota(jnp.int32, (height, 1), 0) + base
            across = lax.broadcasted_iota(jnp.int32, (1, height), 1) + base

            def sources(place, b):
                within = place - offset[b]
                return jnp.where(
                    (within >= 0) & (within < size[b]), within + begin[b] - window[b], -1
                )

            picked = None
            for b in range(blocks):
                spread = lax.broadcasted_iota(jnp.int32, (height, reach), 1)
                one_hot = jnp.where(spread == sources(down, b), 1.0, 0.0).astype(BF16)
                part = jnp.dot(
                    one_hot, queries[b][pl.ds(window[b], reach), :], preferred_element_type=F32
                )
                picked = part if picked is None else picked + part
            picked = picked.astype(BF16)
            merged = [jnp.zeros((height, 128), F32) for _ in range(GW // 128)]
            extra = jnp.zeros((height, PACK), F32)
            place = lax.broadcasted_iota(jnp.int32, (height, PACK), 1)
            for k, (first, width) in enumerate(windows()):
                lanes = slice(first, first + width)
                mask = head_mask(k, first, (height, width))
                query = jnp.where(mask, picked[:, lanes], jnp.zeros((), BF16))
                scores = lax.dot_general(
                    query,
                    keys[0, :, lanes],
                    (((1,), (1,)), ((), ())),
                    preferred_element_type=F32,
                )
                peak = jnp.max(scores, axis=1, keepdims=True)
                weights = jnp.exp2((scores - peak) * (SCALE * LOG2E))
                mass = jnp.sum(weights, axis=1, keepdims=True)
                blended = jnp.dot(
                    weights.astype(BF16), values[0, :, lanes], preferred_element_type=F32
                )
                blended = blended * (1.0 / mass)
                for w in range(width // 128):
                    at = first // 128 + w
                    cut = slice(w * 128, w * 128 + 128)
                    merged[at] = jnp.where(mask[:, cut], blended[:, cut], merged[at])
                level = peak * SCALE + jnp.log(mass)
                high = level.astype(BF16).astype(F32)
                middle = (level - high).astype(BF16).astype(F32)
                low = level - high - middle
                for n, term in enumerate((high, middle, low)):
                    extra = jnp.where(place == 32 * n + k, term, extra)
            packed = jnp.concatenate(merged + [extra], axis=1).astype(BF16)
            for b in range(blocks):
                spread = lax.broadcasted_iota(jnp.int32, (reach, height), 0)
                one_hot = jnp.where(spread == sources(across, b), 1.0, 0.0).astype(BF16)
                totals[b, pl.ds(window[b], reach), :] += jnp.dot(
                    one_hot, packed, preferred_element_type=F32
                )

        large = 256
        small = 128
        full = lax.div(count, large)
        rest = count - full * large

        def body(j, carry):
            tile(j * large, large)
            return carry

        lax.fori_loop(0, full + jnp.where(rest > small, 1, 0), body, 0)

        @pl.when((rest > 0) & (rest <= small))
        def _():
            tile(full * large, small)

    half = slots // 2

    @pl.when(slot < half)
    def _():
        serve(k_own, v_own)

    @pl.when(slot >= half)
    def _():
        serve(k_other, v_other)

    @pl.when(slot == slots - 1)
    def _():
        for b in range(blocks):
            outs[b][...] = totals[b].astype(BF16)


def prefix_attention(group, queries, cache, starts, lengths):
    blocks = len(queries)
    rows = queries[0].shape[0]
    held, length, _ = cache[0].shape
    width = GW + PACK
    whole = lambda s, starts, lengths: (0, 0)
    own = lambda s, starts, lengths: (jnp.minimum(s, held - 1), 0, group)
    other = lambda s, starts, lengths: (jnp.maximum(s - held, 0), 0, group)
    block = (1, length, GW)
    return pl.pallas_call(
        functools.partial(prefix_kernel, blocks),
        out_shape=[jax.ShapeDtypeStruct((rows, width), BF16)] * blocks,
        grid_spec=pltpu.PrefetchScalarGridSpec(
            num_scalar_prefetch=2,
            grid=(2 * held,),
            in_specs=[pl.BlockSpec((rows, GW), whole)] * blocks
            + [pl.BlockSpec(block, own), pl.BlockSpec(block, other)] * 2,
            out_specs=[pl.BlockSpec((rows, width), whole)] * blocks,
            scratch_shapes=[pltpu.VMEM((blocks, rows, width), F32)],
        ),
        compiler_params=params(),
        cost_estimate=LIGHT,
        name="prefix",
    )(starts, lengths, *queries, *cache)


def suffix_kernel(row_start, queries, keys, values, out, levels):
    rows = queries.shape[0]
    tile = 128
    for i in range(rows // tile):
        at = slice(i * tile, (i + 1) * tile)
        wide = (i + 1) * tile
        row = lax.broadcasted_iota(jnp.int32, (tile, wide), 0) + i * tile
        column = lax.broadcasted_iota(jnp.int32, (tile, wide), 1)
        allowed = (column <= row) & (column >= row_start[at, :])
        merged = [jnp.zeros((tile, 128), F32) for _ in range(GW // 128)]
        level_row = jnp.zeros((tile, PACK), F32)
        place = lax.broadcasted_iota(jnp.int32, (tile, PACK), 1)
        for k, (first, width) in enumerate(windows()):
            lanes = slice(first, first + width)
            mask = head_mask(k, first, (tile, width))
            query = jnp.where(mask, queries[at, lanes], jnp.zeros((), BF16))
            scores = lax.dot_general(
                query,
                keys[:wide, lanes],
                (((1,), (1,)), ((), ())),
                preferred_element_type=F32,
            )
            scores = jnp.where(allowed, scores, -jnp.inf)
            peak = jnp.max(scores, axis=1, keepdims=True)
            weights = jnp.exp2((scores - peak) * (SCALE * LOG2E))
            mass = jnp.sum(weights, axis=1, keepdims=True)
            blended = jnp.dot(
                weights.astype(BF16), values[:wide, lanes], preferred_element_type=F32
            )
            blended = blended * (1.0 / mass)
            for w in range(width // 128):
                spot = first // 128 + w
                cut = slice(w * 128, w * 128 + 128)
                merged[spot] = jnp.where(mask[:, cut], blended[:, cut], merged[spot])
            level_row = jnp.where(place == k, peak * SCALE + jnp.log(mass), level_row)
        out[at, :] = jnp.concatenate(merged, axis=1)
        levels[at, :] = level_row


def suffix_attention(row_start, queries, keys, values):
    rows = queries.shape[0]
    return pl.pallas_call(
        suffix_kernel,
        out_shape=(
            jax.ShapeDtypeStruct((rows, GW), F32),
            jax.ShapeDtypeStruct((rows, PACK), F32),
        ),
        compiler_params=params(),
        cost_estimate=LIGHT,
        name="suffix",
    )(row_start, queries, keys, values)


def merge_kernel(blocks, *refs):
    parts = refs[:blocks]
    suffix, levels, out = refs[blocks:]
    rows = suffix.shape[0]
    tile = 128
    for i in range(rows // tile):
        at = slice(i * tile, (i + 1) * tile)
        prefix = parts[0][at, :].astype(F32)
        for b in range(1, blocks):
            prefix = prefix + parts[b][at, :].astype(F32)
        terms = prefix[:, GW:]
        pre = terms + pltpu.roll(terms, PACK - 32, 1) + pltpu.roll(terms, PACK - 64, 1)
        suf = levels[at, :]
        top = jnp.maximum(pre, suf)
        pre = jnp.exp(pre - top)
        suf = jnp.exp(suf - top)
        shares = pre / (pre + suf)
        spread = jnp.zeros((tile, GW), F32)
        for k in range(GROUP_HEADS):
            spread = jnp.where(head_mask(k, 0, (tile, GW)), shares[:, k : k + 1], spread)
        out[at, :] = (spread * prefix[:, :GW] + (1.0 - spread) * suffix[at, :]).astype(BF16)


def merge(parts, suffix, levels):
    rows = suffix.shape[0]
    return pl.pallas_call(
        functools.partial(merge_kernel, len(parts)),
        out_shape=jax.ShapeDtypeStruct((rows, GW), BF16),
        compiler_params=params(),
        cost_estimate=LIGHT,
        name="merge",
    )(*parts, suffix, levels)


def output_kernel(groups, lines, place, *refs):
    attention = refs[: 2 * groups]
    own, landed, crossed, out, held, joined, sems = refs[2 * groups :]
    at = pl.program_id(0)
    rows, share = out.shape[1:]
    depth = own.shape[0]
    half = lines // 2
    side, core = place[0], place[1]

    def own_copy(a):
        lanes = pl.ds(pl.multiple_of((2 * a + side) * share, 128), share)
        return pltpu.make_async_copy(
            own.at[:, lanes], held.at[a, pl.ds(0, depth)], sems.at[2 * a]
        )

    def other_copy(a):
        source = landed if a < half else crossed
        spot = lax.rem(a + core * half, lines)
        lanes = pl.ds((a % half) * share, share)
        return pltpu.make_async_copy(
            source.at[:, lanes], held.at[spot, pl.ds(depth, depth)], sems.at[2 * a + 1]
        )

    @pl.when(at == 0)
    def _():
        for a in range(lines):
            own_copy(a).start()
            other_copy(a).start()
        for n in range(2 * groups):
            joined[:, n * GW : (n + 1) * GW] = attention[n][...]

    own_copy(at).wait()
    sent = lax.rem(at + core * half, lines)
    pltpu.make_async_copy(
        landed.at[:, pl.ds(0, share)],
        held.at[at, pl.ds(depth, depth)],
        sems.at[2 * sent + 1],
    ).wait()
    out[0] = jnp.dot(joined[...], held[at], preferred_element_type=F32)


def output_projection(place, attention, own, landed, crossed, lines):
    rows = attention[0].shape[0]
    depth, features = own.shape
    share = features // (2 * lines)
    vmem = pl.BlockSpec((rows, GW), lambda a, place: (0, 0))
    anywhere = pl.BlockSpec(memory_space=pl.ANY)
    return pl.pallas_call(
        functools.partial(output_kernel, len(attention) // 2, lines),
        out_shape=jax.ShapeDtypeStruct((lines, rows, share), F32),
        grid_spec=pltpu.PrefetchScalarGridSpec(
            num_scalar_prefetch=1,
            grid=(lines,),
            in_specs=[vmem] * len(attention) + [anywhere] * 3,
            out_specs=pl.BlockSpec((1, rows, share), lambda a, place: (a, 0, 0)),
            scratch_shapes=[
                pltpu.VMEM((lines, 2 * depth, share), BF16),
                pltpu.VMEM((rows, 2 * depth), BF16),
                pltpu.SemaphoreType.DMA((2 * lines,)),
            ],
        ),
        compiler_params=params(),
        cost_estimate=LIGHT,
        name="output",
    )(place, *attention, own, landed, crossed)


def on_device(
    hidden_states,
    norm_gain,
    norm_bias,
    qkv_weight,
    qkv_bias,
    dense_weight,
    dense_bias,
    prefix_keys,
    prefix_values,
    suffix_len,
    request_order,
    group_slot,
):
    rows, share = hidden_states.shape
    held, prefix_length, local_width = prefix_keys.shape
    groups_local = local_width // GW
    tok_size = lax.axis_size("tok")
    head_size = lax.axis_size("head")
    chips = tok_size // 2
    lines = head_size // 2
    group_count = held * tok_size
    tok = lax.axis_index("tok")
    head = lax.axis_index("head")
    core, chip = tok % 2, tok // 2
    side, line = head % 2, head // 2

    def to_core(x):
        return lax.ppermute(x, "tok", [(t, t ^ 1) for t in range(tok_size)])

    def to_chip(x, shift):
        return lax.ppermute(
            x,
            "tok",
            [(t, (t // 2 + shift) % chips * 2 + t % 2) for t in range(tok_size)],
        )

    def to_side(x):
        return lax.ppermute(x, "head", [(h, h ^ 1) for h in range(head_size)])

    def after(x, *others):
        return lax.optimization_barrier((x, others))[0]

    layout = jnp.stack([suffix_len[0], request_order[0]])
    layouts = [layout] + [to_chip(layout, shift) for shift in range(1, chips)]
    (first,) = part_by_part(qkv_weight, 0, ((0, 3 * GW),))
    first, layouts = lax.optimization_barrier((first, layouts))

    last = lines - 1

    def to_side_from(x, lowest, highest):
        return lax.ppermute(
            x, "head", [(h, h ^ 1) for h in range(head_size) if lowest <= h // 2 <= highest]
        )

    columns = 3 * GW
    source, _ = lax.optimization_barrier((qkv_weight, layouts))
    cuts = ((0, columns), (0, 2 * GW), (2 * GW, columns))
    later = [part_by_part(source, g, cuts) for g in range(1, groups_local)]
    across = to_side(hidden_states)
    blocks = [hidden_states, across]
    places = [head, head ^ 1]
    arriving = [to_chip(first, shift) for shift in range(1, chips)]
    up = down = hidden_states
    settled = across
    for step in range(last):
        if step > 0:
            up, down, settled, first, later = lax.optimization_barrier(
                (up, down, settled, first, later)
            )
            blocks[1 if step == 1 else tied] = settled
        up = lax.ppermute(
            up, "head", [(h, h + 2) for h in range(head_size) if step <= h // 2 < last]
        )
        down = lax.ppermute(
            down, "head", [(h, h - 2) for h in range(head_size) if 0 < h // 2 <= last - step]
        )
        from_below, from_above = line >= step + 1, line + 1 + step <= last
        below, above = line - 1 - step, line + 1 + step
        blocks += [up, down]
        places += [
            jnp.where(from_below, 2 * below + side, -1),
            jnp.where(from_above, 2 * above + side, -1),
        ]
        marked = len(blocks)
        if 2 * step + 1 < last:
            blocks += [to_side_from(up, step + 1, last), to_side_from(down, 0, last - 1 - step)]
            places += [
                jnp.where(from_below, 2 * below + 1 - side, -1),
                jnp.where(from_above, 2 * above + 1 - side, -1),
            ]
        else:
            here = after(jnp.where(from_below, up, down), blocks[-3])
            lines_with = [h for h in range(head_size) if h // 2 >= step + 1 or h // 2 <= last - 1 - step]
            blocks.append(lax.ppermute(here, "head", [(h, h ^ 1) for h in lines_with]))
            there = jnp.where(from_below, below, above)
            places.append(jnp.where(from_below | from_above, 2 * there + 1 - side, -1))
        if step > 0:
            tied, settled = previous, blocks[previous]
        previous = marked
    places = jnp.stack(places).astype(jnp.int32)

    order = [tok, tok ^ 1]
    for shift in range(1, chips):
        source = (chip + chips - shift) % chips * 2 + core
        order += [source, source ^ 1]
    order = jnp.stack(order).astype(jnp.int32)
    lengths = suffix_len[0]
    starts, row_start, within = shard_layout(lengths, request_order[0], rows)
    labels = jnp.arange(group_count, dtype=jnp.int32)
    slot_match = (group_slot[:, None] == labels[None, :]).astype(jnp.int32)

    def served_spans(one):
        firsts = shard_layout(one[0], one[1], rows)[0]
        spans = jnp.stack(
            [
                jnp.sum(firsts[:, None] * slot_match, axis=0),
                jnp.sum(one[0][:, None] * slot_match, axis=0),
            ]
        )
        return jnp.concatenate(
            [
                lax.dynamic_slice(spans, (0, tok * held), (2, held)),
                lax.dynamic_slice(spans, (0, (tok ^ 1) * held), (2, held)),
            ],
            axis=1,
        )

    served = jnp.stack([served_spans(one) for one in layouts], axis=2)
    tables = rotary_tables(prefix_length + within)
    bias = qkv_bias.astype(F32).reshape(groups_local, GROUP_HEADS, 3, HS)
    bias = jnp.transpose(bias, (0, 2, 1, 3)).reshape(groups_local, 1, columns)
    bias = [
        [bias[g]] if g == 0 else [bias[g][:, : 2 * GW], bias[g][:, 2 * GW :]]
        for g in range(groups_local)
    ]

    half = lines // 2
    outgoing = jnp.concatenate(
        [
            lax.dynamic_slice(
                dense_weight,
                (0, (2 * (core * half + a) + 1 - side) * share),
                (dense_weight.shape[0], share),
            )
            for a in range(half)
        ],
        axis=1,
    )
    ready = (
        served[0].reshape(-1),
        served[1].reshape(-1),
        tables,
        bias,
        order,
        row_start[:, None],
        jnp.stack([side, core]).astype(jnp.int32),
        outgoing,
        later,
        places,
        blocks,
    )
    arriving, ready = lax.optimization_barrier((arriving, ready))
    span_start, span_length, tables, bias, order, row_start, place, outgoing, later = ready[:9]
    places, blocks = ready[9:]

    def send(mine):
        return [to_chip(mine, shift) for shift in range(1, chips)]

    def exchange(queries):
        return [queries] + [to_chip(queries, shift) for shift in range(1, chips)]

    def pieces_of(own, arrived, first, width):
        pieces = [[(one, first, width)] for one in own]
        for n in range(chips - 1):
            for which in range(2):
                pieces.append([(part[n][which], 0, part[n][which].shape[1]) for part in arrived])
        return pieces

    def crossing(arrived):
        return [(one, to_core(one)) for one in arrived]

    coming = [send(after(one[1], arriving)) for one in later]
    first_pieces = pieces_of((first, to_core(first)), [crossing(arriving)], 0, columns)
    normed = layer_norm(blocks, places, norm_gain, norm_bias)
    landed = to_side(after(outgoing, normed))
    cache = [prefix_keys, to_core(after(prefix_keys, arriving))]
    cache += [prefix_values, to_core(after(prefix_values, arriving))]
    own = [(one[0], to_core(after(one[0], normed))) for one in later]
    heads = [project(normed, first_pieces, order, bias[0][0], tables, (0, 1, 2))]
    asked = [exchange(heads[0][0])]
    settled = heads[0]
    values_coming = []
    for g in range(1, groups_local):
        arrived = crossing(after(coming[g - 1], settled))
        pair = project(
            normed, pieces_of(own[g - 1], [arrived], 0, 2 * GW), order, bias[g][0], tables, (0, 1)
        )
        heads.append(pair)
        asked.append(exchange(pair[0]))
        settled = pair
    suffixes = [suffix_attention(after(row_start, settled), *heads[0])]
    values_coming = [
        send(after(one[2], asked[0][1:], asked[-1][1:], suffixes[0])) for one in later
    ]
    asked[0] = after(asked[0], suffixes[0])
    returned = []
    for g in range(groups_local):
        if g > 0:
            asked[g] = after(asked[g], answers)
        answers = prefix_attention(g, asked[g], cache, span_start, span_length)
        returned.append([answers[0]] + [to_chip(answers[s], chips - s) for s in range(1, chips)])
    crossed = to_core(after(landed, answers))
    attention_own, attention_side = [], []
    for g in range(1, groups_local):
        arrived = crossing(after(values_coming[g - 1], answers))
        (values,) = project(
            normed, pieces_of(own[g - 1], [arrived], 2 * GW, GW), order, bias[g][1], tables, (2,)
        )
        parts_first = after(returned[g - 1], values)
        attention_own.append(merge(parts_first, *suffixes[g - 1]))
        attention_side.append(to_side(attention_own[-1]))
        suffixes.append(
            suffix_attention(after(row_start, attention_own[-1]), heads[g][0], heads[g][1], values)
        )
    attention_own.append(merge(after(returned[-1], attention_side), *suffixes[-1]))
    attention_side.append(to_side(attention_own[-1]))
    partial = output_projection(
        place, attention_own + attention_side, dense_weight, landed, crossed, lines
    )

    cuts = 2
    height = rows // cuts

    def chunk(place, cut):
        place = jnp.clip(place, 0, last)
        return lax.dynamic_slice(
            partial, (place, cut * height, 0), (1, height, share)
        ).reshape(height, share)

    passing = [None] * cuts
    for step in range(last):
        up_pairs = [(h, h + 2) for h in range(head_size) if h // 2 <= step and h // 2 < last]
        down_pairs = [(h, h - 2) for h in range(head_size) if last - h // 2 <= step and h // 2 > 0]
        for cut in range(cuts):
            up = chunk(last + line - step, cut)
            down = chunk(line - last + step, cut)
            if passing[cut] is not None:
                if cut > 0:
                    passing[cut], sent = lax.optimization_barrier((passing[cut], sent))
                up = up + passing[cut][0].astype(F32)
                down = down + passing[cut][1].astype(F32)
            up, down = lax.optimization_barrier((up.astype(BF16), down.astype(BF16)))
            sent = up
            passing[cut] = lax.optimization_barrier(
                (lax.ppermute(up, "head", up_pairs), lax.ppermute(down, "head", down_pairs))
            )
    base = hidden_states.astype(F32) + dense_bias.astype(F32)
    done = [
        base[cut * height : (cut + 1) * height]
        + (chunk(line, cut) + passing[cut][0].astype(F32) + passing[cut][1].astype(F32))
        for cut in range(cuts)
    ]
    return jnp.concatenate(done, axis=0).astype(BF16)


def solution(mesh):
    placed = (
        P("tok", "head"),
        P(),
        P(),
        P("tok", "head"),
        P("head"),
        P("head", None),
        P("head"),
        P("tok", None, "head"),
        P("tok", None, "head"),
        P("tok", None),
        P("tok", None),
        P(),
    )
    return jax.shard_map(
        on_device, mesh=mesh, in_specs=placed, out_specs=P("tok", "head"), check_vma=False
    )
```

```python
import functools
import math

import jax
import jax.numpy as jnp
from jax import lax
from jax.experimental import pallas as pl
from jax.experimental.pallas import tpu as pltpu
from jax.sharding import PartitionSpec as P

HS = 96
GROUP_HEADS = 4
GW = GROUP_HEADS * HS
PACK = 128
F32 = jnp.float32
BF16 = jnp.bfloat16
VMEM_LIMIT = 56 * 1024 * 1024
SCALE = 1.0 / math.sqrt(HS)
LOG2E = math.log2(math.e)
LIGHT = pl.CostEstimate(flops=1000, bytes_accessed=1000, transcendentals=0)


def windows():
    found = []
    for k in range(GROUP_HEADS):
        first = k * HS // 128 * 128
        last = -(-(k * HS + HS) // 128) * 128
        found.append((first, last - first))
    return found


def head_mask(k, first, shape):
    lane = lax.broadcasted_iota(jnp.int32, shape, 1) + first
    return (lane >= k * HS) & (lane < (k + 1) * HS)


def params():
    return pltpu.CompilerParams(vmem_limit_bytes=VMEM_LIMIT)


def norm_kernel(count, chunks, places, *refs):
    blocks = refs[:count]
    gain, shift, out, held, ready, sems, out_sems = refs[count:]
    share = blocks[0].shape[1]
    height = held.shape[0] // chunks
    tile = 32

    def copy(j, chunk):
        lanes = pl.ds(pl.multiple_of(places[j] * share, 128), share)
        rows = pl.ds(chunk * height, height)
        return pltpu.make_async_copy(
            blocks[j].at[rows, :], held.at[rows, lanes], sems.at[j, chunk]
        )

    def out_copy(chunk):
        rows = pl.ds(chunk * height, height)
        return pltpu.make_async_copy(ready.at[rows, :], out.at[rows, :], out_sems.at[chunk])

    for chunk in range(chunks):
        for j in range(count):

            @pl.when(places[j] >= 0)
            def _(j=j, chunk=chunk):
                copy(j, chunk).start()

    for chunk in range(chunks):
        for j in range(count):

            @pl.when(places[j] >= 0)
            def _(j=j, chunk=chunk):
                copy(j, chunk).wait()

        def body(i, carry, chunk=chunk):
            rows = pl.ds(pl.multiple_of(chunk * height + i * tile, tile), tile)
            widened = held[rows, :].astype(F32)
            center = jnp.mean(widened, axis=-1, keepdims=True)
            moved = widened - center
            spread = jnp.mean(jnp.square(moved), axis=-1, keepdims=True)
            scaled = moved * lax.rsqrt(spread + 1e-05) * gain[...] + shift[...]
            ready[rows, :] = scaled.astype(BF16)
            return carry

        lax.fori_loop(0, height // tile, body, 0)
        out_copy(chunk).start()
    for chunk in range(chunks):
        out_copy(chunk).wait()


def layer_norm(blocks, places, gain, shift):
    rows = blocks[0].shape[0]
    features = gain.shape[0]
    count = len(blocks)
    chunks = 4
    vmem = pl.BlockSpec(memory_space=pltpu.VMEM)
    return pl.pallas_call(
        functools.partial(norm_kernel, count, chunks),
        out_shape=jax.ShapeDtypeStruct((rows, features), BF16),
        in_specs=[pl.BlockSpec(memory_space=pltpu.SMEM)]
        + [pl.BlockSpec(memory_space=pl.ANY)] * count
        + [vmem] * 2,
        out_specs=pl.BlockSpec(memory_space=pl.ANY),
        scratch_shapes=[
            pltpu.VMEM((rows, features), BF16),
            pltpu.VMEM((rows, features), BF16),
            pltpu.SemaphoreType.DMA((count, chunks)),
            pltpu.SemaphoreType.DMA((chunks,)),
        ],
        compiler_params=params(),
        cost_estimate=LIGHT,
        name="norm",
    )(places, *blocks, gain[None, :], shift[None, :])


def shard_layout(lengths, ordering, row_count):
    group_count = lengths.shape[0]
    labels = jnp.arange(group_count, dtype=jnp.int32)
    chosen = (ordering[:, None] == labels[None, :]).astype(jnp.int32)
    ranking = jnp.sum(labels[:, None] * chosen, axis=0)
    earlier = (ranking[None, :] < ranking[:, None]).astype(jnp.int32)
    starts = jnp.sum(earlier * lengths[None, :], axis=1)
    places = jnp.arange(row_count, dtype=jnp.int32)
    member = (
        (places[:, None] >= starts[None, :]) & (places[:, None] < (starts + lengths)[None, :])
    ).astype(jnp.int32)
    row_start = jnp.sum(member * starts[None, :], axis=1)
    return starts, row_start, places - row_start


def rotary_tables(positions):
    rot = HS // 4
    half = rot // 2
    inverse = 10000.0 ** (-(jnp.arange(half, dtype=F32) * 2.0) / rot)
    lanes = jnp.concatenate([inverse, inverse, jnp.zeros((HS - rot,), F32)])
    lanes = jnp.tile(lanes, GROUP_HEADS)
    angles = positions.astype(F32)[:, None] * lanes[None, :]
    return [jnp.cos(angles), jnp.sin(angles)]


def part_kernel(bundles, wide, *outs):
    columns = wide[...]
    for c in range(3):
        merged = [None] * (GW // 128)
        for k, (first, width) in enumerate(windows()):
            source = 2 * HS * k + HS * c + first
            cut = columns[:, source : source + width]
            mask = head_mask(k, first, cut.shape)
            for w in range(width // 128):
                at = first // 128 + w
                lanes = slice(w * 128, w * 128 + 128)
                if merged[at] is None:
                    merged[at] = cut[:, lanes]
                else:
                    merged[at] = jnp.where(mask[:, lanes], cut[:, lanes], merged[at])
        for out, (begin, end) in zip(outs, bundles):
            for at, piece in enumerate(merged):
                first = c * GW + at * 128
                if begin <= first < end:
                    out[:, first - begin : first - begin + 128] = piece


def part_by_part(weight, group, bundles):
    rows = weight.shape[0]
    tile = 128
    return pl.pallas_call(
        functools.partial(part_kernel, bundles),
        out_shape=[jax.ShapeDtypeStruct((rows, end - begin), BF16) for begin, end in bundles],
        grid=(rows // tile,),
        in_specs=[pl.BlockSpec((tile, 3 * GW), lambda i: (i, group))],
        out_specs=[pl.BlockSpec((tile, end - begin), lambda i: (i, 0)) for begin, end in bundles],
        compiler_params=params(),
        cost_estimate=LIGHT,
        name="parts",
    )(weight)


def qkv_kernel(pieces, bundle, order, normed, *refs):
    count = 1 + max(part[0] for piece in pieces for part in piece)
    weights = refs[:count]
    bias, cosine, sine = refs[count : count + 3]
    outs = refs[count + 3 : count + 3 + len(bundle)]
    total, held_rows, held_weights, row_sems, weight_sems = refs[count + 3 + len(bundle) :]
    depth = weights[0].shape[0]

    def row_copy(j):
        lanes = pl.ds(pl.multiple_of(order[j] * depth, 128), depth)
        return pltpu.make_async_copy(
            normed.at[:, lanes], held_rows.at[:, pl.ds(j * depth, depth)], row_sems.at[j]
        )

    def weight_copies(j):
        found, at = [], 0
        for n, (source, first, width) in enumerate(pieces[j]):
            found.append(
                pltpu.make_async_copy(
                    weights[source].at[:, pl.ds(first, width)],
                    held_weights.at[pl.ds(j * depth, depth), pl.ds(at, width)],
                    weight_sems.at[j, n],
                )
            )
            at += width
        return found

    for j in range(len(pieces)):
        row_copy(j).start()
        for one in weight_copies(j):
            one.start()
    halves = 2
    each = len(pieces) // halves
    height = total.shape[0] // 2
    for n in range(halves):
        for j in range(n * each, (n + 1) * each):
            row_copy(j).wait()
            for one in weight_copies(j):
                one.wait()
        inner = slice(n * each * depth, (n + 1) * each * depth)
        for m in range(2):
            rows = slice(m * height, (m + 1) * height)
            part = jnp.dot(
                held_rows[rows, inner], held_weights[inner, :], preferred_element_type=F32
            )
            if n == 0:
                total[rows, :] = part
            else:
                total[rows, :] += part

    tile = 64

    def body(i, carry):
        rows = pl.ds(pl.multiple_of(i * tile, tile), tile)
        for spot, c in enumerate(bundle):
            lanes = slice(spot * GW, (spot + 1) * GW)
            x = total[rows, lanes] + bias[:, lanes]
            if c < 2:
                lane = lax.broadcasted_iota(jnp.int32, x.shape, 1) % HS
                turned = jnp.where(
                    lane < HS // 8,
                    -pltpu.roll(x, GW - HS // 8, 1),
                    pltpu.roll(x, HS // 8, 1),
                )
                x = x * cosine[rows, :] + turned * sine[rows, :]
            outs[spot][rows, :] = x.astype(BF16)
        return carry

    lax.fori_loop(0, total.shape[0] // tile, body, 0)


def project(normed, pieces, order, bias, tables, bundle):
    rows, features = normed.shape
    arrays, plan = [], []
    for piece in pieces:
        parts = []
        for array, first, width in piece:
            arrays.append(array)
            parts.append((len(arrays) - 1, first, width))
        plan.append(parts)
    depth = arrays[0].shape[0]
    columns = len(bundle) * GW
    out = jax.ShapeDtypeStruct((rows, GW), BF16)
    vmem = pl.BlockSpec(memory_space=pltpu.VMEM)
    anywhere = pl.BlockSpec(memory_space=pl.ANY)
    return pl.pallas_call(
        functools.partial(qkv_kernel, plan, bundle),
        out_shape=[out] * len(bundle),
        in_specs=[pl.BlockSpec(memory_space=pltpu.SMEM)]
        + [anywhere] * (len(arrays) + 1)
        + [vmem] * 3,
        out_specs=[vmem] * len(bundle),
        scratch_shapes=[
            pltpu.VMEM((rows, columns), F32),
            pltpu.VMEM((rows, features), BF16),
            pltpu.VMEM((features, columns), BF16),
            pltpu.SemaphoreType.DMA((len(plan),)),
            pltpu.SemaphoreType.DMA((len(plan), max(len(parts) for parts in plan))),
        ],
        compiler_params=params(),
        cost_estimate=LIGHT,
        name="project",
    )(order, normed, *arrays, bias, *tables)


def prefix_kernel(blocks, starts, lengths, *refs):
    queries = refs[:blocks]
    k_own, k_other, v_own, v_other = refs[blocks : blocks + 4]
    outs = refs[blocks + 4 : 2 * blocks + 4]
    totals = refs[2 * blocks + 4]
    slot = pl.program_id(0)
    slots = pl.num_programs(0)
    rows = queries[0].shape[0]

    @pl.when(slot == 0)
    def _():
        totals[...] = jnp.zeros_like(totals)

    reach = min(256, rows)
    begin, size, offset, window = [], [], [], []
    count = 0
    for b in range(blocks):
        begin.append(starts[slot * blocks + b])
        first_row = jnp.minimum(lax.div(begin[b], 16) * 16, rows - reach)
        window.append(pl.multiple_of(first_row, 16))
        size.append(lengths[slot * blocks + b])
        offset.append(count)
        count = count + size[b]

    def serve(keys, values):
        def tile(base, height):
            down = lax.broadcasted_iota(jnp.int32, (height, 1), 0) + base
            across = lax.broadcasted_iota(jnp.int32, (1, height), 1) + base

            def sources(place, b):
                within = place - offset[b]
                return jnp.where(
                    (within >= 0) & (within < size[b]), within + begin[b] - window[b], -1
                )

            picked = None
            for b in range(blocks):
                spread = lax.broadcasted_iota(jnp.int32, (height, reach), 1)
                one_hot = jnp.where(spread == sources(down, b), 1.0, 0.0).astype(BF16)
                part = jnp.dot(
                    one_hot, queries[b][pl.ds(window[b], reach), :], preferred_element_type=F32
                )
                picked = part if picked is None else picked + part
            picked = picked.astype(BF16)
            merged = [jnp.zeros((height, 128), F32) for _ in range(GW // 128)]
            extra = jnp.zeros((height, PACK), F32)
            place = lax.broadcasted_iota(jnp.int32, (height, PACK), 1)
            for k, (first, width) in enumerate(windows()):
                lanes = slice(first, first + width)
                mask = head_mask(k, first, (height, width))
                query = jnp.where(mask, picked[:, lanes], jnp.zeros((), BF16))
                scores = lax.dot_general(
                    query,
                    keys[0, :, lanes],
                    (((1,), (1,)), ((), ())),
                    preferred_element_type=F32,
                )
                peak = jnp.max(scores, axis=1, keepdims=True)
                weights = jnp.exp2((scores - peak) * (SCALE * LOG2E))
                mass = jnp.sum(weights, axis=1, keepdims=True)
                blended = jnp.dot(
                    weights.astype(BF16), values[0, :, lanes], preferred_element_type=F32
                )
                blended = blended * (1.0 / mass)
                for w in range(width // 128):
                    at = first // 128 + w
                    cut = slice(w * 128, w * 128 + 128)
                    merged[at] = jnp.where(mask[:, cut], blended[:, cut], merged[at])
                level = peak * SCALE + jnp.log(mass)
                high = level.astype(BF16).astype(F32)
                middle = (level - high).astype(BF16).astype(F32)
                low = level - high - middle
                for n, term in enumerate((high, middle, low)):
                    extra = jnp.where(place == 32 * n + k, term, extra)
            packed = jnp.concatenate(merged + [extra], axis=1).astype(BF16)
            for b in range(blocks):
                spread = lax.broadcasted_iota(jnp.int32, (reach, height), 0)
                one_hot = jnp.where(spread == sources(across, b), 1.0, 0.0).astype(BF16)
                totals[b, pl.ds(window[b], reach), :] += jnp.dot(
                    one_hot, packed, preferred_element_type=F32
                )

        large = 256
        small = 128
        full = lax.div(count, large)
        rest = count - full * large

        def body(j, carry):
            tile(j * large, large)
            return carry

        lax.fori_loop(0, full + jnp.where(rest > small, 1, 0), body, 0)

        @pl.when((rest > 0) & (rest <= small))
        def _():
            tile(full * large, small)

    half = slots // 2

    @pl.when(slot < half)
    def _():
        serve(k_own, v_own)

    @pl.when(slot >= half)
    def _():
        serve(k_other, v_other)

    @pl.when(slot == slots - 1)
    def _():
        for b in range(blocks):
            outs[b][...] = totals[b].astype(BF16)


def prefix_attention(group, queries, cache, starts, lengths):
    blocks = len(queries)
    rows = queries[0].shape[0]
    held, length, _ = cache[0].shape
    width = GW + PACK
    whole = lambda s, starts, lengths: (0, 0)
    own = lambda s, starts, lengths: (jnp.minimum(s, held - 1), 0, group)
    other = lambda s, starts, lengths: (jnp.maximum(s - held, 0), 0, group)
    block = (1, length, GW)
    return pl.pallas_call(
        functools.partial(prefix_kernel, blocks),
        out_shape=[jax.ShapeDtypeStruct((rows, width), BF16)] * blocks,
        grid_spec=pltpu.PrefetchScalarGridSpec(
            num_scalar_prefetch=2,
            grid=(2 * held,),
            in_specs=[pl.BlockSpec((rows, GW), whole)] * blocks
            + [pl.BlockSpec(block, own), pl.BlockSpec(block, other)] * 2,
            out_specs=[pl.BlockSpec((rows, width), whole)] * blocks,
            scratch_shapes=[pltpu.VMEM((blocks, rows, width), F32)],
        ),
        compiler_params=params(),
        cost_estimate=LIGHT,
        name="prefix",
    )(starts, lengths, *queries, *cache)


def suffix_kernel(row_start, queries, keys, values, out, levels):
    rows = queries.shape[0]
    tile = 128
    for i in range(rows // tile):
        at = slice(i * tile, (i + 1) * tile)
        wide = (i + 1) * tile
        row = lax.broadcasted_iota(jnp.int32, (tile, wide), 0) + i * tile
        column = lax.broadcasted_iota(jnp.int32, (tile, wide), 1)
        allowed = (column <= row) & (column >= row_start[at, :])
        merged = [jnp.zeros((tile, 128), F32) for _ in range(GW // 128)]
        level_row = jnp.zeros((tile, PACK), F32)
        place = lax.broadcasted_iota(jnp.int32, (tile, PACK), 1)
        for k, (first, width) in enumerate(windows()):
            lanes = slice(first, first + width)
            mask = head_mask(k, first, (tile, width))
            query = jnp.where(mask, queries[at, lanes], jnp.zeros((), BF16))
            scores = lax.dot_general(
                query,
                keys[:wide, lanes],
                (((1,), (1,)), ((), ())),
                preferred_element_type=F32,
            )
            scores = jnp.where(allowed, scores, -jnp.inf)
            peak = jnp.max(scores, axis=1, keepdims=True)
            weights = jnp.exp2((scores - peak) * (SCALE * LOG2E))
            mass = jnp.sum(weights, axis=1, keepdims=True)
            blended = jnp.dot(
                weights.astype(BF16), values[:wide, lanes], preferred_element_type=F32
            )
            blended = blended * (1.0 / mass)
            for w in range(width // 128):
                spot = first // 128 + w
                cut = slice(w * 128, w * 128 + 128)
                merged[spot] = jnp.where(mask[:, cut], blended[:, cut], merged[spot])
            level_row = jnp.where(place == k, peak * SCALE + jnp.log(mass), level_row)
        out[at, :] = jnp.concatenate(merged, axis=1)
        levels[at, :] = level_row


def suffix_attention(row_start, queries, keys, values):
    rows = queries.shape[0]
    return pl.pallas_call(
        suffix_kernel,
        out_shape=(
            jax.ShapeDtypeStruct((rows, GW), F32),
            jax.ShapeDtypeStruct((rows, PACK), F32),
        ),
        compiler_params=params(),
        cost_estimate=LIGHT,
        name="suffix",
    )(row_start, queries, keys, values)


def merge_kernel(blocks, *refs):
    parts = refs[:blocks]
    suffix, levels, out = refs[blocks:]
    rows = suffix.shape[0]
    tile = 128
    for i in range(rows // tile):
        at = slice(i * tile, (i + 1) * tile)
        prefix = parts[0][at, :].astype(F32)
        for b in range(1, blocks):
            prefix = prefix + parts[b][at, :].astype(F32)
        terms = prefix[:, GW:]
        pre = terms + pltpu.roll(terms, PACK - 32, 1) + pltpu.roll(terms, PACK - 64, 1)
        suf = levels[at, :]
        top = jnp.maximum(pre, suf)
        pre = jnp.exp(pre - top)
        suf = jnp.exp(suf - top)
        shares = pre / (pre + suf)
        spread = jnp.zeros((tile, GW), F32)
        for k in range(GROUP_HEADS):
            spread = jnp.where(head_mask(k, 0, (tile, GW)), shares[:, k : k + 1], spread)
        out[at, :] = (spread * prefix[:, :GW] + (1.0 - spread) * suffix[at, :]).astype(BF16)


def merge(parts, suffix, levels):
    rows = suffix.shape[0]
    return pl.pallas_call(
        functools.partial(merge_kernel, len(parts)),
        out_shape=jax.ShapeDtypeStruct((rows, GW), BF16),
        compiler_params=params(),
        cost_estimate=LIGHT,
        name="merge",
    )(*parts, suffix, levels)


def output_kernel(groups, lines, place, *refs):
    attention = refs[: 2 * groups]
    own, landed, crossed, out, held, joined, sems = refs[2 * groups :]
    at = pl.program_id(0)
    rows, share = out.shape[1:]
    depth = own.shape[0]
    half = lines // 2
    side, core = place[0], place[1]

    def own_copy(a):
        lanes = pl.ds(pl.multiple_of((2 * a + side) * share, 128), share)
        return pltpu.make_async_copy(
            own.at[:, lanes], held.at[a, pl.ds(0, depth)], sems.at[2 * a]
        )

    def other_copy(a):
        source = landed if a < half else crossed
        spot = lax.rem(a + core * half, lines)
        lanes = pl.ds((a % half) * share, share)
        return pltpu.make_async_copy(
            source.at[:, lanes], held.at[spot, pl.ds(depth, depth)], sems.at[2 * a + 1]
        )

    @pl.when(at == 0)
    def _():
        for a in range(lines):
            own_copy(a).start()
            other_copy(a).start()
        for n in range(2 * groups):
            joined[:, n * GW : (n + 1) * GW] = attention[n][...]

    own_copy(at).wait()
    sent = lax.rem(at + core * half, lines)
    pltpu.make_async_copy(
        landed.at[:, pl.ds(0, share)],
        held.at[at, pl.ds(depth, depth)],
        sems.at[2 * sent + 1],
    ).wait()
    out[0] = jnp.dot(joined[...], held[at], preferred_element_type=F32)


def output_projection(place, attention, own, landed, crossed, lines):
    rows = attention[0].shape[0]
    depth, features = own.shape
    share = features // (2 * lines)
    vmem = pl.BlockSpec((rows, GW), lambda a, place: (0, 0))
    anywhere = pl.BlockSpec(memory_space=pl.ANY)
    return pl.pallas_call(
        functools.partial(output_kernel, len(attention) // 2, lines),
        out_shape=jax.ShapeDtypeStruct((lines, rows, share), F32),
        grid_spec=pltpu.PrefetchScalarGridSpec(
            num_scalar_prefetch=1,
            grid=(lines,),
            in_specs=[vmem] * len(attention) + [anywhere] * 3,
            out_specs=pl.BlockSpec((1, rows, share), lambda a, place: (a, 0, 0)),
            scratch_shapes=[
                pltpu.VMEM((lines, 2 * depth, share), BF16),
                pltpu.VMEM((rows, 2 * depth), BF16),
                pltpu.SemaphoreType.DMA((2 * lines,)),
            ],
        ),
        compiler_params=params(),
        cost_estimate=LIGHT,
        name="output",
    )(place, *attention, own, landed, crossed)


def on_device(
    hidden_states,
    norm_gain,
    norm_bias,
    qkv_weight,
    qkv_bias,
    dense_weight,
    dense_bias,
    prefix_keys,
    prefix_values,
    suffix_len,
    request_order,
    group_slot,
):
    rows, share = hidden_states.shape
    held, prefix_length, local_width = prefix_keys.shape
    groups_local = local_width // GW
    tok_size = lax.axis_size("tok")
    head_size = lax.axis_size("head")
    chips = tok_size // 2
    lines = head_size // 2
    group_count = held * tok_size
    tok = lax.axis_index("tok")
    head = lax.axis_index("head")
    core, chip = tok % 2, tok // 2
    side, line = head % 2, head // 2

    def to_core(x):
        return lax.ppermute(x, "tok", [(t, t ^ 1) for t in range(tok_size)])

    def to_chip(x, shift):
        return lax.ppermute(
            x,
            "tok",
            [(t, (t // 2 + shift) % chips * 2 + t % 2) for t in range(tok_size)],
        )

    def to_side(x):
        return lax.ppermute(x, "head", [(h, h ^ 1) for h in range(head_size)])

    def after(x, *others):
        return lax.optimization_barrier((x, others))[0]

    layout = jnp.stack([suffix_len[0], request_order[0]])
    layouts = [layout] + [to_chip(layout, shift) for shift in range(1, chips)]
    (first,) = part_by_part(qkv_weight, 0, ((0, 3 * GW),))
    first, layouts = lax.optimization_barrier((first, layouts))

    last = lines - 1

    def to_side_from(x, lowest, highest):
        return lax.ppermute(
            x, "head", [(h, h ^ 1) for h in range(head_size) if lowest <= h // 2 <= highest]
        )

    columns = 3 * GW
    source, _ = lax.optimization_barrier((qkv_weight, layouts))
    cuts = ((0, columns), (0, 2 * GW), (2 * GW, columns))
    later = [part_by_part(source, g, cuts) for g in range(1, groups_local)]
    across = to_side(hidden_states)
    blocks = [hidden_states, across]
    places = [head, head ^ 1]
    arriving = [to_chip(first, shift) for shift in range(1, chips)]
    up = down = hidden_states
    settled = across
    for step in range(last):
        if step > 0:
            up, down, settled, first, later = lax.optimization_barrier(
                (up, down, settled, first, later)
            )
            blocks[1 if step == 1 else tied] = settled
        up = lax.ppermute(
            up, "head", [(h, h + 2) for h in range(head_size) if step <= h // 2 < last]
        )
        down = lax.ppermute(
            down, "head", [(h, h - 2) for h in range(head_size) if 0 < h // 2 <= last - step]
        )
        from_below, from_above = line >= step + 1, line + 1 + step <= last
        below, above = line - 1 - step, line + 1 + step
        blocks += [up, down]
        places += [
            jnp.where(from_below, 2 * below + side, -1),
            jnp.where(from_above, 2 * above + side, -1),
        ]
        marked = len(blocks)
        if 2 * step + 1 < last:
            blocks += [to_side_from(up, step + 1, last), to_side_from(down, 0, last - 1 - step)]
            places += [
                jnp.where(from_below, 2 * below + 1 - side, -1),
                jnp.where(from_above, 2 * above + 1 - side, -1),
            ]
        else:
            here = after(jnp.where(from_below, up, down), blocks[-3])
            lines_with = [h for h in range(head_size) if h // 2 >= step + 1 or h // 2 <= last - 1 - step]
            blocks.append(lax.ppermute(here, "head", [(h, h ^ 1) for h in lines_with]))
            there = jnp.where(from_below, below, above)
            places.append(jnp.where(from_below | from_above, 2 * there + 1 - side, -1))
        if step > 0:
            tied, settled = previous, blocks[previous]
        previous = marked
    places = jnp.stack(places).astype(jnp.int32)

    order = [tok, tok ^ 1]
    for shift in range(1, chips):
        source = (chip + chips - shift) % chips * 2 + core
        order += [source, source ^ 1]
    order = jnp.stack(order).astype(jnp.int32)
    lengths = suffix_len[0]
    starts, row_start, within = shard_layout(lengths, request_order[0], rows)
    labels = jnp.arange(group_count, dtype=jnp.int32)
    slot_match = (group_slot[:, None] == labels[None, :]).astype(jnp.int32)

    def served_spans(one):
        firsts = shard_layout(one[0], one[1], rows)[0]
        spans = jnp.stack(
            [
                jnp.sum(firsts[:, None] * slot_match, axis=0),
                jnp.sum(one[0][:, None] * slot_match, axis=0),
            ]
        )
        return jnp.concatenate(
            [
                lax.dynamic_slice(spans, (0, tok * held), (2, held)),
                lax.dynamic_slice(spans, (0, (tok ^ 1) * held), (2, held)),
            ],
            axis=1,
        )

    served = jnp.stack([served_spans(one) for one in layouts], axis=2)
    tables = rotary_tables(prefix_length + within)
    bias = qkv_bias.astype(F32).reshape(groups_local, GROUP_HEADS, 3, HS)
    bias = jnp.transpose(bias, (0, 2, 1, 3)).reshape(groups_local, 1, columns)
    bias = [
        [bias[g]] if g == 0 else [bias[g][:, : 2 * GW], bias[g][:, 2 * GW :]]
        for g in range(groups_local)
    ]

    half = lines // 2
    outgoing = jnp.concatenate(
        [
            lax.dynamic_slice(
                dense_weight,
                (0, (2 * (core * half + a) + 1 - side) * share),
                (dense_weight.shape[0], share),
            )
            for a in range(half)
        ],
        axis=1,
    )
    ready = (
        served[0].reshape(-1),
        served[1].reshape(-1),
        tables,
        bias,
        order,
        row_start[:, None],
        jnp.stack([side, core]).astype(jnp.int32),
        outgoing,
        later,
        places,
        blocks,
    )
    arriving, ready = lax.optimization_barrier((arriving, ready))
    span_start, span_length, tables, bias, order, row_start, place, outgoing, later = ready[:9]
    places, blocks = ready[9:]

    def send(mine):
        return [to_chip(mine, shift) for shift in range(1, chips)]

    def exchange(queries):
        return [queries] + [to_chip(queries, shift) for shift in range(1, chips)]

    def pieces_of(own, arrived, first, width):
        pieces = [[(one, first, width)] for one in own]
        for n in range(chips - 1):
            for which in range(2):
                pieces.append([(part[n][which], 0, part[n][which].shape[1]) for part in arrived])
        return pieces

    def crossing(arrived):
        return [(one, to_core(one)) for one in arrived]

    coming = [send(after(one[1], arriving)) for one in later]
    first_pieces = pieces_of((first, to_core(first)), [crossing(arriving)], 0, columns)
    normed = layer_norm(blocks, places, norm_gain, norm_bias)
    landed = to_side(after(outgoing, normed))
    cache = [prefix_keys, to_core(after(prefix_keys, arriving))]
    cache += [prefix_values, to_core(after(prefix_values, arriving))]
    own = [(one[0], to_core(after(one[0], normed))) for one in later]
    heads = [project(normed, first_pieces, order, bias[0][0], tables, (0, 1, 2))]
    asked = [exchange(heads[0][0])]
    settled = heads[0]
    values_coming = []
    for g in range(1, groups_local):
        arrived = crossing(after(coming[g - 1], settled))
        pair = project(
            normed, pieces_of(own[g - 1], [arrived], 0, 2 * GW), order, bias[g][0], tables, (0, 1)
        )
        heads.append(pair)
        asked.append(exchange(pair[0]))
        settled = pair
    suffixes = [suffix_attention(after(row_start, settled), *heads[0])]
    values_coming = [
        send(after(one[2], asked[0][1:], asked[-1][1:], suffixes[0])) for one in later
    ]
    asked[0] = after(asked[0], suffixes[0])
    returned = []
    for g in range(groups_local):
        if g > 0:
            asked[g] = after(asked[g], answers)
        answers = prefix_attention(g, asked[g], cache, span_start, span_length)
        returned.append([answers[0]] + [to_chip(answers[s], chips - s) for s in range(1, chips)])
    crossed = to_core(after(landed, answers))
    attention_own, attention_side = [], []
    for g in range(1, groups_local):
        arrived = crossing(after(values_coming[g - 1], answers, returned[g - 1][1:]))
        (values,) = project(
            normed, pieces_of(own[g - 1], [arrived], 2 * GW, GW), order, bias[g][1], tables, (2,)
        )
        parts_first = after(returned[g - 1], values)
        attention_own.append(merge(parts_first, *suffixes[g - 1]))
        attention_side.append(to_side(attention_own[-1]))
        suffixes.append(
            suffix_attention(after(row_start, attention_own[-1]), heads[g][0], heads[g][1], values)
        )
    attention_own.append(merge(after(returned[-1], attention_side), *suffixes[-1]))
    attention_side.append(to_side(attention_own[-1]))
    partial = output_projection(
        place, attention_own + attention_side, dense_weight, landed, crossed, lines
    )

    cuts = 2
    height = rows // cuts

    def chunk(place, cut):
        place = jnp.clip(place, 0, last)
        return lax.dynamic_slice(
            partial, (place, cut * height, 0), (1, height, share)
        ).reshape(height, share)

    passing = [None] * cuts
    for step in range(last):
        up_pairs = [(h, h + 2) for h in range(head_size) if h // 2 <= step and h // 2 < last]
        down_pairs = [(h, h - 2) for h in range(head_size) if last - h // 2 <= step and h // 2 > 0]
        for cut in range(cuts):
            up = chunk(last + line - step, cut)
            down = chunk(line - last + step, cut)
            if passing[cut] is not None:
                if cut > 0:
                    passing[cut], sent = lax.optimization_barrier((passing[cut], sent))
                up = up + passing[cut][0].astype(F32)
                down = down + passing[cut][1].astype(F32)
            up, down = lax.optimization_barrier((up.astype(BF16), down.astype(BF16)))
            sent = up
            passing[cut] = lax.optimization_barrier(
                (lax.ppermute(up, "head", up_pairs), lax.ppermute(down, "head", down_pairs))
            )
    base = hidden_states.astype(F32) + dense_bias.astype(F32)
    done = [
        base[cut * height : (cut + 1) * height]
        + (chunk(line, cut) + passing[cut][0].astype(F32) + passing[cut][1].astype(F32))
        for cut in range(cuts)
    ]
    return jnp.concatenate(done, axis=0).astype(BF16)


def solution(mesh):
    placed = (
        P("tok", "head"),
        P(),
        P(),
        P("tok", "head"),
        P("head"),
        P("head", None),
        P("head"),
        P("tok", None, "head"),
        P("tok", None, "head"),
        P("tok", None),
        P("tok", None),
        P(),
    )
    return jax.shard_map(
        on_device, mesh=mesh, in_specs=placed, out_specs=P("tok", "head"), check_vma=False
    )
```
